32 devices in a mesh: dp: 8 (over z, y), ep: 4 (over x, core).
Axes of the slice: x: 2, y: 2, z: 4, core: 2. Of those that a mesh axis runs over, the one named last changes fastest.
Arguments:
- states: bfloat16 [256, 16, 128, 128], P(('dp', 'ep')), may hold values from -4 to 4
- query_rows: bfloat16 [256, 4, 1024], P(('dp', 'ep')), may hold values from -6 to 6
- key_rows: bfloat16 [256, 4, 1024], P(('dp', 'ep')), may hold values from -6 to 6
- value_rows: bfloat16 [256, 4, 2048], P(('dp', 'ep')), may hold values from -6 to 6
- gate_rows: bfloat16 [256, 4, 2048], P(('dp', 'ep')), may hold values from -6 to 6
- beta_logit: bfloat16 [256, 4, 16], P(('dp', 'ep')), may hold values from -6 to 6
- decay_logit: bfloat16 [256, 4, 16], P(('dp', 'ep')), may hold values from -8 to 8
- residual: bfloat16 [256, 4, 2048], P(('dp', 'ep')), may hold values from -6 to 6
- route_ids: int32 [256, 4, 10], P(('dp', 'ep')), may hold values from 0 to 31, all different within a row; in each aligned block of 32 rows (0 to 31, 32 to 63, ..., all dimensions but the last counted through in order) at most 11 rows name the same one
- route_prob: float32 [256, 4, 10], P(('dp', 'ep')), may hold values from 0.05 to 1
- out_weight: bfloat16 [2048, 2048], P(None, 'ep'), may hold values from -0.125 to 0.125
- core_gain: float32 [128], replicated, may hold values from 0.1 to 1.9
- moe_gain: float32 [2048], replicated, may hold values from 0.1 to 1.9
- gate_up: bfloat16 [32, 2048, 512], P(('dp', 'ep')), may hold values from -0.125 to 0.125
- down_weight: bfloat16 [32, 256, 2048], P(('dp', 'ep')), may hold values from -0.375 to 0.375
- new_home: int32 [256], P(('dp', 'ep')), may hold values from 0 to 255, as said below
Outputs:
- mixed_out: bfloat16 [256, 4, 2048], P(('dp', 'ep'))
- moved_out: bfloat16 [256, 16, 128, 128], P(('dp', 'ep'))
The draws below stay inside these ranges and needn't reach their ends.
Inputs may be any that keep to these rules, and one draw needn't show every extreme that they name: `route_ids`: each row names 10 different experts; among the 32 rows of one device (its requests, each with its 4 tokens) no expert is named more than 11 times, a bound that some block reaches. `new_home`: A permutation of the request positions; a request stays among the 4 devices of its dp index, and every device hands exactly 2 of its requests to each device of that group, itself included.
All inputs are finite; a program needn't handle non-finite values.
Results may differ from the reference program's by a relative error of at most 0.01.
Values may be sent and summed in bfloat16 or wider, within the bound.
No kernel may reach another device: no remote copies, remote signals or barrier semaphores. Data moves between devices by JAX's collectives and lax.ppermute only.
A program may use at most 128 MiB of HBM per device.

```python
import math
import jax
import jax.numpy as jnp
import numpy as np
from jax import lax

D = 2048
VH = 16
HD = 128
FE = 256
TOP = 10
STEPS = 4
REQ_DEV = 8
KH = 8
REQS = 256
EXPERTS = 32
CAP = 11
MIG_CAP = 2
N_DP = 8
N_EP = 4
DEVICES = 32


def draw_new_home(key, part):
    key_shift, key_place = jax.random.split(jax.random.fold_in(key, 7))
    shifts = jax.vmap(lambda subkey: jax.random.permutation(subkey, N_EP))(jax.random.split(key_shift, N_DP))
    places = jax.vmap(lambda subkey: jax.random.permutation(subkey, REQ_DEV))(jax.random.split(key_place, N_DP * N_EP))
    places = places.reshape(N_DP, N_EP, REQ_DEV)
    groups = jnp.arange(N_DP, dtype=jnp.int32)[:, None, None]
    source = jnp.arange(N_EP, dtype=jnp.int32)[None, :, None]
    request = jnp.arange(REQ_DEV, dtype=jnp.int32)[None, None, :]
    blocks = request // MIG_CAP
    offset = shifts[groups, blocks]
    target = (source + offset) % N_EP
    positions = places[groups, target, request]
    new_place = (groups * N_EP + target) * REQ_DEV + positions
    return new_place.reshape(-1).astype(jnp.int32)


def shard_levels(rng, extent, cuts, smallest, high):
    factor_of, own = 1.0, jax.random.fold_in(rng, 6)
    for dim, blocks in cuts:
        heights = jnp.exp(jax.random.uniform(jax.random.fold_in(own, dim), (blocks,), jnp.float32, smallest / len(cuts), high / len(cuts)))
        factor_of = factor_of * jnp.repeat(heights, extent[dim] // blocks).reshape([-1 if axis == dim else 1 for axis in range(len(extent))])
    return factor_of


def deal_out(key, own, number, rows, number_of, top, reach, lean):
    order = jax.random.permutation(key, number_of)
    crowded, ordinary = portions_of(number_of, rows * top, reach, lean, True), portions_of(number_of, rows * top, reach, lean, False)
    places = jnp.arange(number_of)

    def named(sizes, turn):
        used = int((sizes > 0).sum())
        fixed = max(1, used // 4)
        passed = fixed + (places - fixed + turn * (used - fixed)) % max(1, number_of - fixed)
        return jnp.zeros((number_of,), jnp.int32).at[order[jnp.where(places < fixed, places, passed)]].set(jnp.asarray(sizes, jnp.int32))

    sizes = jnp.where(number % 4 == 0, named(crowded, number // 4), named(ordinary, number - number // 4 - 1))
    mixed = jax.random.permutation(jax.random.fold_in(own, 3), number_of)
    donor, sink = mixed[0:number_of // 2 * 2:2], mixed[1:number_of // 2 * 2:2]
    margin = jnp.minimum(sizes[donor] - 1, reach - sizes[sink]) // 2
    margin = jnp.where((donor == order[0]) | (sink == order[0]) | (sizes[sink] == 0), 0, jnp.maximum(margin, 0))
    passed = jax.random.randint(jax.random.fold_in(own, 4), (number_of // 2,), 0, 1 << 20) % (margin + 1)
    sizes = sizes.at[donor].add(-passed).at[sink].add(passed)
    members = jnp.searchsorted(jnp.cumsum(sizes), jnp.arange(rows * top), side="right").astype(jnp.int32)
    table = members.reshape(top, rows).T
    table = table[jax.random.permutation(jax.random.fold_in(own, 1), rows)]
    turn = jax.random.randint(jax.random.fold_in(own, 2), (rows, 1), 0, top)
    return jnp.take_along_axis(table, (jnp.arange(top)[None, :] + turn) % top, axis=1)


def portions_of(amount, total, reach, skew, full):
    portions = [(1 << 20) // math.isqrt(standing ** skew) + 1 for standing in range(1, amount + 1)]
    largest = reach if full else min(reach, max(-(-total // amount), total * portions[0] // sum(portions)))
    least = 1 if total - largest >= amount - 1 else 0
    given, surplus = [largest] + [least] * (amount - 1), total - largest - least * (amount - 1)
    while surplus > 0:
        movable = [i for i in range(1, amount) if given[i] < largest] or [i for i in range(1, amount) if given[i] < reach]
        whole, left = sum([portions[i] for i in movable]), surplus
        for i in movable:
            extra = min(reach - given[i], max(1, left * portions[i] // whole), surplus)
            given[i] = given[i] + extra
            surplus = surplus - extra
    return np.array(given)


def bell_draw(own_key, extent, spread, bound, cuts=(), held_as=jnp.bfloat16):
    values = jax.random.normal(own_key, extent, jnp.float32) * spread
    if len(cuts) > 0:
        values = shard_levels(own_key, extent, cuts, -0.22, 0.18) * values
    return jnp.clip(values, min=-bound, max=bound).astype(held_as)


def setup_inputs(seed: int = 0) -> dict:
    key_of = jax.random.split(jax.random.key(seed), 17)
    states = bell_draw(key_of[0], (REQS, VH, HD, HD), 0.5, 4.0, ((0, 32),))
    query_rows = bell_draw(key_of[1], (REQS, STEPS, KH * HD), 1.0, 6.0, ((0, 32),))
    key_rows = bell_draw(key_of[2], (REQS, STEPS, KH * HD), 1.0, 6.0, ((0, 32),))
    value_rows = bell_draw(key_of[3], (REQS, STEPS, VH * HD), 1.0, 6.0, ((0, 32),))
    gate_rows = bell_draw(key_of[4], (REQS, STEPS, VH * HD), 1.0, 6.0, ((0, 32),))
    beta_logit = bell_draw(key_of[5], (REQS, STEPS, VH), 1.5, 6.0, ((0, 32),))
    decay_logit = bell_draw(key_of[6], (REQS, STEPS, VH), 2.0, 8.0, ((0, 32),))
    residual = bell_draw(key_of[7], (REQS, STEPS, D), 1.0, 6.0, ((0, 32),))
    route_ids_keys = jax.random.split(jax.random.fold_in(key_of[8], 1), REQS * STEPS // (REQ_DEV * STEPS))
    route_ids_turns = jax.random.permutation(jax.random.fold_in(key_of[8], 3), REQS * STEPS // (REQ_DEV * STEPS))
    route_ids = jax.vmap(lambda own, number: deal_out(jax.random.fold_in(key_of[8], 2), own, number, REQ_DEV * STEPS, EXPERTS, TOP, CAP, 2))(route_ids_keys, route_ids_turns).reshape((REQS, STEPS, TOP))
    route_prob = jnp.clip(jnp.exp(math.log(1.0) - 2.9957323 * jax.random.uniform(key_of[9], (REQS, STEPS, TOP), jnp.float32) ** shard_levels(key_of[9], (REQS, STEPS, TOP), ((0, 32),), -0.2, 0.2)), 0.05, 1.0)
    out_weight = bell_draw(key_of[10], (VH * HD, D), (VH * HD) ** -0.5, 0.125, ((1, 4),))
    core_gain = jnp.clip(1.0 + 0.18 * jax.random.normal(key_of[11], (HD,), jnp.float32), 0.1, 1.9)
    moe_gain = jnp.clip(1.0 + 0.18 * jax.random.normal(key_of[12], (D,), jnp.float32), 0.1, 1.9)
    gate_up = bell_draw(key_of[13], (EXPERTS, D, 2 * FE), D ** -0.5, 0.125, ((0, 32),))
    down_weight = bell_draw(key_of[14], (EXPERTS, FE, D), FE ** -0.5, 0.375, ((0, 32),))
    new_home = draw_new_home(jax.random.fold_in(key_of[16], 71), 0)
    return {"states": states, "query_rows": query_rows, "key_rows": key_rows, "value_rows": value_rows, "gate_rows": gate_rows, "beta_logit": beta_logit, "decay_logit": decay_logit, "residual": residual, "route_ids": route_ids, "route_prob": route_prob, "out_weight": out_weight, "core_gain": core_gain, "moe_gain": moe_gain, "gate_up": gate_up, "down_weight": down_weight, "new_home": new_home}


epsilon = 1e-06

def unit_rows(values):
    return values * lax.rsqrt(lax.optimization_barrier(jnp.sum(values * values, -1, keepdims=True)) + epsilon)

def delta_block(state_in, query_rows, key_rows, value_rows, gate_rows, beta_logit, decay_logit, core_gain):
    batch_size = state_in.shape[0]
    head_count = decay_logit.shape[-1]
    head_width = state_in.shape[-1]
    key_heads = query_rows.shape[-1] // head_width
    repeats = head_count // key_heads
    memory_state = state_in.astype(jnp.float32)
    outputs = []
    for position in range(query_rows.shape[1]):
        queries = unit_rows(query_rows[:, position].astype(jnp.float32).reshape(batch_size, key_heads, head_width))
        queries = jnp.repeat(queries, repeats, axis=1) * head_width ** (-0.5)
        key_units = unit_rows(key_rows[:, position].astype(jnp.float32).reshape(batch_size, key_heads, head_width))
        key_units = jnp.repeat(key_units, repeats, axis=1)
        values = value_rows[:, position].astype(jnp.float32).reshape(batch_size, head_count, head_width)
        decays = jax.nn.sigmoid(decay_logit[:, position].astype(jnp.float32))
        strength = jax.nn.sigmoid(beta_logit[:, position].astype(jnp.float32))
        memory_state = memory_state * decays[:, :, None, None]
        memory = jnp.einsum('bhkv,bhk->bhv', memory_state, key_units, precision=lax.Precision.HIGHEST)
        update = (values - memory) * strength[:, :, None]
        memory_state = memory_state + key_units[:, :, :, None] * update[:, :, None, :]
        reading = jnp.einsum('bhkv,bhk->bhv', memory_state, queries, precision=lax.Precision.HIGHEST)
        scaled = reading * lax.rsqrt(lax.optimization_barrier(jnp.mean(reading * reading, -1, keepdims=True)) + epsilon)
        gate_vals = gate_rows[:, position].astype(jnp.float32).reshape(batch_size, head_count, head_width)
        gated_out = scaled * core_gain * jax.nn.silu(gate_vals)
        outputs.append(gated_out.reshape(batch_size, head_count * head_width).astype(jnp.bfloat16))
    return (memory_state.astype(jnp.bfloat16), jnp.stack(outputs, axis=1))

def rms_scale(values, gain):
    return values * lax.rsqrt(lax.optimization_barrier(jnp.mean(values * values, -1, keepdims=True)) + epsilon) * gain

def expert_apply(chosen_rows, gate_up, down_weight):
    hidden_units = down_weight.shape[0]
    joined = jnp.dot(chosen_rows, gate_up, preferred_element_type=jnp.float32)
    active = (jax.nn.silu(joined[:, :hidden_units]) * joined[:, hidden_units:]).astype(jnp.bfloat16)
    return jnp.dot(active, down_weight, preferred_element_type=jnp.float32).astype(jnp.bfloat16)

def reference(states, query_rows, key_rows, value_rows, gate_rows, beta_logit, decay_logit, residual, route_ids, route_prob, out_weight, core_gain, moe_gain, gate_up, down_weight, new_home):

    def per_device(pieces):
        return delta_block(pieces[0], pieces[1], pieces[2], pieces[3], pieces[4], pieces[5], pieces[6], core_gain)
    shaped = tuple((array.reshape((DEVICES, REQ_DEV) + array.shape[1:]) for array in (states, query_rows, key_rows, value_rows, gate_rows, beta_logit, decay_logit)))
    fresh_states, core_out = lax.map(per_device, shaped)
    fresh_states = fresh_states.reshape(states.shape)
    core_out = core_out.reshape(REQS * STEPS, VH * HD)
    attention = jnp.dot(core_out, out_weight, preferred_element_type=jnp.float32).astype(jnp.bfloat16)
    hidden = (residual.reshape(REQS * STEPS, D).astype(jnp.float32) + attention.astype(jnp.float32)).astype(jnp.bfloat16)
    normed = rms_scale(hidden.astype(jnp.float32), moe_gain).astype(jnp.bfloat16)
    flat_ids = route_ids.reshape(-1).astype(jnp.int32)
    route_total = flat_ids.shape[0]
    sorted_routes = jnp.argsort(flat_ids, stable=True).astype(jnp.int32)
    counts = jnp.zeros((EXPERTS,), jnp.int32).at[flat_ids].add(1)
    starts = (jnp.cumsum(counts) - counts).astype(jnp.int32)
    most_rows = DEVICES * CAP
    padded_order = jnp.concatenate([sorted_routes, jnp.full((most_rows,), route_total, jnp.int32)])

    def expert_step(outputs, expert_index):
        picked = lax.dynamic_slice_in_dim(padded_order, starts[expert_index], most_rows)
        live_rows = jnp.arange(most_rows, dtype=jnp.int32) < counts[expert_index]
        picked = jnp.where(live_rows, picked, route_total).astype(jnp.int32)
        chosen_rows = normed[jnp.minimum(picked, route_total - 1) // TOP]
        result = expert_apply(chosen_rows, gate_up[expert_index], down_weight[expert_index])
        return (outputs.at[picked].set(result, mode='drop'), None)
    routed, _ = lax.scan(expert_step, jnp.zeros((route_total, D), jnp.bfloat16), jnp.arange(EXPERTS, dtype=jnp.int32))
    weights = route_prob.reshape(REQS * STEPS, TOP).astype(jnp.float32)
    weights = weights / lax.optimization_barrier(jnp.sum(weights, -1, keepdims=True))
    combined = lax.optimization_barrier(jnp.sum(routed.reshape(REQS * STEPS, TOP, D).astype(jnp.float32) * weights[:, :, None], axis=1))
    mixed_out = (hidden.astype(jnp.float32) + combined).astype(jnp.bfloat16).reshape(REQS, STEPS, D)
    moved_out = jnp.zeros_like(fresh_states).at[new_home].set(fresh_states)
    return (mixed_out, moved_out)
```

```python
import functools

import jax
import jax.numpy as jnp
from jax import lax
from jax.experimental import pallas as pl
from jax.experimental.pallas import tpu as pltpu
from jax.sharding import PartitionSpec as P

EPS = 1e-06
F32 = jnp.float32
BF16 = jnp.bfloat16
MIB = 1 << 20


def row_sum(x):
    return jnp.sum(x, axis=-1, keepdims=True)


def spread_rows(ref, scratch, requests, steps):
    for r in range(requests):
        split_heads(ref[r].astype(F32), scratch, r, steps)


def split_heads(values, scratch, r, steps):
    hd = scratch.shape[-1]
    for h in range(scratch.shape[0]):
        scratch[h, r * steps : (r + 1) * steps, :] = values[:, h * hd : (h + 1) * hd]


def at_step(scratch, t, requests, steps, head=None):
    if head is None:
        return scratch[pl.ds(t, requests, stride=steps), :]
    return scratch[head, pl.ds(t, requests, stride=steps), :]


def recurrence(kh, repeats, steps, requests, hd, k_s, q_s, v_s, a_s, b_s, m_s, emit_out, emit_state):
    per = m_s.shape[1] // requests
    ks = [at_step(k_s, t, requests, steps, kh) for t in range(steps)]
    rk = [lax.rsqrt(row_sum(k * k) + EPS) for k in ks]
    kn = [k * r for k, r in zip(ks, rk)]
    kk = {(i, t): row_sum(kn[i] * kn[t]) for t in range(steps) for i in range(t)}
    if emit_out is not None:
        qs = [at_step(q_s, t, requests, steps, kh) for t in range(steps)]
        rq = [lax.rsqrt(row_sum(q * q) + EPS) * hd**-0.5 for q in qs]
        qn = [q * r for q, r in zip(qs, rq)]
        kq = {(i, t): row_sum(kn[i] * qn[t]) for t in range(steps) for i in range(t + 1)}
    for h in range(kh * repeats, (kh + 1) * repeats):
        decayed = []
        c = None
        for t in range(steps):
            a = at_step(a_s, t, requests, steps)[:, h : h + 1]
            b = at_step(b_s, t, requests, steps)[:, h : h + 1]
            decayed = [w * a for w in decayed]
            c = a if c is None else c * a
            m = (c * rk[t]) * at_step(m_s, t, requests, per, h)
            for i in range(t):
                m = m + kk[i, t] * decayed[i]
            decayed.append((at_step(v_s, t, requests, steps, h) - m) * b)
            if emit_out is not None:
                o = (c * rq[t]) * at_step(m_s, steps + t, requests, per, h)
                for i in range(t + 1):
                    o = o + kq[i, t] * decayed[i]
                emit_out(t, h, o)
        if emit_state is not None:
            emit_state(h, c, [w * r for w, r in zip(decayed, rk)])


def sigmoid_rows(ref, scratch, requests, steps):
    for r in range(requests):
        scratch[r * steps : (r + 1) * steps, : ref.shape[-1]] = jax.nn.sigmoid(ref[r].astype(F32))


def core_kernel(
    state_ref, q_ref, k_ref, v_ref, g_ref, b_ref, a_ref, gain_ref, out_ref,
    k_s, q_s, v_s, g_s, a_s, b_s, m_s, o_s,
):
    r = pl.program_id(0)
    requests, steps, key_width = k_ref.shape
    heads, hd = state_ref.shape[1], state_ref.shape[-1]
    key_heads = key_width // hd
    repeats = heads // key_heads
    rows = jnp.concatenate([k_ref[r].astype(F32), q_ref[r].astype(F32)], axis=0).astype(BF16)
    base = pl.multiple_of(r * 2 * steps, 2 * steps)
    for h in range(heads):
        kh = h // repeats
        m_s[h, pl.ds(base, 2 * steps), :] = jnp.dot(
            rows[:, kh * hd : (kh + 1) * hd], state_ref[0, h], preferred_element_type=F32
        )

    @pl.when(r == requests - 1)
    def _():
        spread_rows(k_ref, k_s, requests, steps)
        spread_rows(q_ref, q_s, requests, steps)
        spread_rows(v_ref, v_s, requests, steps)
        spread_rows(g_ref, g_s, requests, steps)
        sigmoid_rows(a_ref, a_s, requests, steps)
        sigmoid_rows(b_ref, b_s, requests, steps)
        gain = gain_ref[...]

        def emit(t, h, o):
            gate = at_step(g_s, t, requests, steps, h)
            scaled = o * lax.rsqrt(row_sum(o * o) * (1.0 / hd) + EPS)
            o_s[h, pl.ds(t, requests, stride=steps), :] = scaled * gain * jax.nn.silu(gate)

        for kh in range(key_heads):
            recurrence(kh, repeats, steps, requests, hd, k_s, q_s, v_s, a_s, b_s, m_s, emit, None)
        for h in range(heads):
            out_ref[:, h * hd : (h + 1) * hd] = o_s[h].astype(BF16)


def core_rows(states, query_rows, key_rows, value_rows, gate_rows, beta_logit, decay_logit, core_gain):
    requests, heads, hd, _ = states.shape
    steps = key_rows.shape[1]
    kw, vw = key_rows.shape[-1], value_rows.shape[-1]
    whole = lambda x: pl.BlockSpec(x.shape, lambda r: (0,) * x.ndim)
    tokens = requests * steps
    gain = core_gain.reshape(1, hd)
    small = (query_rows, key_rows, value_rows, gate_rows, beta_logit, decay_logit, gain)
    return pl.pallas_call(
        core_kernel,
        grid=(requests,),
        in_specs=[pl.BlockSpec((1, heads, hd, hd), lambda r: (r, 0, 0, 0))] + [whole(x) for x in small],
        out_specs=pl.BlockSpec((tokens, vw), lambda r: (0, 0)),
        out_shape=jax.ShapeDtypeStruct((tokens, vw), BF16),
        scratch_shapes=[
            pltpu.VMEM((kw // hd, tokens, hd), F32),
            pltpu.VMEM((kw // hd, tokens, hd), F32),
            pltpu.VMEM((heads, tokens, hd), F32),
            pltpu.VMEM((heads, tokens, hd), F32),
            pltpu.VMEM((tokens, 128), F32),
            pltpu.VMEM((tokens, 128), F32),
            pltpu.VMEM((heads, 2 * tokens, hd), F32),
            pltpu.VMEM((heads, tokens, hd), F32),
        ],
        compiler_params=pltpu.CompilerParams(vmem_limit_bytes=32 * MIB),
        cost_estimate=pl.CostEstimate(flops=20_000_000, bytes_accessed=5 * MIB, transcendentals=100_000),
        name="core_rows",
    )(states, *small)


def pack_kernel(order_ref, state_ref, pay_ref, *rest):
    groups = len(rest) // 2
    outs, sems = rest[:-1], rest[-1]
    cap = outs[0].shape[0]
    half = len(outs) // 2
    copies = []
    for d in range(half):
        for j in range(cap):
            source = order_ref[(d + 1) * cap + j]
            copies.append(
                pltpu.make_async_copy(state_ref.at[source], outs[d].at[j], sems.at[0, d * cap + j])
            )
            copies.append(
                pltpu.make_async_copy(pay_ref.at[source], outs[half + d].at[j], sems.at[1, d * cap + j])
            )
    for c in copies:
        c.start()
    for c in copies:
        c.wait()


def pack_lanes(order, states, payload, lanes):
    requests = states.shape[0]
    cap = requests // lanes
    hbm = pl.BlockSpec(memory_space=pl.ANY)
    outs = pl.pallas_call(
        pack_kernel,
        in_specs=[pl.BlockSpec(memory_space=pltpu.SMEM), hbm, hbm],
        out_specs=[hbm] * (2 * (lanes - 1)),
        out_shape=[jax.ShapeDtypeStruct((cap,) + states.shape[1:], BF16)] * (lanes - 1)
        + [jax.ShapeDtypeStruct((cap,) + payload.shape[1:], BF16)] * (lanes - 1),
        scratch_shapes=[pltpu.SemaphoreType.DMA((2, (lanes - 1) * cap))],
        cost_estimate=pl.CostEstimate(flops=0, bytes_accessed=6 * MIB, transcendentals=0),
        name="pack_lanes",
    )(order, states, payload)
    return outs[: lanes - 1], outs[lanes - 1 :]


def state_kernel(kw, vw, heads, order_ref, place_ref, own_ref, *rest):
    lanes = len(rest) - 13 + 1
    sources = (own_ref,) + rest[: lanes - 1]
    pay_ref, out_ref = rest[lanes - 1], rest[lanes]
    k_s, v_s, a_s, b_s, m_s, u_s, c_s, held, ready, in_sem, out_sem = rest[lanes + 1 :]
    requests, steps, _ = pay_ref.shape
    hd = held.shape[-1]
    repeats = heads // (kw // hd)
    cap = requests // lanes
    copies = []
    for r in range(requests):
        d, j = divmod(r, cap)
        source = own_ref.at[order_ref[j]] if d == 0 else sources[d].at[j]
        copies.append(pltpu.make_async_copy(source, held.at[r], in_sem.at[r]))
        copies[-1].start()
    for r in range(requests):
        rows = slice(r * steps, (r + 1) * steps)
        pay = pay_ref[r].astype(F32)
        split_heads(pay[:, :kw], k_s, r, steps)
        split_heads(pay[:, kw : kw + vw], v_s, r, steps)
        a_s[rows, :] = jax.nn.sigmoid(pay[:, kw + vw : kw + vw + 128])
        b_s[rows, :] = jax.nn.sigmoid(pay[:, kw + vw + 128 : kw + vw + 256])
    for r in range(requests):
        copies[r].wait()
        rows = slice(r * steps, (r + 1) * steps)
        for h in range(heads):
            m_s[h, rows, :] = jnp.dot(
                k_s[h // repeats, rows, :].astype(BF16), held[r, h], preferred_element_type=F32
            )

    def emit(h, c, updates):
        c_s[h] = jnp.broadcast_to(c, (requests, hd))
        for t, u in enumerate(updates):
            u_s[h, pl.ds(t, requests, stride=steps), :] = u

    for kh in range(kw // hd):
        recurrence(kh, repeats, steps, requests, hd, k_s, None, v_s, a_s, b_s, m_s, None, emit)
    sent = []
    for r in range(requests):
        slot = r % 2
        if r >= 2:
            sent[r - 2].wait()
        rows = slice(r * steps, (r + 1) * steps)
        for h in range(heads):
            k4 = k_s[h // repeats, rows, :]
            k8 = jnp.concatenate([k4, k4], axis=0).astype(BF16)
            u4 = u_s[h, rows, :]
            high = u4.astype(BF16).astype(F32)
            u8 = jnp.concatenate([high, u4 - high], axis=0).astype(BF16)
            added = lax.dot_general(
                k8, u8, (((0,), (0,)), ((), ())), preferred_element_type=F32
            )
            kept = held[r, h].astype(F32) * c_s[h, r : r + 1, :]
            ready[slot, h] = (kept + added).astype(BF16)
        sent.append(pltpu.make_async_copy(ready.at[slot], out_ref.at[place_ref[r]], out_sem.at[slot]))
        sent[-1].start()
    for c in sent[-2:]:
        c.wait()


def landed_states(order, place, own, arrived, payload, kw, vw):
    requests, heads, hd, _ = own.shape
    steps = payload.shape[1]
    tokens = requests * steps
    hbm = pl.BlockSpec(memory_space=pl.ANY)
    smem = pl.BlockSpec(memory_space=pltpu.SMEM)
    return pl.pallas_call(
        functools.partial(state_kernel, kw, vw, heads),
        in_specs=[smem, smem, hbm] + [hbm] * len(arrived) + [pl.BlockSpec(memory_space=pltpu.VMEM)],
        out_specs=hbm,
        out_shape=jax.ShapeDtypeStruct(own.shape, BF16),
        scratch_shapes=[
            pltpu.VMEM((kw // hd, tokens, hd), F32),
            pltpu.VMEM((heads, tokens, hd), F32),
            pltpu.VMEM((tokens, 128), F32),
            pltpu.VMEM((tokens, 128), F32),
            pltpu.VMEM((heads, tokens, hd), F32),
            pltpu.VMEM((heads, tokens, hd), F32),
            pltpu.VMEM((heads, requests, hd), F32),
            pltpu.VMEM(own.shape, BF16),
            pltpu.VMEM((2, heads, hd, hd), BF16),
            pltpu.SemaphoreType.DMA((requests,)),
            pltpu.SemaphoreType.DMA((2,)),
        ],
        compiler_params=pltpu.CompilerParams(vmem_limit_bytes=40 * MIB),
        cost_estimate=pl.CostEstimate(flops=20_000_000, bytes_accessed=9 * MIB, transcendentals=10_000),
        name="landed_states",
    )(order, place, own, *arrived, payload)


def expert_kernel(me_ref, h_ref, route_ref, gain_ref, up_ref, down_ref, out_ref):
    groups, parts, tokens, cols = h_ref.shape
    rows = groups * tokens
    hidden_units = down_ref.shape[1]
    pieces = [h_ref[:, e].reshape(rows, cols).astype(F32) for e in range(parts)]
    total = sum(row_sum(p * p) for p in pieces)
    scale = lax.rsqrt(total * (1.0 / (parts * cols)) + EPS)
    joined = None
    for e in range(parts):
        span = slice(e * cols, (e + 1) * cols)
        normed = (pieces[e] * scale * gain_ref[:, span]).astype(BF16)
        term = jnp.dot(normed, up_ref[0, span, :], preferred_element_type=F32)
        joined = term if joined is None else joined + term
    active = (jax.nn.silu(joined[:, :hidden_units]) * joined[:, hidden_units:]).astype(BF16)
    result = jnp.dot(active, down_ref[0], preferred_element_type=F32).astype(BF16)
    route = route_ref[...]
    top = route.shape[1] // 2
    named = route[:, :top] == me_ref[0].astype(F32)
    weight = row_sum(jnp.where(named, route[:, top:], 0.0))
    out_ref[...] = (result.astype(F32) * weight).astype(BF16)


def expert_all(me, hidden, routes, moe_gain, gate_up, down_weight):
    groups, parts, tokens, cols = hidden.shape
    width = parts * cols
    step = max(1, min(groups, 256 // tokens))
    rows = step * tokens
    const = lambda x: pl.BlockSpec(x.shape, lambda i: (0,) * x.ndim)
    gain = moe_gain.reshape(1, width)
    return pl.pallas_call(
        expert_kernel,
        grid=(groups // step,),
        in_specs=[
            pl.BlockSpec(memory_space=pltpu.SMEM),
            pl.BlockSpec((step, parts, tokens, cols), lambda i: (i, 0, 0, 0)),
            pl.BlockSpec((rows, routes.shape[1]), lambda i: (i, 0)),
            const(gain),
            const(gate_up),
            const(down_weight),
        ],
        out_specs=pl.BlockSpec((rows, width), lambda i: (i, 0)),
        out_shape=jax.ShapeDtypeStruct((groups * tokens, width), BF16),
        compiler_params=pltpu.CompilerParams(vmem_limit_bytes=40 * MIB),
        cost_estimate=pl.CostEstimate(
            flops=6 * groups * tokens * width * 256, bytes_accessed=12 * MIB, transcendentals=0
        ),
        name="expert_all",
    )(me, hidden, routes, gain, gate_up, down_weight)


def shards(
    states, query_rows, key_rows, value_rows, gate_rows, beta_logit, decay_logit, residual,
    route_ids, route_prob, out_weight, core_gain, moe_gain, gate_up, down_weight, new_home,
):
    requests, heads, hd, _ = states.shape
    steps = query_rows.shape[1]
    width = residual.shape[-1]
    tokens = requests * steps
    lanes = lax.axis_size("ep")
    groups = lax.axis_size("dp")
    my_lane = lax.axis_index("ep")
    me = lax.axis_index("dp") * lanes + my_lane
    cap = requests // lanes
    kw, vw = key_rows.shape[-1], value_rows.shape[-1]
    top = route_ids.shape[-1]

    with jax.named_scope("order"):
        lane = (new_home // requests % lanes) ^ my_lane
        ids = jnp.arange(requests, dtype=jnp.int32)
        earlier = (lane[:, None] == lane[None, :]) & (ids[None, :] < ids[:, None])
        slot = lane * cap + jnp.sum(earlier.astype(jnp.int32), axis=1)
        order = jnp.sum(jnp.where(slot[:, None] == ids[None, :], ids[:, None], 0), axis=0)
        place = (new_home % requests).astype(BF16)
        place = jnp.broadcast_to(place[:, None, None], (requests, steps, 1))
        fill = lambda n: jnp.zeros((requests, steps, n), BF16)
        payload = jnp.concatenate(
            [key_rows, value_rows, decay_logit, place, fill(127 - heads), beta_logit, fill(128 - heads)],
            axis=-1,
        )
    with jax.named_scope("send_states"):
        packed, pays = pack_lanes(order, states, payload, lanes)
        swap = lambda x, d: lax.ppermute(x, "ep", [(i, i ^ d) for i in range(lanes)])
        arrived = [swap(packed[d - 1], d) for d in range(1, lanes)]
        arrived_pay = [swap(pays[d - 1], d) for d in range(1, lanes)]

    with jax.named_scope("routes"):
        weights = route_prob.reshape(tokens, top)
        weights = weights / jnp.sum(weights, -1, keepdims=True)
        routes = jnp.concatenate([route_ids.reshape(tokens, top).astype(F32), weights], axis=-1)
        routes = lax.all_gather(routes, ("dp", "ep"), axis=0, tiled=True)
        group_residual = lax.all_gather(residual.reshape(tokens, width), "ep", axis=0, tiled=True)

    with jax.named_scope("core"):
        core = core_rows(
            states, query_rows, key_rows, value_rows, gate_rows, beta_logit, decay_logit, core_gain
        )
        group_core = lax.all_gather(core, "ep", axis=0, tiled=True)
    with jax.named_scope("attention"):
        cols = out_weight.shape[1]
        attention = jnp.dot(group_core, out_weight, preferred_element_type=F32).astype(BF16)
        before = lax.dynamic_slice_in_dim(group_residual, my_lane * cols, cols, axis=1)
        hidden_cols = (before.astype(F32) + attention.astype(F32)).astype(BF16)
        gathered = lax.all_gather(hidden_cols, ("dp", "ep"), axis=0, tiled=False)
        gathered = gathered.reshape(groups, lanes, tokens * lanes, cols)

    with jax.named_scope("experts"):
        partial = expert_all(me.reshape(1), gathered, routes, moe_gain, gate_up, down_weight)
        combined = lax.psum_scatter(partial, ("dp", "ep"), scatter_dimension=0, tiled=True)
        own = lax.dynamic_slice(
            gathered,
            (lax.axis_index("dp"), 0, my_lane * tokens, 0),
            (1, lanes, tokens, cols),
        )[0]
        own = own.transpose(1, 0, 2).reshape(tokens, width)
        mixed_out = (own.astype(F32) + combined.astype(F32)).astype(BF16)

    with jax.named_scope("landed"):
        own_pay = payload[order[:cap]]
        all_pay = jnp.concatenate([own_pay] + arrived_pay, axis=0)
        place = all_pay[:, 0, kw + vw + heads].astype(jnp.int32)
        moved_out = landed_states(order, place, states, arrived, all_pay, kw, vw)
    return mixed_out.reshape(requests, steps, width), moved_out


def solution(mesh):
    row = P(("dp", "ep"), None, None)
    placed = (P(("dp", "ep"), None, None, None),) + (row,) * 9 + (
        P(None, "ep"), P(), P(), row, row, P(("dp", "ep")),
    )
    return jax.shard_map(
        shards,
        mesh=mesh,
        in_specs=placed,
        out_specs=(row, P(("dp", "ep"), None, None, None)),
        check_vma=False,
    )
```

```python
import functools

import jax
import jax.numpy as jnp
from jax import lax
from jax.experimental import pallas as pl
from jax.experimental.pallas import tpu as pltpu
from jax.sharding import PartitionSpec as P

EPS = 1e-06
F32 = jnp.float32
BF16 = jnp.bfloat16
MIB = 1 << 20


def row_sum(x):
    return jnp.sum(x, axis=-1, keepdims=True)


def spread_rows(ref, scratch, requests, steps):
    for r in range(requests):
        split_heads(ref[r].astype(F32), scratch, r, steps)


def split_heads(values, scratch, r, steps):
    hd = scratch.shape[-1]
    for h in range(scratch.shape[0]):
        scratch[h, r * steps : (r + 1) * steps, :] = values[:, h * hd : (h + 1) * hd]


def at_step(scratch, t, requests, steps, head=None):
    if head is None:
        return scratch[pl.ds(t, requests, stride=steps), :]
    return scratch[head, pl.ds(t, requests, stride=steps), :]


def recurrence(kh, repeats, steps, requests, hd, k_s, q_s, v_s, a_s, b_s, m_s, emit_out, emit_state):
    per = m_s.shape[1] // requests
    ks = [at_step(k_s, t, requests, steps, kh) for t in range(steps)]
    rk = [lax.rsqrt(row_sum(k * k) + EPS) for k in ks]
    kn = [k * r for k, r in zip(ks, rk)]
    kk = {(i, t): row_sum(kn[i] * kn[t]) for t in range(steps) for i in range(t)}
    if emit_out is not None:
        qs = [at_step(q_s, t, requests, steps, kh) for t in range(steps)]
        rq = [lax.rsqrt(row_sum(q * q) + EPS) * hd**-0.5 for q in qs]
        qn = [q * r for q, r in zip(qs, rq)]
        kq = {(i, t): row_sum(kn[i] * qn[t]) for t in range(steps) for i in range(t + 1)}
    for h in range(kh * repeats, (kh + 1) * repeats):
        decayed = []
        c = None
        for t in range(steps):
            a = at_step(a_s, t, requests, steps)[:, h : h + 1]
            b = at_step(b_s, t, requests, steps)[:, h : h + 1]
            decayed = [w * a for w in decayed]
            c = a if c is None else c * a
            m = (c * rk[t]) * at_step(m_s, t, requests, per, h)
            for i in range(t):
                m = m + kk[i, t] * decayed[i]
            decayed.append((at_step(v_s, t, requests, steps, h) - m) * b)
            if emit_out is not None:
                o = (c * rq[t]) * at_step(m_s, steps + t, requests, per, h)
                for i in range(t + 1):
                    o = o + kq[i, t] * decayed[i]
                emit_out(t, h, o)
        if emit_state is not None:
            emit_state(h, c, [w * r for w, r in zip(decayed, rk)])


def sigmoid_rows(ref, scratch, requests, steps):
    for r in range(requests):
        scratch[r * steps : (r + 1) * steps, : ref.shape[-1]] = jax.nn.sigmoid(ref[r].astype(F32))


def core_kernel(
    lanes, order_ref, home_ref,
    state_ref, q_ref, k_ref, v_ref, g_ref, b_ref, a_ref, gain_ref, out_ref, *rest,
):
    packed, pays = rest[: lanes - 1], rest[lanes - 1 : 2 * lanes - 1]
    k_s, q_s, v_s, g_s, a_s, b_s, m_s, o_s = rest[2 * lanes - 1 :]
    i = pl.program_id(0)
    r = order_ref[i]
    requests, steps, key_width = k_ref.shape
    heads, hd = state_ref.shape[1], state_ref.shape[-1]
    value_width = v_ref.shape[-1]
    key_heads = key_width // hd
    repeats = heads // key_heads
    cap = requests // lanes
    rows = jnp.concatenate([k_ref[r].astype(F32), q_ref[r].astype(F32)], axis=0).astype(BF16)
    base = pl.multiple_of(r * 2 * steps, 2 * steps)
    for h in range(heads):
        kh = h // repeats
        m_s[h, pl.ds(base, 2 * steps), :] = jnp.dot(
            rows[:, kh * hd : (kh + 1) * hd], state_ref[0, h], preferred_element_type=F32
        )
    home = jnp.full((steps, 128), home_ref[i].astype(F32), F32).astype(BF16)
    for d in range(lanes):

        @pl.when(i // cap == d)
        def _():
            if d:
                packed[d - 1][...] = state_ref[...]
            pay = pays[d]
            pay[0, :, :key_width] = k_ref[r]
            pay[0, :, key_width : key_width + value_width] = v_ref[r]
            tail = key_width + value_width
            pay[0, :, tail : tail + heads] = a_ref[r]
            pay[0, :, tail + 128 : tail + 128 + heads] = b_ref[r]
            pay[0, :, tail + 256 : tail + 384] = home

    @pl.when(i == requests - 1)
    def _():
        spread_rows(k_ref, k_s, requests, steps)
        spread_rows(q_ref, q_s, requests, steps)
        spread_rows(v_ref, v_s, requests, steps)
        spread_rows(g_ref, g_s, requests, steps)
        sigmoid_rows(a_ref, a_s, requests, steps)
        sigmoid_rows(b_ref, b_s, requests, steps)
        gain = gain_ref[...]

        def emit(t, h, o):
            gate = at_step(g_s, t, requests, steps, h)
            scaled = o * lax.rsqrt(row_sum(o * o) * (1.0 / hd) + EPS)
            o_s[h, pl.ds(t, requests, stride=steps), :] = scaled * gain * jax.nn.silu(gate)

        for kh in range(key_heads):
            recurrence(kh, repeats, steps, requests, hd, k_s, q_s, v_s, a_s, b_s, m_s, emit, None)
        for h in range(heads):
            out_ref[:, h * hd : (h + 1) * hd] = o_s[h].astype(BF16)


def core_rows(
    order, home, lanes, states, query_rows, key_rows, value_rows, gate_rows, beta_logit, decay_logit, core_gain
):
    requests, heads, hd, _ = states.shape
    steps = key_rows.shape[1]
    kw, vw = key_rows.shape[-1], value_rows.shape[-1]
    cap = requests // lanes
    pay_width = kw + vw + 384
    whole = lambda x: pl.BlockSpec(x.shape, lambda i, *_: (0,) * x.ndim)
    tokens = requests * steps
    gain = core_gain.reshape(1, hd)
    small = (query_rows, key_rows, value_rows, gate_rows, beta_logit, decay_logit, gain)
    slot = lambda d: lambda i, *_: jnp.clip(i - d * cap, 0, cap - 1)
    state_out = lambda d: pl.BlockSpec((1, heads, hd, hd), lambda i, *_: (slot(d)(i), 0, 0, 0))
    pay_out = lambda d: pl.BlockSpec((1, steps, pay_width), lambda i, *_: (slot(d)(i), 0, 0))
    outs = pl.pallas_call(
        functools.partial(core_kernel, lanes),
        grid_spec=pltpu.PrefetchScalarGridSpec(
            num_scalar_prefetch=2,
            grid=(requests,),
            in_specs=[pl.BlockSpec((1, heads, hd, hd), lambda i, order, home: (order[i], 0, 0, 0))]
            + [whole(x) for x in small],
            out_specs=[pl.BlockSpec((tokens, vw), lambda i, *_: (0, 0))]
            + [state_out(d) for d in range(1, lanes)]
            + [pay_out(d) for d in range(lanes)],
            scratch_shapes=[
                pltpu.VMEM((kw // hd, tokens, hd), F32),
                pltpu.VMEM((kw // hd, tokens, hd), F32),
                pltpu.VMEM((heads, tokens, hd), F32),
                pltpu.VMEM((heads, tokens, hd), F32),
                pltpu.VMEM((tokens, 128), F32),
                pltpu.VMEM((tokens, 128), F32),
                pltpu.VMEM((heads, 2 * tokens, hd), F32),
                pltpu.VMEM((heads, tokens, hd), F32),
            ],
        ),
        out_shape=[jax.ShapeDtypeStruct((tokens, vw), BF16)]
        + [jax.ShapeDtypeStruct((cap, heads, hd, hd), BF16)] * (lanes - 1)
        + [jax.ShapeDtypeStruct((cap, steps, pay_width), BF16)] * lanes,
        compiler_params=pltpu.CompilerParams(vmem_limit_bytes=60 * MIB),
        cost_estimate=pl.CostEstimate(flops=20_000_000, bytes_accessed=8 * MIB, transcendentals=100_000),
        name="core_rows",
    )(order, home, states, *small)
    return outs[0], outs[1:lanes], outs[lanes:]


def state_kernel(lanes, kw, vw, heads, order_ref, place_ref, own_ref, *rest):
    sources = (own_ref,) + rest[: lanes - 1]
    pays, out_ref = rest[lanes - 1 : 2 * lanes - 1], rest[2 * lanes - 1]
    k_s, v_s, a_s, b_s, m_s, u_s, c_s, held, ready, in_sem, out_sem = rest[2 * lanes :]
    requests = held.shape[0]
    steps = pays[0].shape[1]
    hd = held.shape[-1]
    repeats = heads // (kw // hd)
    cap = requests // lanes
    copies = []
    for r in range(requests):
        d, j = divmod(r, cap)
        source = own_ref.at[order_ref[j]] if d == 0 else sources[d].at[j]
        copies.append(pltpu.make_async_copy(source, held.at[r], in_sem.at[r]))
        copies[-1].start()
    for r in range(requests):
        rows = slice(r * steps, (r + 1) * steps)
        pay = pays[r // cap][r % cap].astype(F32)
        split_heads(pay[:, :kw], k_s, r, steps)
        split_heads(pay[:, kw : kw + vw], v_s, r, steps)
        a_s[rows, :] = jax.nn.sigmoid(pay[:, kw + vw : kw + vw + 128])
        b_s[rows, :] = jax.nn.sigmoid(pay[:, kw + vw + 128 : kw + vw + 256])
    for r in range(requests):
        copies[r].wait()
        rows = slice(r * steps, (r + 1) * steps)
        for h in range(heads):
            m_s[h, rows, :] = jnp.dot(
                k_s[h // repeats, rows, :].astype(BF16), held[r, h], preferred_element_type=F32
            )

    def emit(h, c, updates):
        c_s[h] = jnp.broadcast_to(c, (requests, hd))
        for t, u in enumerate(updates):
            u_s[h, pl.ds(t, requests, stride=steps), :] = u

    for kh in range(kw // hd):
        recurrence(kh, repeats, steps, requests, hd, k_s, None, v_s, a_s, b_s, m_s, None, emit)
    sent = []
    for r in range(requests):
        slot = r % 2
        if r >= 2:
            sent[r - 2].wait()
        rows = slice(r * steps, (r + 1) * steps)
        for h in range(heads):
            k4 = k_s[h // repeats, rows, :]
            k8 = jnp.concatenate([k4, k4], axis=0).astype(BF16)
            u4 = u_s[h, rows, :]
            high = u4.astype(BF16).astype(F32)
            u8 = jnp.concatenate([high, u4 - high], axis=0).astype(BF16)
            added = lax.dot_general(
                k8, u8, (((0,), (0,)), ((), ())), preferred_element_type=F32
            )
            kept = held[r, h].astype(F32) * c_s[h, r : r + 1, :]
            ready[slot, h] = (kept + added).astype(BF16)
        sent.append(pltpu.make_async_copy(ready.at[slot], out_ref.at[place_ref[r]], out_sem.at[slot]))
        sent[-1].start()
    for c in sent[-2:]:
        c.wait()


def landed_states(order, place, own, arrived, pays, kw, vw):
    requests, heads, hd, _ = own.shape
    steps = pays[0].shape[1]
    lanes = len(pays)
    tokens = requests * steps
    hbm = pl.BlockSpec(memory_space=pl.ANY)
    smem = pl.BlockSpec(memory_space=pltpu.SMEM)
    return pl.pallas_call(
        functools.partial(state_kernel, lanes, kw, vw, heads),
        in_specs=[smem, smem, hbm] + [hbm] * len(arrived) + [pl.BlockSpec(memory_space=pltpu.VMEM)] * lanes,
        out_specs=hbm,
        out_shape=jax.ShapeDtypeStruct(own.shape, BF16),
        scratch_shapes=[
            pltpu.VMEM((kw // hd, tokens, hd), F32),
            pltpu.VMEM((heads, tokens, hd), F32),
            pltpu.VMEM((tokens, 128), F32),
            pltpu.VMEM((tokens, 128), F32),
            pltpu.VMEM((heads, tokens, hd), F32),
            pltpu.VMEM((heads, tokens, hd), F32),
            pltpu.VMEM((heads, requests, hd), F32),
            pltpu.VMEM(own.shape, BF16),
            pltpu.VMEM((2, heads, hd, hd), BF16),
            pltpu.SemaphoreType.DMA((requests,)),
            pltpu.SemaphoreType.DMA((2,)),
        ],
        compiler_params=pltpu.CompilerParams(vmem_limit_bytes=40 * MIB),
        cost_estimate=pl.CostEstimate(flops=20_000_000, bytes_accessed=9 * MIB, transcendentals=10_000),
        name="landed_states",
    )(order, place, own, *arrived, *pays)


def expert_kernel(sides, own_out, where_ref, *rest):
    pieces = rest[: 2 * sides]
    weight_ref, gain_ref, up_ref, down_ref = rest[2 * sides : 2 * sides + 4]
    keeps = rest[2 * sides + 4 : 3 * sides + 4]
    give_ref = rest[3 * sides + 4]
    result_s = rest[-1]
    spans, group_rows, cols = pieces[0].shape
    tokens = give_ref.shape[2]
    width = down_ref.shape[-1]
    hidden_units = down_ref.shape[1]
    e = where_ref[0]
    blocks = [(x, c) for x in range(spans) for c in range(2)]
    values = {}
    for x, c in blocks:
        parts = [pieces[2 * y + c][x] for y in range(sides)]
        values[x, c] = jnp.concatenate(parts, axis=0).astype(F32)
    total = sum(row_sum(values[b] * values[b]) for b in blocks)
    scale = lax.rsqrt(total * (1.0 / width) + EPS)
    joined = None
    for x, c in blocks:
        block = e ^ (2 * x + c)
        normed = (values[x, c] * scale * gain_ref[pl.ds(block, 1), :]).astype(BF16)
        up = up_ref[0, pl.ds(pl.multiple_of(block * cols, cols), cols), :]
        term = jnp.dot(normed, up, preferred_element_type=F32)
        joined = term if joined is None else joined + term
        if own_out:
            rest[3 * sides + 5][:, pl.ds(pl.multiple_of(block * cols, cols), cols)] = pieces[c][
                x, pl.ds(pl.multiple_of(e * tokens, tokens), tokens), :
            ]
    active = (jax.nn.silu(joined[:, :hidden_units]) * joined[:, hidden_units:]).astype(BF16)
    result = jnp.dot(active, down_ref[0], preferred_element_type=F32).astype(BF16)
    eye = lax.broadcasted_iota(jnp.int32, (group_rows, group_rows), 0) == lax.broadcasted_iota(
        jnp.int32, (group_rows, group_rows), 1
    )
    weights = []
    for y in range(sides):
        line = weight_ref[pl.ds(where_ref[1 + y], 1), :]
        weights.append(row_sum(jnp.where(eye, jnp.broadcast_to(line, eye.shape), 0.0)))
    result_s[...] = (result.astype(F32) * jnp.concatenate(weights, axis=0)).astype(BF16)
    for y in range(sides):
        for x in range(spans):
            for c in range(2):
                start = y * group_rows + (e ^ (2 * x + c)) * tokens
                rows = result_s[pl.ds(pl.multiple_of(start, tokens), tokens), :]
                if c:
                    give_ref[y, x] = rows
                else:
                    keeps[y][x] = rows


def expert_chunk(where, pieces, weights, gain, gate_up, down_weight, tokens, own_out):
    sides = len(pieces) // 2
    spans, group_rows, cols = pieces[0].shape
    width = down_weight.shape[-1]
    vmem = pl.BlockSpec(memory_space=pltpu.VMEM)
    keep = jax.ShapeDtypeStruct((spans, tokens, width), BF16)
    give = jax.ShapeDtypeStruct((sides, spans, tokens, width), BF16)
    own = [jax.ShapeDtypeStruct((tokens, width), BF16)] if own_out else []
    rows = sides * group_rows
    outs = pl.pallas_call(
        functools.partial(expert_kernel, sides, own_out),
        in_specs=[pl.BlockSpec(memory_space=pltpu.SMEM)] + [vmem] * (len(pieces) + 4),
        out_specs=[vmem] * (sides + 1 + len(own)),
        out_shape=[keep] * sides + [give] + own,
        scratch_shapes=[pltpu.VMEM((rows, width), BF16)],
        compiler_params=pltpu.CompilerParams(vmem_limit_bytes=32 * MIB),
        cost_estimate=pl.CostEstimate(
            flops=6 * rows * width * down_weight.shape[1], bytes_accessed=6 * MIB, transcendentals=0
        ),
        name="expert_chunk",
    )(where, *pieces, weights, gain, gate_up, down_weight)
    return outs


def swap(x, axis, d):
    size = lax.axis_size(axis)
    return lax.ppermute(x, axis, [(i, i ^ d) for i in range(size)])


def summed(*terms):
    return functools.reduce(lambda p, q: p + q, [t.astype(F32) for t in terms])


def shards(
    states, query_rows, key_rows, value_rows, gate_rows, beta_logit, decay_logit, residual,
    route_ids, route_prob, out_weight, core_gain, moe_gain, gate_up, down_weight, new_home,
):
    requests, heads, hd, _ = states.shape
    steps = query_rows.shape[1]
    width = residual.shape[-1]
    tokens = requests * steps
    lanes = lax.axis_size("ep")
    groups = lax.axis_size("dp")
    my_lane = lax.axis_index("ep")
    my_group = lax.axis_index("dp")
    cap = requests // lanes
    kw, vw = key_rows.shape[-1], value_rows.shape[-1]
    top = route_ids.shape[-1]

    with jax.named_scope("order"):
        lane = (new_home // requests % lanes) ^ my_lane
        ids = jnp.arange(requests, dtype=jnp.int32)
        earlier = (lane[:, None] == lane[None, :]) & (ids[None, :] < ids[:, None])
        slot = lane * cap + jnp.sum(earlier.astype(jnp.int32), axis=1)
        placed = slot[:, None] == ids[None, :]
        order = jnp.sum(jnp.where(placed, ids[:, None], 0), axis=0)
        home = jnp.sum(jnp.where(placed, new_home[:, None] % requests, 0), axis=0)

    with jax.named_scope("routes"):
        weights = route_prob.reshape(tokens, top)
        weights = weights / jnp.sum(weights, -1, keepdims=True)
        named = route_ids.reshape(tokens, top)[None] == jnp.arange(groups * lanes, dtype=jnp.int32)[:, None, None]
        weights = jnp.sum(jnp.where(named, weights[None], 0.0), axis=-1)
        weights = lax.all_to_all(weights, ("dp", "ep"), split_axis=0, concat_axis=0, tiled=True)
        weights = weights.reshape(groups, lanes * tokens)

    with jax.named_scope("core"):
        group_residual = lax.all_gather(residual.reshape(tokens, width), "ep", axis=0, tiled=True)
        core, packed, pays = core_rows(
            order, home, lanes, states, query_rows, key_rows, value_rows, gate_rows, beta_logit,
            decay_logit, core_gain,
        )
        core, group_residual, weights = lax.optimization_barrier((core, group_residual, weights))
        group_core = lax.all_gather(core, "ep", axis=0, tiled=True)
    with jax.named_scope("attention"):
        cols = out_weight.shape[1]
        attention = jnp.dot(group_core, out_weight, preferred_element_type=F32).astype(BF16)
        before = lax.dynamic_slice_in_dim(group_residual, my_lane * cols, cols, axis=1)
        hidden_cols = (before.astype(F32) + attention.astype(F32)).astype(BF16)
        held = jnp.stack([hidden_cols] + [swap(hidden_cols, "ep", d) for d in range(2, lanes, 2)])
        held, packed, pays = lax.optimization_barrier((held, packed, pays))

    with jax.named_scope("send_states"):
        arrived = [swap(packed[d - 1], "ep", d) for d in range(1, lanes)]
        arrived_pays = [pays[0]] + [swap(pays[d], "ep", d) for d in range(1, lanes)]

    gain = moe_gain.reshape(lanes, cols)
    sums = []
    own_rows = None
    for d in range(0, groups, 2):
        with jax.named_scope("tokens"):
            near = swap(held, "dp", d) if d else held
            across = swap(near, "dp", 1)
            pieces = [near, swap(near, "ep", 1), across, swap(across, "ep", 1)]
        with jax.named_scope("experts"):
            where = jnp.stack([my_lane, my_group ^ d, my_group ^ d ^ 1])
            outs = expert_chunk(where, pieces, weights, gain, gate_up, down_weight, tokens, d == 0)
            keep_near, keep_across, give = outs[:3]
            if d == 0:
                own_rows = outs[3]
        with jax.named_scope("way_back"):
            got = swap(give, "ep", 1)
            back = swap(summed(keep_across, got[1]).astype(BF16), "dp", 1)
            chunk = summed(keep_near, got[0], back)
            sums.append(swap(chunk.astype(BF16), "dp", d) if d else chunk)
    with jax.named_scope("mixed"):
        mixed = summed(own_rows, *[s[0] for s in sums])
        for x in range(1, lanes // 2):
            mixed = mixed + swap(summed(*[s[x] for s in sums]).astype(BF16), "ep", 2 * x).astype(F32)
        mixed_out = mixed.astype(BF16)

    with jax.named_scope("landed"):
        place = jnp.concatenate([p[:, 0, kw + vw + 256] for p in arrived_pays]).astype(jnp.int32)
        moved_out = landed_states(order, place, states, arrived, arrived_pays, kw, vw)
    return mixed_out.reshape(requests, steps, width), moved_out


def solution(mesh):
    row = P(("dp", "ep"), None, None)
    placed = (P(("dp", "ep"), None, None, None),) + (row,) * 9 + (
        P(None, "ep"), P(), P(), row, row, P(("dp", "ep")),
    )
    return jax.shard_map(
        shards,
        mesh=mesh,
        in_specs=placed,
        out_specs=(row, P(("dp", "ep"), None, None, None)),
        check_vma=False,
    )
```

```python
import functools

import jax
import jax.numpy as jnp
from jax import lax
from jax.experimental import pallas as pl
from jax.experimental.pallas import tpu as pltpu
from jax.sharding import PartitionSpec as P

EPS = 1e-06
F32 = jnp.float32
BF16 = jnp.bfloat16
MIB = 1 << 20


def row_sum(x):
    return jnp.sum(x, axis=-1, keepdims=True)


def spread_rows(ref, scratch, requests, steps):
    for r in range(requests):
        split_heads(ref[r].astype(F32), scratch, r, steps)


def split_heads(values, scratch, r, steps):
    hd = scratch.shape[-1]
    for h in range(scratch.shape[0]):
        scratch[h, r * steps : (r + 1) * steps, :] = values[:, h * hd : (h + 1) * hd]


def at_step(scratch, t, requests, steps, head=None):
    if head is None:
        return scratch[pl.ds(t, requests, stride=steps), :]
    return scratch[head, pl.ds(t, requests, stride=steps), :]


def recurrence(kh, repeats, steps, requests, hd, k_s, q_s, v_s, a_s, b_s, m_s, emit_out, emit_state):
    per = m_s.shape[1] // requests
    ks = [at_step(k_s, t, requests, steps, kh) for t in range(steps)]
    rk = [lax.rsqrt(row_sum(k * k) + EPS) for k in ks]
    kn = [k * r for k, r in zip(ks, rk)]
    kk = {(i, t): row_sum(kn[i] * kn[t]) for t in range(steps) for i in range(t)}
    if emit_out is not None:
        qs = [at_step(q_s, t, requests, steps, kh) for t in range(steps)]
        rq = [lax.rsqrt(row_sum(q * q) + EPS) * hd**-0.5 for q in qs]
        qn = [q * r for q, r in zip(qs, rq)]
        kq = {(i, t): row_sum(kn[i] * qn[t]) for t in range(steps) for i in range(t + 1)}
    for h in range(kh * repeats, (kh + 1) * repeats):
        decayed = []
        c = None
        for t in range(steps):
            a = at_step(a_s, t, requests, steps)[:, h : h + 1]
            b = at_step(b_s, t, requests, steps)[:, h : h + 1]
            decayed = [w * a for w in decayed]
            c = a if c is None else c * a
            m = (c * rk[t]) * at_step(m_s, t, requests, per, h)
            for i in range(t):
                m = m + kk[i, t] * decayed[i]
            decayed.append((at_step(v_s, t, requests, steps, h) - m) * b)
            if emit_out is not None:
                o = (c * rq[t]) * at_step(m_s, steps + t, requests, per, h)
                for i in range(t + 1):
                    o = o + kq[i, t] * decayed[i]
                emit_out(t, h, o)
        if emit_state is not None:
            emit_state(h, c, [w * r for w, r in zip(decayed, rk)])


def sigmoid_rows(ref, scratch, requests, steps):
    for r in range(requests):
        scratch[r * steps : (r + 1) * steps, : ref.shape[-1]] = jax.nn.sigmoid(ref[r].astype(F32))


def packed_rows(key_heads, heads, steps):
    used = (key_heads + heads + 3) * steps
    return used, -(-used // 16) * 16


def core_kernel(
    lanes, home_ref, state_ref, q_ref, k_ref, v_ref, g_ref, b_ref, a_ref, gain_ref, out_ref, packed_ref,
    k_s, q_s, v_s, g_s, a_s, b_s, m_s, o_s, held, pay_f, pay_s, in_sem, out_sem,
):
    requests, steps, _ = k_ref.shape
    hd = held.shape[-1]
    heads, key_heads = v_s.shape[0], k_s.shape[0]
    repeats = heads // key_heads
    cap = requests // lanes
    copies = []
    for r in range(requests):
        copies.append(pltpu.make_async_copy(state_ref.at[r], held.at[r], in_sem.at[r]))
        copies[-1].start()
    spread_rows(k_ref, k_s, requests, steps)
    spread_rows(q_ref, q_s, requests, steps)
    spread_rows(v_ref, v_s, requests, steps)
    spread_rows(g_ref, g_s, requests, steps)
    sigmoid_rows(a_ref, a_s, requests, steps)
    sigmoid_rows(b_ref, b_s, requests, steps)
    target = [lax.rem(lax.div(home_ref[r], requests), lanes) for r in range(requests)]
    slots = [
        target[r] * cap + sum([(target[p] == target[r]).astype(jnp.int32) for p in range(r)], jnp.int32(0))
        for r in range(requests)
    ]
    state_rows = heads * hd
    sent = []
    pay_f[...] = jnp.zeros_like(pay_f)
    for r in range(requests):
        rows = slice(r * steps, (r + 1) * steps)
        for kh in range(key_heads):
            pay_f[kh * steps : (kh + 1) * steps, :] = k_s[kh, rows, :]
        for h in range(heads):
            at = (key_heads + h) * steps
            pay_f[at : at + steps, :] = v_s[h, rows, :]
        at = (key_heads + heads) * steps
        pay_f[at : at + steps, :heads] = a_ref[r].astype(F32)
        pay_f[at + steps : at + 2 * steps, :heads] = b_ref[r].astype(F32)
        place = lax.rem(home_ref[r], requests).astype(F32)
        pay_f[at + 2 * steps : at + 3 * steps, :] = jnp.full((steps, hd), place, F32)
        pay_s[r] = pay_f[...].astype(BF16)
        sent.append(
            pltpu.make_async_copy(
                pay_s.at[r], packed_ref.at[slots[r], pl.ds(state_rows, pay_s.shape[1])], out_sem.at[0, r]
            )
        )
        sent[-1].start()
    for r in range(requests):
        copies[r].wait()
        rows = slice(r * steps, (r + 1) * steps)
        for kh in range(key_heads):
            left = jnp.concatenate([k_s[kh, rows, :], q_s[kh, rows, :]], axis=0).astype(BF16)
            for h in range(kh * repeats, (kh + 1) * repeats):
                m_s[h, r * 2 * steps : (r + 1) * 2 * steps, :] = jnp.dot(
                    left, held[r, h * hd : (h + 1) * hd, :], preferred_element_type=F32
                )
        sent.append(
            pltpu.make_async_copy(
                held.at[r], packed_ref.at[slots[r], pl.ds(0, state_rows)], out_sem.at[1, r]
            )
        )
        sent[-1].start()
    gain = gain_ref[...]

    def emit(t, h, o):
        gate = at_step(g_s, t, requests, steps, h)
        scaled = o * lax.rsqrt(row_sum(o * o) * (1.0 / hd) + EPS)
        o_s[h, pl.ds(t, requests, stride=steps), :] = scaled * gain * jax.nn.silu(gate)

    for kh in range(key_heads):
        recurrence(kh, repeats, steps, requests, hd, k_s, q_s, v_s, a_s, b_s, m_s, emit, None)
    for h in range(heads):
        out_ref[:, h * hd : (h + 1) * hd] = o_s[h].astype(BF16)
    for c in sent:
        c.wait()


def core_rows(
    home, lanes, states, query_rows, key_rows, value_rows, gate_rows, beta_logit, decay_logit, core_gain
):
    requests, heads, hd, _ = states.shape
    steps = key_rows.shape[1]
    kw, vw = key_rows.shape[-1], value_rows.shape[-1]
    tokens = requests * steps
    _, pay_rows = packed_rows(kw // hd, heads, steps)
    vmem, hbm = pl.BlockSpec(memory_space=pltpu.VMEM), pl.BlockSpec(memory_space=pl.ANY)
    return pl.pallas_call(
        functools.partial(core_kernel, lanes),
        in_specs=[pl.BlockSpec(memory_space=pltpu.SMEM), hbm] + [vmem] * 7,
        out_specs=[vmem, hbm],
        out_shape=[
            jax.ShapeDtypeStruct((tokens, vw), BF16),
            jax.ShapeDtypeStruct((requests, heads * hd + pay_rows, hd), BF16),
        ],
        scratch_shapes=[
            pltpu.VMEM((kw // hd, tokens, hd), F32),
            pltpu.VMEM((kw // hd, tokens, hd), F32),
            pltpu.VMEM((heads, tokens, hd), F32),
            pltpu.VMEM((heads, tokens, hd), F32),
            pltpu.VMEM((tokens, 128), F32),
            pltpu.VMEM((tokens, 128), F32),
            pltpu.VMEM((heads, 2 * tokens, hd), F32),
            pltpu.VMEM((heads, tokens, hd), F32),
            pltpu.VMEM((requests, heads * hd, hd), BF16),
            pltpu.VMEM((pay_rows, hd), F32),
            pltpu.VMEM((requests, pay_rows, hd), BF16),
            pltpu.SemaphoreType.DMA((requests,)),
            pltpu.SemaphoreType.DMA((2, requests)),
        ],
        compiler_params=pltpu.CompilerParams(vmem_limit_bytes=60 * MIB),
        cost_estimate=pl.CostEstimate(flops=20_000_000, bytes_accessed=9 * MIB, transcendentals=100_000),
        name="core_rows",
    )(
        home, states.reshape(requests, heads * hd, hd), query_rows, key_rows, value_rows, gate_rows,
        beta_logit, decay_logit, core_gain.reshape(1, hd),
    )


def state_kernel(
    key_heads, heads, steps, place_ref, arrived_ref, out_ref,
    k_s, v_s, a_s, b_s, m_s, u_s, c_s, held, pay_s, ready, in_sem, pay_sem, out_sem,
):
    requests, state_rows, hd = held.shape
    repeats = heads // key_heads
    pays, copies = [], []
    for r in range(requests):
        pays.append(
            pltpu.make_async_copy(
                arrived_ref.at[r, pl.ds(state_rows, pay_s.shape[1])], pay_s.at[r], pay_sem.at[r]
            )
        )
        pays[-1].start()
    for r in range(requests):
        copies.append(
            pltpu.make_async_copy(arrived_ref.at[r, pl.ds(0, state_rows)], held.at[r], in_sem.at[r])
        )
        copies[-1].start()
    for r in range(requests):
        pays[r].wait()
        rows = slice(r * steps, (r + 1) * steps)
        pay = pay_s[r].astype(F32)
        for kh in range(key_heads):
            k_s[kh, rows, :] = pay[kh * steps : (kh + 1) * steps]
        for h in range(heads):
            v_s[h, rows, :] = pay[(key_heads + h) * steps : (key_heads + h + 1) * steps]
        at = (key_heads + heads) * steps
        a_s[rows, :] = jax.nn.sigmoid(pay[at : at + steps])
        b_s[rows, :] = jax.nn.sigmoid(pay[at + steps : at + 2 * steps])
    for r in range(requests):
        copies[r].wait()
        rows = slice(r * steps, (r + 1) * steps)
        for h in range(heads):
            m_s[h, rows, :] = jnp.dot(
                k_s[h // repeats, rows, :].astype(BF16),
                held[r, h * hd : (h + 1) * hd, :],
                preferred_element_type=F32,
            )

    def emit(h, c, updates):
        c_s[h] = jnp.broadcast_to(c, (requests, hd))
        for t, u in enumerate(updates):
            u_s[h, pl.ds(t, requests, stride=steps), :] = u

    for kh in range(key_heads):
        recurrence(kh, repeats, steps, requests, hd, k_s, None, v_s, a_s, b_s, m_s, None, emit)
    sent = []
    for r in range(requests):
        slot = r % 2
        if r >= 2:
            sent[r - 2].wait()
        rows = slice(r * steps, (r + 1) * steps)
        for h in range(heads):
            k4 = k_s[h // repeats, rows, :]
            k8 = jnp.concatenate([k4, k4], axis=0).astype(BF16)
            u4 = u_s[h, rows, :]
            high = u4.astype(BF16).astype(F32)
            u8 = jnp.concatenate([high, u4 - high], axis=0).astype(BF16)
            added = lax.dot_general(
                k8, u8, (((0,), (0,)), ((), ())), preferred_element_type=F32
            )
            kept = held[r, h * hd : (h + 1) * hd, :].astype(F32) * c_s[h, r : r + 1, :]
            ready[slot, h * hd : (h + 1) * hd, :] = (kept + added).astype(BF16)
        sent.append(pltpu.make_async_copy(ready.at[slot], out_ref.at[place_ref[r]], out_sem.at[slot]))
        sent[-1].start()
    for c in sent[-2:]:
        c.wait()


def landed_states(place, arrived, key_heads, heads, steps):
    requests, all_rows, hd = arrived.shape
    tokens = requests * steps
    state_rows = heads * hd
    hbm = pl.BlockSpec(memory_space=pl.ANY)
    out = pl.pallas_call(
        functools.partial(state_kernel, key_heads, heads, steps),
        in_specs=[pl.BlockSpec(memory_space=pltpu.SMEM), hbm],
        out_specs=hbm,
        out_shape=jax.ShapeDtypeStruct((requests, state_rows, hd), BF16),
        scratch_shapes=[
            pltpu.VMEM((key_heads, tokens, hd), F32),
            pltpu.VMEM((heads, tokens, hd), F32),
            pltpu.VMEM((tokens, hd), F32),
            pltpu.VMEM((tokens, hd), F32),
            pltpu.VMEM((heads, tokens, hd), F32),
            pltpu.VMEM((heads, tokens, hd), F32),
            pltpu.VMEM((heads, requests, hd), F32),
            pltpu.VMEM((requests, state_rows, hd), BF16),
            pltpu.VMEM((requests, all_rows - state_rows, hd), BF16),
            pltpu.VMEM((2, state_rows, hd), BF16),
            pltpu.SemaphoreType.DMA((requests,)),
            pltpu.SemaphoreType.DMA((requests,)),
            pltpu.SemaphoreType.DMA((2,)),
        ],
        compiler_params=pltpu.CompilerParams(vmem_limit_bytes=32 * MIB),
        cost_estimate=pl.CostEstimate(flops=20_000_000, bytes_accessed=9 * MIB, transcendentals=10_000),
        name="landed_states",
    )(place, arrived)
    return out.reshape(requests, heads, hd, hd)


def expert_kernel(sides, own_out, where_ref, *rest):
    pieces = rest[: 2 * sides]
    weight_ref, gain_ref, up_ref, down_ref = rest[2 * sides : 2 * sides + 4]
    keeps = rest[2 * sides + 4 : 3 * sides + 4]
    give_ref = rest[3 * sides + 4]
    result_s = rest[-1]
    spans, group_rows, cols = pieces[0].shape
    tokens = give_ref.shape[2]
    width = down_ref.shape[-1]
    hidden_units = down_ref.shape[1]
    e = where_ref[0]
    blocks = [(x, c) for x in range(spans) for c in range(2)]
    values = {}
    for x, c in blocks:
        parts = [pieces[2 * y + c][x] for y in range(sides)]
        values[x, c] = jnp.concatenate(parts, axis=0).astype(F32)
    total = sum(row_sum(values[b] * values[b]) for b in blocks)
    scale = lax.rsqrt(total * (1.0 / width) + EPS)
    joined = None
    for x, c in blocks:
        block = e ^ (2 * x + c)
        normed = (values[x, c] * scale * gain_ref[pl.ds(block, 1), :]).astype(BF16)
        up = up_ref[0, pl.ds(pl.multiple_of(block * cols, cols), cols), :]
        term = jnp.dot(normed, up, preferred_element_type=F32)
        joined = term if joined is None else joined + term
        if own_out:
            rest[3 * sides + 5][:, pl.ds(pl.multiple_of(block * cols, cols), cols)] = pieces[c][
                x, pl.ds(pl.multiple_of(e * tokens, tokens), tokens), :
            ]
    active = (jax.nn.silu(joined[:, :hidden_units]) * joined[:, hidden_units:]).astype(BF16)
    result = jnp.dot(active, down_ref[0], preferred_element_type=F32).astype(BF16)
    eye = lax.broadcasted_iota(jnp.int32, (group_rows, group_rows), 0) == lax.broadcasted_iota(
        jnp.int32, (group_rows, group_rows), 1
    )
    weights = []
    for y in range(sides):
        line = weight_ref[pl.ds(where_ref[1 + y], 1), :]
        weights.append(row_sum(jnp.where(eye, jnp.broadcast_to(line, eye.shape), 0.0)))
    result_s[...] = (result.astype(F32) * jnp.concatenate(weights, axis=0)).astype(BF16)
    for y in range(sides):
        for x in range(spans):
            for c in range(2):
                start = y * group_rows + (e ^ (2 * x + c)) * tokens
                rows = result_s[pl.ds(pl.multiple_of(start, tokens), tokens), :]
                if c:
                    give_ref[y, x] = rows
                else:
                    keeps[y][x] = rows


def expert_chunk(where, pieces, weights, gain, gate_up, down_weight, tokens, own_out):
    sides = len(pieces) // 2
    spans, group_rows, cols = pieces[0].shape
    width = down_weight.shape[-1]
    vmem = pl.BlockSpec(memory_space=pltpu.VMEM)
    keep = jax.ShapeDtypeStruct((spans, tokens, width), BF16)
    give = jax.ShapeDtypeStruct((sides, spans, tokens, width), BF16)
    own = [jax.ShapeDtypeStruct((tokens, width), BF16)] if own_out else []
    rows = sides * group_rows
    outs = pl.pallas_call(
        functools.partial(expert_kernel, sides, own_out),
        in_specs=[pl.BlockSpec(memory_space=pltpu.SMEM)] + [vmem] * (len(pieces) + 4),
        out_specs=[vmem] * (sides + 1 + len(own)),
        out_shape=[keep] * sides + [give] + own,
        scratch_shapes=[pltpu.VMEM((rows, width), BF16)],
        compiler_params=pltpu.CompilerParams(vmem_limit_bytes=32 * MIB),
        cost_estimate=pl.CostEstimate(
            flops=6 * rows * width * down_weight.shape[1], bytes_accessed=6 * MIB, transcendentals=0
        ),
        name="expert_chunk",
    )(where, *pieces, weights, gain, gate_up, down_weight)
    return outs


def swap(x, axis, d):
    size = lax.axis_size(axis)
    return lax.ppermute(x, axis, [(i, i ^ d) for i in range(size)])


def summed(*terms):
    return functools.reduce(lambda p, q: p + q, [t.astype(F32) for t in terms])


def shards(
    states, query_rows, key_rows, value_rows, gate_rows, beta_logit, decay_logit, residual,
    route_ids, route_prob, out_weight, core_gain, moe_gain, gate_up, down_weight, new_home,
):
    requests, heads, hd, _ = states.shape
    steps = query_rows.shape[1]
    width = residual.shape[-1]
    tokens = requests * steps
    lanes = lax.axis_size("ep")
    groups = lax.axis_size("dp")
    my_lane = lax.axis_index("ep")
    my_group = lax.axis_index("dp")
    kw, vw = key_rows.shape[-1], value_rows.shape[-1]
    top = route_ids.shape[-1]

    experts = groups * lanes
    cols = out_weight.shape[1]
    everyone = functools.partial(lax.all_to_all, split_axis=0, concat_axis=0, tiled=True)

    with jax.named_scope("core"):
        before = lax.all_to_all(
            residual.reshape(tokens, width), "ep", split_axis=1, concat_axis=0, tiled=True
        )
        core, packed = core_rows(
            new_home, lanes, states, query_rows, key_rows, value_rows, gate_rows, beta_logit,
            decay_logit, core_gain,
        )
        group_core = lax.all_gather(core, "ep", axis=0, tiled=True)
    with jax.named_scope("attention"):
        attention = jnp.dot(group_core, out_weight, preferred_element_type=F32).astype(BF16)
        hidden_cols = (before.astype(F32) + attention.astype(F32)).astype(BF16)
        held = jnp.stack([hidden_cols] + [swap(hidden_cols, "ep", d) for d in range(2, lanes, 2)])
        held, packed = lax.optimization_barrier((held, packed))
        first_across = swap(held, "dp", 1)
    with jax.named_scope("send_states"):
        arrived = everyone(packed, "ep")
    with jax.named_scope("routes"):
        route_prob, first_across = lax.optimization_barrier((route_prob, first_across))
        weights = route_prob.reshape(tokens, top)
        weights = weights / jnp.sum(weights, -1, keepdims=True)
        named = route_ids.reshape(tokens, top)[None] == jnp.arange(experts, dtype=jnp.int32)[:, None, None]
        weights = jnp.sum(jnp.where(named, weights[None], 0.0), axis=-1)
        weights = everyone(weights, ("dp", "ep")).reshape(groups, lanes * tokens)

    gain = moe_gain.reshape(lanes, cols)
    sums = []
    own_rows = None
    for d in range(0, groups, 2):
        with jax.named_scope("tokens"):
            near = swap(held, "dp", d) if d else held
            across = swap(near, "dp", 1) if d else first_across
            pieces = [near, swap(near, "ep", 1), across, swap(across, "ep", 1)]
        with jax.named_scope("experts"):
            where = jnp.stack([my_lane, my_group ^ d, my_group ^ d ^ 1])
            outs = expert_chunk(where, pieces, weights, gain, gate_up, down_weight, tokens, d == 0)
            keep_near, keep_across, give = outs[:3]
            if d == 0:
                own_rows = outs[3]
        with jax.named_scope("way_back"):
            got = swap(give, "ep", 1)
            back = swap(summed(keep_across, got[1]).astype(BF16), "dp", 1)
            chunk = summed(keep_near, got[0], back)
            sums.append(swap(chunk.astype(BF16), "dp", d) if d else chunk)
    with jax.named_scope("landed"):
        place_row = heads * hd + (kw // hd + heads + 2) * steps
        place = arrived[:, place_row, 0].astype(jnp.int32)
        moved_out = landed_states(place, arrived, kw // hd, heads, steps)
        sums, moved_out = lax.optimization_barrier((sums, moved_out))
    with jax.named_scope("mixed"):
        mixed = summed(own_rows, *[s[0] for s in sums])
        for x in range(1, lanes // 2):
            mixed = mixed + swap(summed(*[s[x] for s in sums]).astype(BF16), "ep", 2 * x).astype(F32)
        mixed_out = mixed.astype(BF16)
    return mixed_out.reshape(requests, steps, width), moved_out


def solution(mesh):
    row = P(("dp", "ep"), None, None)
    placed = (P(("dp", "ep"), None, None, None),) + (row,) * 9 + (
        P(None, "ep"), P(), P(), row, row, P(("dp", "ep")),
    )
    return jax.shard_map(
        shards,
        mesh=mesh,
        in_specs=placed,
        out_specs=(row, P(("dp", "ep"), None, None, None)),
        check_vma=False,
    )
```

```python
import functools

import jax
import jax.numpy as jnp
from jax import lax
from jax.experimental import pallas as pl
from jax.experimental.pallas import tpu as pltpu
from jax.sharding import PartitionSpec as P

EPS = 1e-06
F32 = jnp.float32
BF16 = jnp.bfloat16
MIB = 1 << 20


def row_sum(x):
    return jnp.sum(x, axis=-1, keepdims=True)


def spread_rows(ref, scratch, requests, steps):
    for r in range(requests):
        split_heads(ref[r].astype(F32), scratch, r, steps)


def split_heads(values, scratch, r, steps):
    hd = scratch.shape[-1]
    for h in range(scratch.shape[0]):
        scratch[h, r * steps : (r + 1) * steps, :] = values[:, h * hd : (h + 1) * hd]


def at_step(scratch, t, requests, steps, head=None):
    if head is None:
        return scratch[pl.ds(t, requests, stride=steps), :]
    return scratch[head, pl.ds(t, requests, stride=steps), :]


def recurrence(kh, repeats, steps, requests, hd, k_s, q_s, v_s, a_s, b_s, m_s, emit_out, emit_state):
    per = m_s.shape[1] // requests
    ks = [at_step(k_s, t, requests, steps, kh) for t in range(steps)]
    rk = [lax.rsqrt(row_sum(k * k) + EPS) for k in ks]
    kn = [k * r for k, r in zip(ks, rk)]
    kk = {(i, t): row_sum(kn[i] * kn[t]) for t in range(steps) for i in range(t)}
    if emit_out is not None:
        qs = [at_step(q_s, t, requests, steps, kh) for t in range(steps)]
        rq = [lax.rsqrt(row_sum(q * q) + EPS) * hd**-0.5 for q in qs]
        qn = [q * r for q, r in zip(qs, rq)]
        kq = {(i, t): row_sum(kn[i] * qn[t]) for t in range(steps) for i in range(t + 1)}
    for h in range(kh * repeats, (kh + 1) * repeats):
        decayed = []
        c = None
        for t in range(steps):
            a = at_step(a_s, t, requests, steps)[:, h : h + 1]
            b = at_step(b_s, t, requests, steps)[:, h : h + 1]
            decayed = [w * a for w in decayed]
            c = a if c is None else c * a
            m = (c * rk[t]) * at_step(m_s, t, requests, per, h)
            for i in range(t):
                m = m + kk[i, t] * decayed[i]
            decayed.append((at_step(v_s, t, requests, steps, h) - m) * b)
            if emit_out is not None:
                o = (c * rq[t]) * at_step(m_s, steps + t, requests, per, h)
                for i in range(t + 1):
                    o = o + kq[i, t] * decayed[i]
                emit_out(t, h, o)
        if emit_state is not None:
            emit_state(h, c, [w * r for w, r in zip(decayed, rk)])


def sigmoid_rows(ref, scratch, requests, steps):
    for r in range(requests):
        scratch[r * steps : (r + 1) * steps, : ref.shape[-1]] = jax.nn.sigmoid(ref[r].astype(F32))


def packed_rows(key_heads, heads, steps):
    used = (key_heads + heads + 3) * steps
    return used, -(-used // 16) * 16


def core_kernel(
    lanes, experts, home_ref, lane_ref, state_ref, q_ref, k_ref, v_ref, g_ref, b_ref, a_ref, gain_ref,
    res_ref, ids_ref, prob_ref, out_ref, *rest,
):
    packed = rest[:lanes]
    k_s, q_s, v_s, g_s, a_s, b_s, m_s, o_s, r_s, w_s, held, pay_f, pay_s, in_sem, out_sem = rest[lanes:]
    requests, steps, _ = k_ref.shape
    hd = held.shape[-1]
    heads, key_heads = v_s.shape[0], k_s.shape[0]
    repeats = heads // key_heads
    cap = requests // lanes
    copies = []
    for r in range(requests):
        copies.append(pltpu.make_async_copy(state_ref.at[r], held.at[r], in_sem.at[r]))
        copies[-1].start()
    spread_rows(k_ref, k_s, requests, steps)
    spread_rows(q_ref, q_s, requests, steps)
    spread_rows(v_ref, v_s, requests, steps)
    spread_rows(g_ref, g_s, requests, steps)
    sigmoid_rows(a_ref, a_s, requests, steps)
    sigmoid_rows(b_ref, b_s, requests, steps)
    target = [lax.rem(lax.div(home_ref[r], requests), lanes) ^ lane_ref[0] for r in range(requests)]
    ranks = [
        sum([(target[p] == target[r]).astype(jnp.int32) for p in range(r)], jnp.int32(0))
        for r in range(requests)
    ]
    state_rows = heads * hd

    def send(source, r, start, kind):
        rows = pl.ds(start, source.shape[0])
        for d in range(lanes):

            @pl.when(target[r] == d)
            def _():
                pltpu.make_async_copy(
                    source, packed[d].at[ranks[r], rows], out_sem.at[kind, r]
                ).start()

        return pltpu.make_async_copy(source, packed[0].at[0, rows], out_sem.at[kind, r])

    sent = []
    pay_f[...] = jnp.zeros_like(pay_f)
    for r in range(requests):
        rows = slice(r * steps, (r + 1) * steps)
        for kh in range(key_heads):
            pay_f[kh * steps : (kh + 1) * steps, :] = k_s[kh, rows, :]
        for h in range(heads):
            at = (key_heads + h) * steps
            pay_f[at : at + steps, :] = v_s[h, rows, :]
        at = (key_heads + heads) * steps
        pay_f[at : at + steps, :heads] = a_ref[r].astype(F32)
        pay_f[at + steps : at + 2 * steps, :heads] = b_ref[r].astype(F32)
        place = lax.rem(home_ref[r], requests).astype(F32)
        pay_f[at + 2 * steps : at + 3 * steps, :] = jnp.full((steps, hd), place, F32)
        pay_s[r] = pay_f[...].astype(BF16)
        sent.append(send(pay_s.at[r], r, state_rows, 0))
    for r in range(requests):
        copies[r].wait()
        rows = slice(r * steps, (r + 1) * steps)
        for kh in range(key_heads):
            left = jnp.concatenate([k_s[kh, rows, :], q_s[kh, rows, :]], axis=0).astype(BF16)
            for h in range(kh * repeats, (kh + 1) * repeats):
                m_s[h, r * 2 * steps : (r + 1) * 2 * steps, :] = jnp.dot(
                    left, held[r, h * hd : (h + 1) * hd, :], preferred_element_type=F32
                )
        sent.append(send(held.at[r], r, 0, 1))
    gain = gain_ref[...]

    def emit(t, h, o):
        gate = at_step(g_s, t, requests, steps, h)
        scaled = o * lax.rsqrt(row_sum(o * o) * (1.0 / hd) + EPS)
        o_s[h, pl.ds(t, requests, stride=steps), :] = scaled * gain * jax.nn.silu(gate)

    for kh in range(key_heads):
        recurrence(kh, repeats, steps, requests, hd, k_s, q_s, v_s, a_s, b_s, m_s, emit, None)
    top = ids_ref.shape[-1]
    place = lax.broadcasted_iota(jnp.int32, (steps, w_s.shape[-1]), 1)
    for r in range(requests):
        rows = slice(r * steps, (r + 1) * steps)
        r_s[rows, :] = res_ref[r].astype(F32)
        prob = prob_ref[r]
        prob = prob / row_sum(prob)
        weight = jnp.zeros(place.shape, F32)
        ids = ids_ref[r]
        for j in range(top):
            high = prob[:, j : j + 1].astype(BF16).astype(F32)
            weight = jnp.where(place == ids[:, j : j + 1], high, weight)
            weight = jnp.where(place == ids[:, j : j + 1] + experts, prob[:, j : j + 1] - high, weight)
        w_s[rows, :] = weight
    width = heads * hd
    cols = res_ref.shape[-1] // lanes
    for p in range(lanes):
        for h in range(heads):
            out_ref[p, :, h * hd : (h + 1) * hd] = o_s[h].astype(BF16)
        out_ref[p, :, width : width + cols] = r_s[:, p * cols : (p + 1) * cols].astype(BF16)
        out_ref[p, :, width + cols :] = w_s[...].astype(BF16)
    for c in sent:
        c.wait()


def core_rows(
    home, lane, lanes, experts, states, query_rows, key_rows, value_rows, gate_rows, beta_logit, decay_logit,
    core_gain, residual, route_ids, route_prob,
):
    requests, heads, hd, _ = states.shape
    steps = key_rows.shape[1]
    kw, vw = key_rows.shape[-1], value_rows.shape[-1]
    tokens = requests * steps
    _, pay_rows = packed_rows(kw // hd, heads, steps)
    width = residual.shape[-1]
    weight_lanes = -(-2 * experts // 128) * 128
    vmem, hbm = pl.BlockSpec(memory_space=pltpu.VMEM), pl.BlockSpec(memory_space=pl.ANY)
    smem = pl.BlockSpec(memory_space=pltpu.SMEM)
    return pl.pallas_call(
        functools.partial(core_kernel, lanes, experts),
        in_specs=[smem, smem, hbm] + [vmem] * 10,
        out_specs=[vmem] + [hbm] * lanes,
        out_shape=[jax.ShapeDtypeStruct((lanes, tokens, vw + width // lanes + weight_lanes), BF16)]
        + [jax.ShapeDtypeStruct((requests // lanes, heads * hd + pay_rows, hd), BF16)] * lanes,
        scratch_shapes=[
            pltpu.VMEM((kw // hd, tokens, hd), F32),
            pltpu.VMEM((kw // hd, tokens, hd), F32),
            pltpu.VMEM((heads, tokens, hd), F32),
            pltpu.VMEM((heads, tokens, hd), F32),
            pltpu.VMEM((tokens, 128), F32),
            pltpu.VMEM((tokens, 128), F32),
            pltpu.VMEM((heads, 2 * tokens, hd), F32),
            pltpu.VMEM((heads, tokens, hd), F32),
            pltpu.VMEM((tokens, width), F32),
            pltpu.VMEM((tokens, weight_lanes), F32),
            pltpu.VMEM((requests, heads * hd, hd), BF16),
            pltpu.VMEM((pay_rows, hd), F32),
            pltpu.VMEM((requests, pay_rows, hd), BF16),
            pltpu.SemaphoreType.DMA((requests,)),
            pltpu.SemaphoreType.DMA((2, requests)),
        ],
        compiler_params=pltpu.CompilerParams(vmem_limit_bytes=60 * MIB),
        cost_estimate=pl.CostEstimate(flops=20_000_000, bytes_accessed=9 * MIB, transcendentals=100_000),
        name="core_rows",
    )(
        home, lane, states.reshape(requests, heads * hd, hd), query_rows, key_rows, value_rows, gate_rows,
        beta_logit, decay_logit, core_gain.reshape(1, hd), residual, route_ids, route_prob,
    )


def state_kernel(
    key_heads, heads, steps, count, place_ref, *rest
):
    arrived = rest[:count]
    out_ref, k_s, v_s, a_s, b_s, m_s, u_s, c_s, held, pay_s, ready, in_sem, pay_sem, out_sem = rest[-14:]
    requests, state_rows, hd = held.shape
    cap = requests // count
    repeats = heads // key_heads
    pays, copies = [], []
    for r in range(requests):
        pays.append(
            pltpu.make_async_copy(
                arrived[r // cap].at[r % cap, pl.ds(state_rows, pay_s.shape[1])], pay_s.at[r], pay_sem.at[r]
            )
        )
        pays[-1].start()
    for r in range(requests):
        copies.append(
            pltpu.make_async_copy(
                arrived[r // cap].at[r % cap, pl.ds(0, state_rows)], held.at[r], in_sem.at[r]
            )
        )
        copies[-1].start()
    for r in range(requests):
        pays[r].wait()
        rows = slice(r * steps, (r + 1) * steps)
        pay = pay_s[r].astype(F32)
        for kh in range(key_heads):
            k_s[kh, rows, :] = pay[kh * steps : (kh + 1) * steps]
        for h in range(heads):
            v_s[h, rows, :] = pay[(key_heads + h) * steps : (key_heads + h + 1) * steps]
        at = (key_heads + heads) * steps
        a_s[rows, :] = jax.nn.sigmoid(pay[at : at + steps])
        b_s[rows, :] = jax.nn.sigmoid(pay[at + steps : at + 2 * steps])
    for r in range(requests):
        copies[r].wait()
        rows = slice(r * steps, (r + 1) * steps)
        for h in range(heads):
            m_s[h, rows, :] = jnp.dot(
                k_s[h // repeats, rows, :].astype(BF16),
                held[r, h * hd : (h + 1) * hd, :],
                preferred_element_type=F32,
            )

    def emit(h, c, updates):
        c_s[h] = jnp.broadcast_to(c, (requests, hd))
        for t, u in enumerate(updates):
            u_s[h, pl.ds(t, requests, stride=steps), :] = u

    for kh in range(key_heads):
        recurrence(kh, repeats, steps, requests, hd, k_s, None, v_s, a_s, b_s, m_s, None, emit)
    sent = []
    for r in range(requests):
        slot = r % 2
        if r >= 2:
            sent[r - 2].wait()
        rows = slice(r * steps, (r + 1) * steps)
        for h in range(heads):
            k4 = k_s[h // repeats, rows, :]
            k8 = jnp.concatenate([k4, k4], axis=0).astype(BF16)
            u4 = u_s[h, rows, :]
            high = u4.astype(BF16).astype(F32)
            u8 = jnp.concatenate([high, u4 - high], axis=0).astype(BF16)
            added = lax.dot_general(
                k8, u8, (((0,), (0,)), ((), ())), preferred_element_type=F32
            )
            kept = held[r, h * hd : (h + 1) * hd, :].astype(F32) * c_s[h, r : r + 1, :]
            ready[slot, h * hd : (h + 1) * hd, :] = (kept + added).astype(BF16)
        sent.append(pltpu.make_async_copy(ready.at[slot], out_ref.at[place_ref[r]], out_sem.at[slot]))
        sent[-1].start()
    for c in sent[-2:]:
        c.wait()


def landed_states(arrived, before, total, key_heads, heads, steps):
    cap, all_rows, hd = arrived[0].shape
    place_row = heads * hd + (key_heads + heads + 2) * steps
    place = jnp.concatenate([a[:, place_row, 0] for a in arrived]).astype(jnp.int32)
    requests = cap * len(arrived)
    tokens = requests * steps
    state_rows = heads * hd
    hbm = pl.BlockSpec(memory_space=pl.ANY)
    out = pl.pallas_call(
        functools.partial(state_kernel, key_heads, heads, steps, len(arrived)),
        in_specs=[pl.BlockSpec(memory_space=pltpu.SMEM)] + [hbm] * (len(arrived) + len(before)),
        out_specs=hbm,
        out_shape=jax.ShapeDtypeStruct((total, state_rows, hd), BF16),
        input_output_aliases={len(arrived) + 1: 0} if before else {},
        scratch_shapes=[
            pltpu.VMEM((key_heads, tokens, hd), F32),
            pltpu.VMEM((heads, tokens, hd), F32),
            pltpu.VMEM((tokens, hd), F32),
            pltpu.VMEM((tokens, hd), F32),
            pltpu.VMEM((heads, tokens, hd), F32),
            pltpu.VMEM((heads, tokens, hd), F32),
            pltpu.VMEM((heads, requests, hd), F32),
            pltpu.VMEM((requests, state_rows, hd), BF16),
            pltpu.VMEM((requests, all_rows - state_rows, hd), BF16),
            pltpu.VMEM((2, state_rows, hd), BF16),
            pltpu.SemaphoreType.DMA((requests,)),
            pltpu.SemaphoreType.DMA((requests,)),
            pltpu.SemaphoreType.DMA((2,)),
        ],
        compiler_params=pltpu.CompilerParams(vmem_limit_bytes=32 * MIB),
        cost_estimate=pl.CostEstimate(flops=20_000_000, bytes_accessed=requests * MIB, transcendentals=10_000),
        name="landed_states",
    )(place, *arrived, *before)
    return out


def expert_kernel(sides, own_out, experts, where_ref, *rest):
    pieces = rest[: 2 * sides]
    gain_ref, up_ref, down_ref = rest[2 * sides : 2 * sides + 3]
    keeps = rest[2 * sides + 3 : 3 * sides + 3]
    give_ref = rest[3 * sides + 3]
    result_s = rest[-1]
    group_rows = pieces[0].shape[0]
    cols = gain_ref.shape[-1]
    spans = give_ref.shape[1]
    tokens = give_ref.shape[2]
    width = down_ref.shape[-1]
    hidden_units = down_ref.shape[1]
    e = where_ref[0]
    blocks = [(x, c) for x in range(spans) for c in range(2)]
    values = {}
    for x, c in blocks:
        parts = [pieces[2 * y + c][:, x * cols : (x + 1) * cols] for y in range(sides)]
        values[x, c] = jnp.concatenate(parts, axis=0).astype(F32)
    total = sum(row_sum(values[b] * values[b]) for b in blocks)
    scale = lax.rsqrt(total * (1.0 / width) + EPS)
    joined = None
    for x, c in blocks:
        block = e ^ (2 * x + c)
        normed = (values[x, c] * scale * gain_ref[pl.ds(block, 1), :]).astype(BF16)
        up = up_ref[0, pl.ds(pl.multiple_of(block * cols, cols), cols), :]
        term = jnp.dot(normed, up, preferred_element_type=F32)
        joined = term if joined is None else joined + term
        if own_out:
            rest[3 * sides + 4][:, pl.ds(pl.multiple_of(block * cols, cols), cols)] = pieces[c][
                pl.ds(pl.multiple_of(e * tokens, tokens), tokens), x * cols : (x + 1) * cols
            ]
    active = (jax.nn.silu(joined[:, :hidden_units]) * joined[:, hidden_units:]).astype(BF16)
    result = jnp.dot(active, down_ref[0], preferred_element_type=F32).astype(BF16)
    marks = [pieces[2 * y][:, spans * cols :].astype(F32) for y in range(sides)]
    marks = jnp.concatenate(marks, axis=0)
    place = lax.broadcasted_iota(jnp.int32, marks.shape, 1)
    mine = (place == where_ref[1]) | (place == where_ref[1] + experts)
    weight = row_sum(jnp.where(mine, marks, 0.0))
    result_s[...] = (result.astype(F32) * weight).astype(BF16)
    for y in range(sides):
        for x in range(spans):
            for c in range(2):
                start = y * group_rows + (e ^ (2 * x + c)) * tokens
                rows = result_s[pl.ds(pl.multiple_of(start, tokens), tokens), :]
                if c:
                    give_ref[y, x] = rows
                else:
                    keeps[y][x] = rows


def expert_chunk(where, pieces, gain, gate_up, down_weight, tokens, experts, own_out):
    sides = len(pieces) // 2
    spans, group_rows = gain.shape[0] // 2, pieces[0].shape[0]
    width = down_weight.shape[-1]
    vmem = pl.BlockSpec(memory_space=pltpu.VMEM)
    keep = jax.ShapeDtypeStruct((spans, tokens, width), BF16)
    give = jax.ShapeDtypeStruct((sides, spans, tokens, width), BF16)
    own = [jax.ShapeDtypeStruct((tokens, width), BF16)] if own_out else []
    rows = sides * group_rows
    outs = pl.pallas_call(
        functools.partial(expert_kernel, sides, own_out, experts),
        in_specs=[pl.BlockSpec(memory_space=pltpu.SMEM)] + [vmem] * (len(pieces) + 3),
        out_specs=[vmem] * (sides + 1 + len(own)),
        out_shape=[keep] * sides + [give] + own,
        scratch_shapes=[pltpu.VMEM((rows, width), BF16)],
        compiler_params=pltpu.CompilerParams(vmem_limit_bytes=32 * MIB),
        cost_estimate=pl.CostEstimate(
            flops=6 * rows * width * down_weight.shape[1], bytes_accessed=6 * MIB, transcendentals=0
        ),
        name="expert_chunk",
    )(where, *pieces, gain, gate_up, down_weight)
    return outs


def swap(x, axis, d):
    size = lax.axis_size(axis)
    return lax.ppermute(x, axis, [(i, i ^ d) for i in range(size)])


def summed(*terms):
    return functools.reduce(lambda p, q: p + q, [t.astype(F32) for t in terms])


def shards(
    states, query_rows, key_rows, value_rows, gate_rows, beta_logit, decay_logit, residual,
    route_ids, route_prob, out_weight, core_gain, moe_gain, gate_up, down_weight, new_home,
):
    requests, heads, hd, _ = states.shape
    steps = query_rows.shape[1]
    width = residual.shape[-1]
    tokens = requests * steps
    lanes = lax.axis_size("ep")
    groups = lax.axis_size("dp")
    my_lane = lax.axis_index("ep")
    my_group = lax.axis_index("dp")
    kw, vw = key_rows.shape[-1], value_rows.shape[-1]
    top = route_ids.shape[-1]

    experts = groups * lanes
    cols = out_weight.shape[1]
    me = my_group * lanes + my_lane

    with jax.named_scope("core"):
        sent, *packed = core_rows(
            new_home, my_lane.reshape(1), lanes, experts, states, query_rows, key_rows, value_rows,
            gate_rows, beta_logit, decay_logit, core_gain, residual, route_ids, route_prob,
        )
        got = lax.all_to_all(sent, "ep", split_axis=0, concat_axis=0, tiled=True)
        got = got.reshape(lanes * tokens, got.shape[-1])
    with jax.named_scope("attention"):
        attention = jnp.dot(got[:, :vw], out_weight, preferred_element_type=F32).astype(BF16)
        before = got[:, vw : vw + cols]
        hidden_cols = (before.astype(F32) + attention.astype(F32)).astype(BF16)
        others = [swap(hidden_cols, "ep", d) for d in range(2, lanes, 2)]
        held = jnp.concatenate([hidden_cols] + others + [got[:, vw + cols :]], axis=1)
        held, packed = lax.optimization_barrier((held, packed))

    with jax.named_scope("send_states"):
        arrived = [packed[0]]
        for d in range(1, lanes):
            if d > 2:
                packed, arrived[-1] = lax.optimization_barrier((packed, arrived[-1]))
            arrived.append(swap(packed[d], "ep", d))

    gain = moe_gain.reshape(lanes, cols)
    where = jnp.stack([my_lane, me])
    far = groups // 2
    chunks = [0] + [d for d in range(groups - 2, 0, -2) if d != far] + [far]
    sums, asides = {}, []
    own_rows = None
    with jax.named_scope("tokens"):
        near = {d: swap(held, "dp", d) if d else held for d in chunks}
    for d in chunks:
        with jax.named_scope("tokens"):
            across = swap(near[d], "dp", 1)
            pieces = [near[d], swap(near[d], "ep", 1), across, swap(across, "ep", 1)]
            if d == far:
                pieces, asides, arrived[2:3] = lax.optimization_barrier((pieces, asides, arrived[2:3]))
        with jax.named_scope("experts"):
            outs = expert_chunk(where, pieces, gain, gate_up, down_weight, tokens, experts, d == 0)
            keep_near, keep_across, give = outs[:3]
            if d == 0:
                own_rows = outs[3]
        with jax.named_scope("way_back"):
            taken = swap(give, "ep", 1)
            asides.append(summed(keep_across, taken[1]).astype(BF16))
            sums[d] = (keep_near, taken)
    with jax.named_scope("way_back"):
        for d, aside in zip(chunks, asides):
            keep_near, taken = sums[d]
            chunk = summed(keep_near, taken[0], swap(aside, "dp", 1))
            sums[d] = swap(chunk.astype(BF16), "dp", d) if d else chunk
        sums = [sums[d] for d in chunks]
    with jax.named_scope("landed"):
        sizes = (requests, kw // hd, heads, steps)
        moved_out = landed_states(arrived[:-1], [], *sizes)
        sums, moved_out = lax.optimization_barrier((sums, moved_out))
        moved_out = landed_states(arrived[-1:], [moved_out], *sizes)
        moved_out = moved_out.reshape(requests, heads, hd, hd)
    with jax.named_scope("mixed"):
        mixed = summed(own_rows, *[s[0] for s in sums])
        for x in range(1, lanes // 2):
            mixed = mixed + swap(summed(*[s[x] for s in sums]).astype(BF16), "ep", 2 * x).astype(F32)
        mixed_out = mixed.astype(BF16)
    return mixed_out.reshape(requests, steps, width), moved_out


def solution(mesh):
    row = P(("dp", "ep"), None, None)
    placed = (P(("dp", "ep"), None, None, None),) + (row,) * 9 + (
        P(None, "ep"), P(), P(), row, row, P(("dp", "ep")),
    )
    return jax.shard_map(
        shards,
        mesh=mesh,
        in_specs=placed,
        out_specs=(row, P(("dp", "ep"), None, None, None)),
        check_vma=False,
    )
```

```python
import functools

import jax
import jax.numpy as jnp
from jax import lax
from jax.experimental import pallas as pl
from jax.experimental.pallas import tpu as pltpu
from jax.sharding import PartitionSpec as P

EPS = 1e-06
F32 = jnp.float32
BF16 = jnp.bfloat16
MIB = 1 << 20


def row_sum(x):
    return jnp.sum(x, axis=-1, keepdims=True)


def spread_rows(ref, scratch, requests, steps):
    for r in range(requests):
        split_heads(ref[r].astype(F32), scratch, r, steps)


def split_heads(values, scratch, r, steps):
    hd = scratch.shape[-1]
    for h in range(scratch.shape[0]):
        scratch[h, r * steps : (r + 1) * steps, :] = values[:, h * hd : (h + 1) * hd]


def at_step(scratch, t, requests, steps, head=None):
    if head is None:
        return scratch[pl.ds(t, requests, stride=steps), :]
    return scratch[head, pl.ds(t, requests, stride=steps), :]


def recurrence(kh, repeats, steps, requests, hd, k_s, q_s, v_s, a_s, b_s, m_s, emit_out, emit_state):
    per = m_s.shape[1] // requests
    ks = [at_step(k_s, t, requests, steps, kh) for t in range(steps)]
    rk = [lax.rsqrt(row_sum(k * k) + EPS) for k in ks]
    kn = [k * r for k, r in zip(ks, rk)]
    kk = {(i, t): row_sum(kn[i] * kn[t]) for t in range(steps) for i in range(t)}
    if emit_out is not None:
        qs = [at_step(q_s, t, requests, steps, kh) for t in range(steps)]
        rq = [lax.rsqrt(row_sum(q * q) + EPS) * hd**-0.5 for q in qs]
        qn = [q * r for q, r in zip(qs, rq)]
        kq = {(i, t): row_sum(kn[i] * qn[t]) for t in range(steps) for i in range(t + 1)}
    for h in range(kh * repeats, (kh + 1) * repeats):
        decayed = []
        c = None
        for t in range(steps):
            a = at_step(a_s, t, requests, steps)[:, h : h + 1]
            b = at_step(b_s, t, requests, steps)[:, h : h + 1]
            decayed = [w * a for w in decayed]
            c = a if c is None else c * a
            m = (c * rk[t]) * at_step(m_s, t, requests, per, h)
            for i in range(t):
                m = m + kk[i, t] * decayed[i]
            decayed.append((at_step(v_s, t, requests, steps, h) - m) * b)
            if emit_out is not None:
                o = (c * rq[t]) * at_step(m_s, steps + t, requests, per, h)
                for i in range(t + 1):
                    o = o + kq[i, t] * decayed[i]
                emit_out(t, h, o)
        if emit_state is not None:
            emit_state(h, c, [w * r for w, r in zip(decayed, rk)])


def sigmoid_rows(ref, scratch, requests, steps):
    for r in range(requests):
        scratch[r * steps : (r + 1) * steps, : ref.shape[-1]] = jax.nn.sigmoid(ref[r].astype(F32))


def packed_rows(key_heads, heads, steps):
    used = (key_heads + heads + 3) * steps
    return used, -(-used // 16) * 16


def core_kernel(
    lanes, experts, home_ref, lane_ref, state_ref, q_ref, k_ref, v_ref, g_ref, b_ref, a_ref, gain_ref,
    res_ref, ids_ref, prob_ref, out_ref, *rest,
):
    packed = rest[:lanes]
    k_s, q_s, v_s, g_s, a_s, b_s, m_s, o_s, r_s, w_s, held, pay_f, pay_s, in_sem, out_sem = rest[lanes:]
    requests, steps, _ = k_ref.shape
    hd = held.shape[-1]
    heads, key_heads = v_s.shape[0], k_s.shape[0]
    repeats = heads // key_heads
    cap = requests // lanes
    copies = []
    for r in range(requests):
        copies.append(pltpu.make_async_copy(state_ref.at[r], held.at[r], in_sem.at[r]))
        copies[-1].start()
    spread_rows(k_ref, k_s, requests, steps)
    spread_rows(q_ref, q_s, requests, steps)
    spread_rows(v_ref, v_s, requests, steps)
    spread_rows(g_ref, g_s, requests, steps)
    sigmoid_rows(a_ref, a_s, requests, steps)
    sigmoid_rows(b_ref, b_s, requests, steps)
    target = [lax.rem(lax.div(home_ref[r], requests), lanes) ^ lane_ref[0] for r in range(requests)]
    ranks = [
        sum([(target[p] == target[r]).astype(jnp.int32) for p in range(r)], jnp.int32(0))
        for r in range(requests)
    ]
    state_rows = heads * hd

    def send(source, r, start, kind):
        rows = pl.ds(start, source.shape[0])
        for d in range(lanes):

            @pl.when(target[r] == d)
            def _():
                pltpu.make_async_copy(
                    source, packed[d].at[ranks[r], rows], out_sem.at[kind, r]
                ).start()

        return pltpu.make_async_copy(source, packed[0].at[0, rows], out_sem.at[kind, r])

    sent = []
    pay_f[...] = jnp.zeros_like(pay_f)
    for r in range(requests):
        rows = slice(r * steps, (r + 1) * steps)
        for kh in range(key_heads):
            pay_f[kh * steps : (kh + 1) * steps, :] = k_s[kh, rows, :]
        for h in range(heads):
            at = (key_heads + h) * steps
            pay_f[at : at + steps, :] = v_s[h, rows, :]
        at = (key_heads + heads) * steps
        pay_f[at : at + steps, :heads] = a_ref[r].astype(F32)
        pay_f[at + steps : at + 2 * steps, :heads] = b_ref[r].astype(F32)
        place = lax.rem(home_ref[r], requests).astype(F32)
        pay_f[at + 2 * steps : at + 3 * steps, :] = jnp.full((steps, hd), place, F32)
        pay_s[r] = pay_f[...].astype(BF16)
        sent.append(send(pay_s.at[r], r, state_rows, 0))
    for r in range(requests):
        copies[r].wait()
        rows = slice(r * steps, (r + 1) * steps)
        for kh in range(key_heads):
            left = jnp.concatenate([k_s[kh, rows, :], q_s[kh, rows, :]], axis=0).astype(BF16)
            for h in range(kh * repeats, (kh + 1) * repeats):
                m_s[h, r * 2 * steps : (r + 1) * 2 * steps, :] = jnp.dot(
                    left, held[r, h * hd : (h + 1) * hd, :], preferred_element_type=F32
                )
        sent.append(send(held.at[r], r, 0, 1))
    gain = gain_ref[...]

    def emit(t, h, o):
        gate = at_step(g_s, t, requests, steps, h)
        scaled = o * lax.rsqrt(row_sum(o * o) * (1.0 / hd) + EPS)
        o_s[h, pl.ds(t, requests, stride=steps), :] = scaled * gain * jax.nn.silu(gate)

    for kh in range(key_heads):
        recurrence(kh, repeats, steps, requests, hd, k_s, q_s, v_s, a_s, b_s, m_s, emit, None)
    top = ids_ref.shape[-1]
    place = lax.broadcasted_iota(jnp.int32, (steps, w_s.shape[-1]), 1)
    for r in range(requests):
        rows = slice(r * steps, (r + 1) * steps)
        r_s[rows, :] = res_ref[r].astype(F32)
        prob = prob_ref[r]
        prob = prob / row_sum(prob)
        weight = jnp.zeros(place.shape, F32)
        ids = ids_ref[r]
        for j in range(top):
            high = prob[:, j : j + 1].astype(BF16).astype(F32)
            weight = jnp.where(place == ids[:, j : j + 1], high, weight)
            weight = jnp.where(place == ids[:, j : j + 1] + experts, prob[:, j : j + 1] - high, weight)
        w_s[rows, :] = weight
    width = heads * hd
    cols = res_ref.shape[-1] // lanes
    for p in range(lanes):
        for h in range(heads):
            out_ref[p, :, h * hd : (h + 1) * hd] = o_s[h].astype(BF16)
        out_ref[p, :, width : width + cols] = r_s[:, p * cols : (p + 1) * cols].astype(BF16)
        out_ref[p, :, width + cols :] = w_s[...].astype(BF16)
    for c in sent:
        c.wait()


def core_rows(
    home, lane, lanes, experts, states, query_rows, key_rows, value_rows, gate_rows, beta_logit, decay_logit,
    core_gain, residual, route_ids, route_prob,
):
    requests, heads, hd, _ = states.shape
    steps = key_rows.shape[1]
    kw, vw = key_rows.shape[-1], value_rows.shape[-1]
    tokens = requests * steps
    _, pay_rows = packed_rows(kw // hd, heads, steps)
    width = residual.shape[-1]
    weight_lanes = -(-2 * experts // 128) * 128
    vmem, hbm = pl.BlockSpec(memory_space=pltpu.VMEM), pl.BlockSpec(memory_space=pl.ANY)
    smem = pl.BlockSpec(memory_space=pltpu.SMEM)
    return pl.pallas_call(
        functools.partial(core_kernel, lanes, experts),
        in_specs=[smem, smem, hbm] + [vmem] * 10,
        out_specs=[vmem] + [hbm] * lanes,
        out_shape=[jax.ShapeDtypeStruct((lanes, tokens, vw + width // lanes + weight_lanes), BF16)]
        + [jax.ShapeDtypeStruct((requests // lanes, heads * hd + pay_rows, hd), BF16)] * lanes,
        scratch_shapes=[
            pltpu.VMEM((kw // hd, tokens, hd), F32),
            pltpu.VMEM((kw // hd, tokens, hd), F32),
            pltpu.VMEM((heads, tokens, hd), F32),
            pltpu.VMEM((heads, tokens, hd), F32),
            pltpu.VMEM((tokens, 128), F32),
            pltpu.VMEM((tokens, 128), F32),
            pltpu.VMEM((heads, 2 * tokens, hd), F32),
            pltpu.VMEM((heads, tokens, hd), F32),
            pltpu.VMEM((tokens, width), F32),
            pltpu.VMEM((tokens, weight_lanes), F32),
            pltpu.VMEM((requests, heads * hd, hd), BF16),
            pltpu.VMEM((pay_rows, hd), F32),
            pltpu.VMEM((requests, pay_rows, hd), BF16),
            pltpu.SemaphoreType.DMA((requests,)),
            pltpu.SemaphoreType.DMA((2, requests)),
        ],
        compiler_params=pltpu.CompilerParams(vmem_limit_bytes=60 * MIB),
        cost_estimate=pl.CostEstimate(flops=20_000_000, bytes_accessed=9 * MIB, transcendentals=100_000),
        name="core_rows",
    )(
        home, lane, states.reshape(requests, heads * hd, hd), query_rows, key_rows, value_rows, gate_rows,
        beta_logit, decay_logit, core_gain.reshape(1, hd), residual, route_ids, route_prob,
    )


def state_kernel(
    key_heads, heads, steps, count, place_ref, *rest
):
    arrived = rest[:count]
    out_ref, k_s, v_s, a_s, b_s, m_s, u_s, c_s, held, pay_s, ready, in_sem, pay_sem, out_sem = rest[-14:]
    requests, state_rows, hd = held.shape
    cap = requests // count
    repeats = heads // key_heads
    pays, copies = [], []
    for r in range(requests):
        pays.append(
            pltpu.make_async_copy(
                arrived[r // cap].at[r % cap, pl.ds(state_rows, pay_s.shape[1])], pay_s.at[r], pay_sem.at[r]
            )
        )
        pays[-1].start()
    for r in range(requests):
        copies.append(
            pltpu.make_async_copy(
                arrived[r // cap].at[r % cap, pl.ds(0, state_rows)], held.at[r], in_sem.at[r]
            )
        )
        copies[-1].start()
    for r in range(requests):
        pays[r].wait()
        rows = slice(r * steps, (r + 1) * steps)
        pay = pay_s[r].astype(F32)
        for kh in range(key_heads):
            k_s[kh, rows, :] = pay[kh * steps : (kh + 1) * steps]
        for h in range(heads):
            v_s[h, rows, :] = pay[(key_heads + h) * steps : (key_heads + h + 1) * steps]
        at = (key_heads + heads) * steps
        a_s[rows, :] = jax.nn.sigmoid(pay[at : at + steps])
        b_s[rows, :] = jax.nn.sigmoid(pay[at + steps : at + 2 * steps])
    for r in range(requests):
        copies[r].wait()
        rows = slice(r * steps, (r + 1) * steps)
        for h in range(heads):
            m_s[h, rows, :] = jnp.dot(
                k_s[h // repeats, rows, :].astype(BF16),
                held[r, h * hd : (h + 1) * hd, :],
                preferred_element_type=F32,
            )

    def emit(h, c, updates):
        c_s[h] = jnp.broadcast_to(c, (requests, hd))
        for t, u in enumerate(updates):
            u_s[h, pl.ds(t, requests, stride=steps), :] = u

    for kh in range(key_heads):
        recurrence(kh, repeats, steps, requests, hd, k_s, None, v_s, a_s, b_s, m_s, None, emit)
    sent = []
    for r in range(requests):
        slot = r % 2
        if r >= 2:
            sent[r - 2].wait()
        rows = slice(r * steps, (r + 1) * steps)
        for h in range(heads):
            k4 = k_s[h // repeats, rows, :]
            k8 = jnp.concatenate([k4, k4], axis=0).astype(BF16)
            u4 = u_s[h, rows, :]
            high = u4.astype(BF16).astype(F32)
            u8 = jnp.concatenate([high, u4 - high], axis=0).astype(BF16)
            added = lax.dot_general(
                k8, u8, (((0,), (0,)), ((), ())), preferred_element_type=F32
            )
            kept = held[r, h * hd : (h + 1) * hd, :].astype(F32) * c_s[h, r : r + 1, :]
            ready[slot, h * hd : (h + 1) * hd, :] = (kept + added).astype(BF16)
        sent.append(pltpu.make_async_copy(ready.at[slot], out_ref.at[place_ref[r]], out_sem.at[slot]))
        sent[-1].start()
    for c in sent[-2:]:
        c.wait()


def landed_states(arrived, before, total, key_heads, heads, steps):
    cap, all_rows, hd = arrived[0].shape
    place_row = heads * hd + (key_heads + heads + 2) * steps
    place = jnp.concatenate([a[:, place_row, 0] for a in arrived]).astype(jnp.int32)
    requests = cap * len(arrived)
    tokens = requests * steps
    state_rows = heads * hd
    hbm = pl.BlockSpec(memory_space=pl.ANY)
    out = pl.pallas_call(
        functools.partial(state_kernel, key_heads, heads, steps, len(arrived)),
        in_specs=[pl.BlockSpec(memory_space=pltpu.SMEM)] + [hbm] * (len(arrived) + len(before)),
        out_specs=hbm,
        out_shape=jax.ShapeDtypeStruct((total, state_rows, hd), BF16),
        input_output_aliases={len(arrived) + 1: 0} if before else {},
        scratch_shapes=[
            pltpu.VMEM((key_heads, tokens, hd), F32),
            pltpu.VMEM((heads, tokens, hd), F32),
            pltpu.VMEM((tokens, hd), F32),
            pltpu.VMEM((tokens, hd), F32),
            pltpu.VMEM((heads, tokens, hd), F32),
            pltpu.VMEM((heads, tokens, hd), F32),
            pltpu.VMEM((heads, requests, hd), F32),
            pltpu.VMEM((requests, state_rows, hd), BF16),
            pltpu.VMEM((requests, all_rows - state_rows, hd), BF16),
            pltpu.VMEM((2, state_rows, hd), BF16),
            pltpu.SemaphoreType.DMA((requests,)),
            pltpu.SemaphoreType.DMA((requests,)),
            pltpu.SemaphoreType.DMA((2,)),
        ],
        compiler_params=pltpu.CompilerParams(vmem_limit_bytes=32 * MIB),
        cost_estimate=pl.CostEstimate(flops=20_000_000, bytes_accessed=requests * MIB, transcendentals=10_000),
        name="landed_states",
    )(place, *arrived, *before)
    return out


def expert_kernel(sides, own_out, experts, where_ref, *rest):
    sources = rest[: 2 * sides]
    gain_ref, up_ref, down_ref = rest[2 * sides : 2 * sides + 3]
    keeps = rest[2 * sides + 3 : 3 * sides + 3]
    give_ref = rest[3 * sides + 3]
    pieces, result_s, sems = rest[-3 - 2 * sides + 1 : -2], rest[-2], rest[-1]
    copies = [pltpu.make_async_copy(a, b, sems.at[i]) for i, (a, b) in enumerate(zip(sources, pieces))]
    for c in copies:
        c.start()
    for c in copies:
        c.wait()
    group_rows = pieces[0].shape[0]
    cols = gain_ref.shape[-1]
    spans = give_ref.shape[1]
    tokens = give_ref.shape[2]
    width = down_ref.shape[-1]
    hidden_units = down_ref.shape[1]
    e = where_ref[0]
    blocks = [(x, c) for x in range(spans) for c in range(2)]
    values = {}
    for x, c in blocks:
        parts = [pieces[2 * y + c][:, x * cols : (x + 1) * cols] for y in range(sides)]
        values[x, c] = jnp.concatenate(parts, axis=0).astype(F32)
    total = sum(row_sum(values[b] * values[b]) for b in blocks)
    scale = lax.rsqrt(total * (1.0 / width) + EPS)
    joined = None
    for x, c in blocks:
        block = e ^ (2 * x + c)
        normed = (values[x, c] * scale * gain_ref[pl.ds(block, 1), :]).astype(BF16)
        up = up_ref[0, pl.ds(pl.multiple_of(block * cols, cols), cols), :]
        term = jnp.dot(normed, up, preferred_element_type=F32)
        joined = term if joined is None else joined + term
        if own_out:
            rest[3 * sides + 4][:, pl.ds(pl.multiple_of(block * cols, cols), cols)] = pieces[c][
                pl.ds(pl.multiple_of(e * tokens, tokens), tokens), x * cols : (x + 1) * cols
            ]
    active = (jax.nn.silu(joined[:, :hidden_units]) * joined[:, hidden_units:]).astype(BF16)
    result = jnp.dot(active, down_ref[0], preferred_element_type=F32).astype(BF16)
    marks = [pieces[2 * y][:, spans * cols :].astype(F32) for y in range(sides)]
    marks = jnp.concatenate(marks, axis=0)
    place = lax.broadcasted_iota(jnp.int32, marks.shape, 1)
    mine = (place == where_ref[1]) | (place == where_ref[1] + experts)
    weight = row_sum(jnp.where(mine, marks, 0.0))
    result_s[...] = (result.astype(F32) * weight).astype(BF16)
    for y in range(sides):
        for x in range(spans):
            for c in range(2):
                start = y * group_rows + (e ^ (2 * x + c)) * tokens
                rows = result_s[pl.ds(pl.multiple_of(start, tokens), tokens), :]
                if c:
                    give_ref[y, x] = rows
                else:
                    keeps[y][x] = rows


def expert_chunk(where, pieces, gain, gate_up, down_weight, tokens, experts, own_out):
    sides = len(pieces) // 2
    spans, group_rows = gain.shape[0] // 2, pieces[0].shape[0]
    width = down_weight.shape[-1]
    vmem = pl.BlockSpec(memory_space=pltpu.VMEM)
    hbm = pl.BlockSpec(memory_space=pltpu.HBM)
    keep = jax.ShapeDtypeStruct((spans, tokens, width), BF16)
    give = jax.ShapeDtypeStruct((sides, spans, tokens, width), BF16)
    own = [jax.ShapeDtypeStruct((tokens, width), BF16)] if own_out else []
    rows = sides * group_rows
    outs = pl.pallas_call(
        functools.partial(expert_kernel, sides, own_out, experts),
        in_specs=[pl.BlockSpec(memory_space=pltpu.SMEM)] + [hbm] * len(pieces) + [vmem] * 3,
        out_specs=[vmem] * (sides + 1 + len(own)),
        out_shape=[keep] * sides + [give] + own,
        scratch_shapes=[pltpu.VMEM(p.shape, BF16) for p in pieces]
        + [pltpu.VMEM((rows, width), BF16), pltpu.SemaphoreType.DMA((len(pieces),))],
        compiler_params=pltpu.CompilerParams(vmem_limit_bytes=32 * MIB),
        cost_estimate=pl.CostEstimate(
            flops=6 * rows * width * down_weight.shape[1], bytes_accessed=6 * MIB, transcendentals=0
        ),
        name="expert_chunk",
    )(where, *pieces, gain, gate_up, down_weight)
    return outs


def swap(x, axis, d):
    size = lax.axis_size(axis)
    return lax.ppermute(x, axis, [(i, i ^ d) for i in range(size)])


def summed(*terms):
    return functools.reduce(lambda p, q: p + q, [t.astype(F32) for t in terms])


def shards(
    states, query_rows, key_rows, value_rows, gate_rows, beta_logit, decay_logit, residual,
    route_ids, route_prob, out_weight, core_gain, moe_gain, gate_up, down_weight, new_home,
):
    requests, heads, hd, _ = states.shape
    steps = query_rows.shape[1]
    width = residual.shape[-1]
    tokens = requests * steps
    lanes = lax.axis_size("ep")
    groups = lax.axis_size("dp")
    my_lane = lax.axis_index("ep")
    my_group = lax.axis_index("dp")
    kw, vw = key_rows.shape[-1], value_rows.shape[-1]
    top = route_ids.shape[-1]

    experts = groups * lanes
    cols = out_weight.shape[1]
    me = my_group * lanes + my_lane

    with jax.named_scope("core"):
        sent, *packed = core_rows(
            new_home, my_lane.reshape(1), lanes, experts, states, query_rows, key_rows, value_rows,
            gate_rows, beta_logit, decay_logit, core_gain, residual, route_ids, route_prob,
        )
        got = lax.all_to_all(sent, "ep", split_axis=0, concat_axis=0, tiled=True)
        got = got.reshape(lanes * tokens, got.shape[-1])
    with jax.named_scope("attention"):
        attention = jnp.dot(got[:, :vw], out_weight, preferred_element_type=F32).astype(BF16)
        before = got[:, vw : vw + cols]
        hidden_cols = (before.astype(F32) + attention.astype(F32)).astype(BF16)
        others = [swap(hidden_cols, "ep", d) for d in range(2, lanes, 2)]
        held = jnp.concatenate([hidden_cols] + others + [got[:, vw + cols :]], axis=1)
        held, packed = lax.optimization_barrier((held, packed))

    with jax.named_scope("send_states"):
        arrived = [packed[0]]
        for d in range(1, lanes):
            if d > 2:
                packed, arrived[-1] = lax.optimization_barrier((packed, arrived[-1]))
            arrived.append(swap(packed[d], "ep", d))

    gain = moe_gain.reshape(lanes, cols)
    where = jnp.stack([my_lane, me])
    far = groups // 2
    chunks = [0] + [d for d in range(groups - 2, 0, -2) if d != far] + [far]
    sums, asides = {}, []
    own_rows = None
    with jax.named_scope("tokens"):
        near = {d: swap(held, "dp", d) if d else held for d in chunks[:-1]}
        across = {d: swap(near[d], "dp", 1) for d in chunks[:-1]}
        later, near[chunks[1]] = lax.optimization_barrier((held, near[chunks[1]]))
        near[far] = swap(later, "dp", far)
    for d in chunks:
        with jax.named_scope("tokens"):
            if d == far:
                near[d], asides[0], across[chunks[1]] = lax.optimization_barrier(
                    (near[d], asides[0], across[chunks[1]])
                )
                across[d] = swap(near[d], "dp", 1)
            pieces = [near[d], swap(near[d], "ep", 1), across[d], swap(across[d], "ep", 1)]
            if d == far:
                pieces, asides, arrived[2:3] = lax.optimization_barrier((pieces, asides, arrived[2:3]))
        with jax.named_scope("experts"):
            outs = expert_chunk(where, pieces, gain, gate_up, down_weight, tokens, experts, d == 0)
            keep_near, keep_across, give = outs[:3]
            if d == 0:
                own_rows = outs[3]
        with jax.named_scope("way_back"):
            taken = swap(give, "ep", 1)
            asides.append(summed(keep_across, taken[1]).astype(BF16))
            sums[d] = (keep_near, taken)
    with jax.named_scope("way_back"):
        for d, aside in zip(chunks, asides):
            keep_near, taken = sums[d]
            chunk = summed(keep_near, taken[0], swap(aside, "dp", 1))
            sums[d] = chunk.astype(BF16) if d else chunk
        sums, arrived[:-1] = lax.optimization_barrier((sums, arrived[:-1]))
        sums = [swap(sums[d], "dp", d) if d else sums[d] for d in chunks]
    with jax.named_scope("landed"):
        sizes = (requests, kw // hd, heads, steps)
        moved_out = landed_states(arrived[:-1], [], *sizes)
        sums, moved_out = lax.optimization_barrier((sums, moved_out))
        moved_out = landed_states(arrived[-1:], [moved_out], *sizes)
        moved_out = moved_out.reshape(requests, heads, hd, hd)
    with jax.named_scope("mixed"):
        mixed = summed(own_rows, *[s[0] for s in sums])
        for x in range(1, lanes // 2):
            mixed = mixed + swap(summed(*[s[x] for s in sums]).astype(BF16), "ep", 2 * x).astype(F32)
        mixed_out = mixed.astype(BF16)
    return mixed_out.reshape(requests, steps, width), moved_out


def solution(mesh):
    row = P(("dp", "ep"), None, None)
    placed = (P(("dp", "ep"), None, None, None),) + (row,) * 9 + (
        P(None, "ep"), P(), P(), row, row, P(("dp", "ep")),
    )
    return jax.shard_map(
        shards,
        mesh=mesh,
        in_specs=placed,
        out_specs=(row, P(("dp", "ep"), None, None, None)),
        check_vma=False,
    )
```

```python
import functools

import jax
import jax.numpy as jnp
from jax import lax
from jax.experimental import pallas as pl
from jax.experimental.pallas import tpu as pltpu
from jax.sharding import PartitionSpec as P

EPS = 1e-06
F32 = jnp.float32
BF16 = jnp.bfloat16
MIB = 1 << 20


def row_sum(x):
    return jnp.sum(x, axis=-1, keepdims=True)


def spread_rows(ref, scratch, requests, steps):
    for r in range(requests):
        split_heads(ref[r].astype(F32), scratch, r, steps)


def split_heads(values, scratch, r, steps):
    hd = scratch.shape[-1]
    for h in range(scratch.shape[0]):
        scratch[h, r * steps : (r + 1) * steps, :] = values[:, h * hd : (h + 1) * hd]


def at_step(scratch, t, requests, steps, head=None):
    if head is None:
        return scratch[pl.ds(t, requests, stride=steps), :]
    return scratch[head, pl.ds(t, requests, stride=steps), :]


def recurrence(kh, repeats, steps, requests, hd, k_s, q_s, v_s, a_s, b_s, m_s, emit_out, emit_state):
    per = m_s.shape[1] // requests
    ks = [at_step(k_s, t, requests, steps, kh) for t in range(steps)]
    rk = [lax.rsqrt(row_sum(k * k) + EPS) for k in ks]
    kn = [k * r for k, r in zip(ks, rk)]
    kk = {(i, t): row_sum(kn[i] * kn[t]) for t in range(steps) for i in range(t)}
    if emit_out is not None:
        qs = [at_step(q_s, t, requests, steps, kh) for t in range(steps)]
        rq = [lax.rsqrt(row_sum(q * q) + EPS) * hd**-0.5 for q in qs]
        qn = [q * r for q, r in zip(qs, rq)]
        kq = {(i, t): row_sum(kn[i] * qn[t]) for t in range(steps) for i in range(t + 1)}
    for h in range(kh * repeats, (kh + 1) * repeats):
        decayed = []
        c = None
        for t in range(steps):
            a = at_step(a_s, t, requests, steps)[:, h : h + 1]
            b = at_step(b_s, t, requests, steps)[:, h : h + 1]
            decayed = [w * a for w in decayed]
            c = a if c is None else c * a
            m = (c * rk[t]) * at_step(m_s, t, requests, per, h)
            for i in range(t):
                m = m + kk[i, t] * decayed[i]
            decayed.append((at_step(v_s, t, requests, steps, h) - m) * b)
            if emit_out is not None:
                o = (c * rq[t]) * at_step(m_s, steps + t, requests, per, h)
                for i in range(t + 1):
                    o = o + kq[i, t] * decayed[i]
                emit_out(t, h, o)
        if emit_state is not None:
            emit_state(h, c, [w * r for w, r in zip(decayed, rk)])


def sigmoid_rows(ref, scratch, requests, steps):
    for r in range(requests):
        scratch[r * steps : (r + 1) * steps, : ref.shape[-1]] = jax.nn.sigmoid(ref[r].astype(F32))


def packed_rows(key_heads, heads, steps):
    used = (key_heads + heads + 3) * steps
    return used, -(-used // 16) * 16


def core_kernel(
    lanes, experts, lane_ref, state_ref, q_ref, k_ref, v_ref, g_ref, b_ref, a_ref, gain_ref,
    res_ref, ids_ref, prob_ref, *rest,
):
    outs = rest[:lanes]
    k_s, q_s, v_s, g_s, a_s, b_s, m_s, o_s, r_s, w_s, held, in_sem = rest[lanes:]
    requests, steps, _ = k_ref.shape
    hd = held.shape[-1]
    heads, key_heads = v_s.shape[0], k_s.shape[0]
    repeats = heads // key_heads
    copies = []
    for r in range(requests):
        copies.append(pltpu.make_async_copy(state_ref.at[r], held.at[r], in_sem.at[r]))
        copies[-1].start()
    spread_rows(k_ref, k_s, requests, steps)
    spread_rows(q_ref, q_s, requests, steps)
    spread_rows(v_ref, v_s, requests, steps)
    spread_rows(g_ref, g_s, requests, steps)
    sigmoid_rows(a_ref, a_s, requests, steps)
    sigmoid_rows(b_ref, b_s, requests, steps)
    top = ids_ref.shape[-1]
    place = lax.broadcasted_iota(jnp.int32, (steps, w_s.shape[-1]), 1)
    for r in range(requests):
        rows = slice(r * steps, (r + 1) * steps)
        r_s[rows, :] = res_ref[r].astype(F32)
        prob = prob_ref[r]
        prob = prob / row_sum(prob)
        weight = jnp.zeros(place.shape, F32)
        ids = ids_ref[r]
        for j in range(top):
            high = prob[:, j : j + 1].astype(BF16).astype(F32)
            weight = jnp.where(place == ids[:, j : j + 1], high, weight)
            weight = jnp.where(place == ids[:, j : j + 1] + experts, prob[:, j : j + 1] - high, weight)
        w_s[rows, :] = weight
    for r in range(requests):
        copies[r].wait()
        rows = slice(r * steps, (r + 1) * steps)
        for kh in range(key_heads):
            left = jnp.concatenate([k_s[kh, rows, :], q_s[kh, rows, :]], axis=0).astype(BF16)
            for h in range(kh * repeats, (kh + 1) * repeats):
                m_s[h, r * 2 * steps : (r + 1) * 2 * steps, :] = jnp.dot(
                    left, held[r, h * hd : (h + 1) * hd, :], preferred_element_type=F32
                )
    gain = gain_ref[...]

    def emit(t, h, o):
        gate = at_step(g_s, t, requests, steps, h)
        scaled = o * lax.rsqrt(row_sum(o * o) * (1.0 / hd) + EPS)
        o_s[h, pl.ds(t, requests, stride=steps), :] = scaled * gain * jax.nn.silu(gate)

    for kh in range(key_heads):
        recurrence(kh, repeats, steps, requests, hd, k_s, q_s, v_s, a_s, b_s, m_s, emit, None)
    width = heads * hd
    cols = res_ref.shape[-1] // lanes
    for h in range(heads):
        part = o_s[h].astype(BF16)
        for j in range(lanes):
            outs[j][:, h * hd : (h + 1) * hd] = part
    marks = w_s[...].astype(BF16)
    for j in range(lanes):
        start = pl.multiple_of((lane_ref[0] ^ j) * cols, cols)
        outs[j][:, width : width + cols] = r_s[:, pl.ds(start, cols)].astype(BF16)
        outs[j][:, width + cols :] = marks


def core_rows(
    lane, lanes, experts, states, query_rows, key_rows, value_rows, gate_rows, beta_logit, decay_logit,
    core_gain, residual, route_ids, route_prob,
):
    requests, heads, hd, _ = states.shape
    steps = key_rows.shape[1]
    kw, vw = key_rows.shape[-1], value_rows.shape[-1]
    tokens = requests * steps
    width = residual.shape[-1]
    weight_lanes = -(-2 * experts // 128) * 128
    vmem, hbm = pl.BlockSpec(memory_space=pltpu.VMEM), pl.BlockSpec(memory_space=pl.ANY)
    return pl.pallas_call(
        functools.partial(core_kernel, lanes, experts),
        in_specs=[pl.BlockSpec(memory_space=pltpu.SMEM), hbm] + [vmem] * 10,
        out_specs=[vmem] * lanes,
        out_shape=[jax.ShapeDtypeStruct((tokens, vw + width // lanes + weight_lanes), BF16)] * lanes,
        scratch_shapes=[
            pltpu.VMEM((kw // hd, tokens, hd), F32),
            pltpu.VMEM((kw // hd, tokens, hd), F32),
            pltpu.VMEM((heads, tokens, hd), F32),
            pltpu.VMEM((heads, tokens, hd), F32),
            pltpu.VMEM((tokens, 128), F32),
            pltpu.VMEM((tokens, 128), F32),
            pltpu.VMEM((heads, 2 * tokens, hd), F32),
            pltpu.VMEM((heads, tokens, hd), F32),
            pltpu.VMEM((tokens, width), F32),
            pltpu.VMEM((tokens, weight_lanes), F32),
            pltpu.VMEM((requests, heads * hd, hd), BF16),
            pltpu.SemaphoreType.DMA((requests,)),
        ],
        compiler_params=pltpu.CompilerParams(vmem_limit_bytes=60 * MIB),
        cost_estimate=pl.CostEstimate(flops=20_000_000, bytes_accessed=9 * MIB, transcendentals=100_000),
        name="core_rows",
    )(
        lane, states.reshape(requests, heads * hd, hd), query_rows, key_rows, value_rows, gate_rows,
        beta_logit, decay_logit, core_gain.reshape(1, hd), residual, route_ids, route_prob,
    )


def pack_kernel(lanes, key_heads, home_ref, lane_ref, state_ref, k_ref, v_ref, b_ref, a_ref, *rest):
    outs = rest[:-4]
    held, pay_f, in_sem, out_sem = rest[-4:]
    requests, steps, _ = k_ref.shape
    hd = held.shape[-1]
    heads = v_ref.shape[-1] // hd
    state_rows = heads * hd
    cap = requests // lanes
    copies = []
    for r in range(requests):
        source = state_ref.at[r]
        copies.append(pltpu.make_async_copy(source, held.at[r, pl.ds(0, state_rows)], in_sem.at[r]))
        copies[-1].start()
    target = [lax.rem(lax.div(home_ref[r], requests), lanes) ^ lane_ref[0] for r in range(requests)]
    ranks = [
        sum([(target[p] == target[r]).astype(jnp.int32) for p in range(r)], jnp.int32(0))
        for r in range(requests)
    ]
    pay_f[...] = jnp.zeros_like(pay_f)
    for r in range(requests):
        keys, vals = k_ref[r].astype(F32), v_ref[r].astype(F32)
        for kh in range(key_heads):
            pay_f[kh * steps : (kh + 1) * steps, :] = keys[:, kh * hd : (kh + 1) * hd]
        for h in range(heads):
            at = (key_heads + h) * steps
            pay_f[at : at + steps, :] = vals[:, h * hd : (h + 1) * hd]
        at = (key_heads + heads) * steps
        pay_f[at : at + steps, :heads] = a_ref[r].astype(F32)
        pay_f[at + steps : at + 2 * steps, :heads] = b_ref[r].astype(F32)
        place = lax.rem(home_ref[r], requests).astype(F32)
        pay_f[at + 2 * steps : at + 3 * steps, :] = jnp.full((steps, hd), place, F32)
        held[r, state_rows:, :] = pay_f[...].astype(BF16)
    for r in range(requests):
        copies[r].wait()
        for d in range(lanes):
            for q in range(cap if d > 1 else 1):
                dest = outs[d].at[ranks[r]] if d < 2 else outs[2 + (d - 2) * cap + q].at[0]
                chosen = (target[r] == d) & (ranks[r] == q) if d > 1 else target[r] == d

                @pl.when(chosen)
                def _():
                    pltpu.make_async_copy(held.at[r], dest, out_sem.at[r]).start()

    for r in range(requests):
        pltpu.make_async_copy(held.at[r], outs[0].at[0], out_sem.at[r]).wait()


def pack_states(home, lane, lanes, states, key_rows, value_rows, beta_logit, decay_logit):
    requests, heads, hd, _ = states.shape
    steps = key_rows.shape[1]
    key_heads = key_rows.shape[-1] // hd
    cap = requests // lanes
    _, pay_rows = packed_rows(key_heads, heads, steps)
    all_rows = heads * hd + pay_rows
    vmem, hbm = pl.BlockSpec(memory_space=pltpu.VMEM), pl.BlockSpec(memory_space=pl.ANY)
    smem = pl.BlockSpec(memory_space=pltpu.SMEM)
    sizes = [cap] * 2 + [1] * (cap * (lanes - 2))
    return pl.pallas_call(
        functools.partial(pack_kernel, lanes, key_heads),
        in_specs=[smem, smem, hbm] + [vmem] * 4,
        out_specs=[hbm] * len(sizes),
        out_shape=[jax.ShapeDtypeStruct((n, all_rows, hd), BF16) for n in sizes],
        scratch_shapes=[
            pltpu.VMEM((requests, all_rows, hd), BF16),
            pltpu.VMEM((pay_rows, hd), F32),
            pltpu.SemaphoreType.DMA((requests,)),
            pltpu.SemaphoreType.DMA((requests,)),
        ],
        compiler_params=pltpu.CompilerParams(vmem_limit_bytes=48 * MIB),
        cost_estimate=pl.CostEstimate(flops=0, bytes_accessed=9 * MIB, transcendentals=0),
        name="pack_states",
    )(home, lane, states.reshape(requests, heads * hd, hd), key_rows, value_rows, beta_logit, decay_logit)


def project_kernel(*refs):
    lanes = len(refs) - 3
    weight_ref, out_ref, marks_ref = refs[lanes:]
    depth, cols = weight_ref.shape
    rows = jnp.concatenate([refs[j][...] for j in range(lanes)], axis=0)
    attention = jnp.dot(rows[:, :depth], weight_ref[...], preferred_element_type=F32).astype(BF16)
    before = rows[:, depth : depth + cols].astype(F32)
    out_ref[...] = (before + attention.astype(F32)).astype(BF16)
    marks_ref[...] = rows[:, depth + cols :]


def project(got, out_weight):
    tokens, wide = got[0].shape
    depth, cols = out_weight.shape
    rows = tokens * len(got)
    vmem = pl.BlockSpec(memory_space=pltpu.VMEM)
    return pl.pallas_call(
        project_kernel,
        in_specs=[vmem] * (len(got) + 1),
        out_specs=[vmem] * 2,
        out_shape=[
            jax.ShapeDtypeStruct((rows, cols), BF16),
            jax.ShapeDtypeStruct((rows, wide - depth - cols), BF16),
        ],
        compiler_params=pltpu.CompilerParams(vmem_limit_bytes=24 * MIB),
        cost_estimate=pl.CostEstimate(
            flops=2 * rows * depth * cols, bytes_accessed=3 * MIB, transcendentals=0
        ),
        name="project",
    )(*got, out_weight)


def state_kernel(
    key_heads, heads, steps, count, place_ref, *rest
):
    arrived = rest[:count]
    out_ref, k_s, v_s, a_s, b_s, m_s, u_s, c_s, held, pay_s, ready, in_sem, pay_sem, out_sem = rest[-14:]
    requests, state_rows, hd = held.shape
    origin = [(a, j) for a in arrived for j in range(a.shape[0])]
    repeats = heads // key_heads
    pays, copies = [], []
    for r in range(requests):
        pays.append(
            pltpu.make_async_copy(
                origin[r][0].at[origin[r][1], pl.ds(state_rows, pay_s.shape[1])], pay_s.at[r], pay_sem.at[r]
            )
        )
        pays[-1].start()
    for r in range(requests):
        copies.append(
            pltpu.make_async_copy(
                origin[r][0].at[origin[r][1], pl.ds(0, state_rows)], held.at[r], in_sem.at[r]
            )
        )
        copies[-1].start()
    for r in range(requests):
        pays[r].wait()
        rows = slice(r * steps, (r + 1) * steps)
        pay = pay_s[r].astype(F32)
        for kh in range(key_heads):
            k_s[kh, rows, :] = pay[kh * steps : (kh + 1) * steps]
        for h in range(heads):
            v_s[h, rows, :] = pay[(key_heads + h) * steps : (key_heads + h + 1) * steps]
        at = (key_heads + heads) * steps
        a_s[rows, :] = jax.nn.sigmoid(pay[at : at + steps])
        b_s[rows, :] = jax.nn.sigmoid(pay[at + steps : at + 2 * steps])
    for r in range(requests):
        copies[r].wait()
        rows = slice(r * steps, (r + 1) * steps)
        for h in range(heads):
            m_s[h, rows, :] = jnp.dot(
                k_s[h // repeats, rows, :].astype(BF16),
                held[r, h * hd : (h + 1) * hd, :],
                preferred_element_type=F32,
            )

    def emit(h, c, updates):
        c_s[h] = jnp.broadcast_to(c, (requests, hd))
        for t, u in enumerate(updates):
            u_s[h, pl.ds(t, requests, stride=steps), :] = u

    for kh in range(key_heads):
        recurrence(kh, repeats, steps, requests, hd, k_s, None, v_s, a_s, b_s, m_s, None, emit)
    sent = []
    for r in range(requests):
        slot = r % 2
        if r >= 2:
            sent[r - 2].wait()
        rows = slice(r * steps, (r + 1) * steps)
        for h in range(heads):
            k4 = k_s[h // repeats, rows, :]
            k8 = jnp.concatenate([k4, k4], axis=0).astype(BF16)
            u4 = u_s[h, rows, :]
            high = u4.astype(BF16).astype(F32)
            u8 = jnp.concatenate([high, u4 - high], axis=0).astype(BF16)
            added = lax.dot_general(
                k8, u8, (((0,), (0,)), ((), ())), preferred_element_type=F32
            )
            kept = held[r, h * hd : (h + 1) * hd, :].astype(F32) * c_s[h, r : r + 1, :]
            ready[slot, h * hd : (h + 1) * hd, :] = (kept + added).astype(BF16)
        sent.append(pltpu.make_async_copy(ready.at[slot], out_ref.at[place_ref[r]], out_sem.at[slot]))
        sent[-1].start()
    for c in sent[-2:]:
        c.wait()


def landed_states(arrived, before, total, key_heads, heads, steps):
    _, all_rows, hd = arrived[0].shape
    place_row = heads * hd + (key_heads + heads + 2) * steps
    place = jnp.concatenate([a[:, place_row, 0] for a in arrived]).astype(jnp.int32)
    requests = place.shape[0]
    tokens = requests * steps
    state_rows = heads * hd
    hbm = pl.BlockSpec(memory_space=pl.ANY)
    out = pl.pallas_call(
        functools.partial(state_kernel, key_heads, heads, steps, len(arrived)),
        in_specs=[pl.BlockSpec(memory_space=pltpu.SMEM)] + [hbm] * (len(arrived) + len(before)),
        out_specs=hbm,
        out_shape=jax.ShapeDtypeStruct((total, state_rows, hd), BF16),
        input_output_aliases={len(arrived) + 1: 0} if before else {},
        scratch_shapes=[
            pltpu.VMEM((key_heads, tokens, hd), F32),
            pltpu.VMEM((heads, tokens, hd), F32),
            pltpu.VMEM((tokens, hd), F32),
            pltpu.VMEM((tokens, hd), F32),
            pltpu.VMEM((heads, tokens, hd), F32),
            pltpu.VMEM((heads, tokens, hd), F32),
            pltpu.VMEM((heads, requests, hd), F32),
            pltpu.VMEM((requests, state_rows, hd), BF16),
            pltpu.VMEM((requests, all_rows - state_rows, hd), BF16),
            pltpu.VMEM((2, state_rows, hd), BF16),
            pltpu.SemaphoreType.DMA((requests,)),
            pltpu.SemaphoreType.DMA((requests,)),
            pltpu.SemaphoreType.DMA((2,)),
        ],
        compiler_params=pltpu.CompilerParams(vmem_limit_bytes=32 * MIB),
        cost_estimate=pl.CostEstimate(flops=20_000_000, bytes_accessed=requests * MIB, transcendentals=10_000),
        name="landed_states",
    )(place, *arrived, *before)
    return out


def expert_kernel(sides, own_out, experts, where_ref, *rest):
    sources = rest[: 2 * sides]
    gain_ref, up_ref, down_ref = rest[2 * sides : 2 * sides + 3]
    keeps = rest[2 * sides + 3 : 3 * sides + 3]
    give_ref = rest[3 * sides + 3]
    pieces, result_s, sems = rest[-3 - 2 * sides + 1 : -2], rest[-2], rest[-1]
    copies = [pltpu.make_async_copy(a, b, sems.at[i]) for i, (a, b) in enumerate(zip(sources, pieces))]
    for c in copies:
        c.start()
    for c in copies:
        c.wait()
    group_rows = pieces[0].shape[0]
    cols = gain_ref.shape[-1]
    spans = give_ref.shape[1]
    tokens = give_ref.shape[2]
    width = down_ref.shape[-1]
    hidden_units = down_ref.shape[1]
    e = where_ref[0]
    blocks = [(x, c) for x in range(spans) for c in range(2)]
    values = {}
    for x, c in blocks:
        span = slice(x * cols, (x + 1) * cols)
        parts = [
            pieces[2 * y + c][(p ^ c) * tokens : ((p ^ c) + 1) * tokens, span]
            for y in range(sides)
            for p in range(2 * spans)
        ]
        values[x, c] = jnp.concatenate(parts, axis=0).astype(F32)
    total = sum(row_sum(values[b] * values[b]) for b in blocks)
    scale = lax.rsqrt(total * (1.0 / width) + EPS)
    joined = None
    for x, c in blocks:
        block = e ^ (2 * x + c)
        normed = (values[x, c] * scale * gain_ref[pl.ds(block, 1), :]).astype(BF16)
        up = up_ref[0, pl.ds(pl.multiple_of(block * cols, cols), cols), :]
        term = jnp.dot(normed, up, preferred_element_type=F32)
        joined = term if joined is None else joined + term
        if own_out:
            own = values[x, c][:tokens].astype(BF16)
            rest[3 * sides + 4][:, pl.ds(pl.multiple_of(block * cols, cols), cols)] = own
    active = (jax.nn.silu(joined[:, :hidden_units]) * joined[:, hidden_units:]).astype(BF16)
    result = jnp.dot(active, down_ref[0], preferred_element_type=F32).astype(BF16)
    marks = [pieces[2 * y][:, spans * cols :].astype(F32) for y in range(sides)]
    marks = jnp.concatenate(marks, axis=0)
    place = lax.broadcasted_iota(jnp.int32, marks.shape, 1)
    mine = (place == where_ref[1]) | (place == where_ref[1] + experts)
    weight = row_sum(jnp.where(mine, marks, 0.0))
    result_s[...] = (result.astype(F32) * weight).astype(BF16)
    for y in range(sides):
        for x in range(spans):
            for c in range(2):
                start = y * group_rows + (2 * x + c) * tokens
                rows = result_s[start : start + tokens, :]
                if c:
                    give_ref[y, x] = rows
                else:
                    keeps[y][x] = rows


def expert_chunk(where, pieces, gain, gate_up, down_weight, tokens, experts, own_out):
    sides = len(pieces) // 2
    spans, group_rows = gain.shape[0] // 2, pieces[0].shape[0]
    width = down_weight.shape[-1]
    vmem = pl.BlockSpec(memory_space=pltpu.VMEM)
    hbm = pl.BlockSpec(memory_space=pltpu.HBM)
    keep = jax.ShapeDtypeStruct((spans, tokens, width), BF16)
    give = jax.ShapeDtypeStruct((sides, spans, tokens, width), BF16)
    own = [jax.ShapeDtypeStruct((tokens, width), BF16)] if own_out else []
    rows = sides * group_rows
    outs = pl.pallas_call(
        functools.partial(expert_kernel, sides, own_out, experts),
        in_specs=[pl.BlockSpec(memory_space=pltpu.SMEM)] + [hbm] * len(pieces) + [vmem] * 3,
        out_specs=[vmem] * (sides + 1 + len(own)),
        out_shape=[keep] * sides + [give] + own,
        scratch_shapes=[pltpu.VMEM(p.shape, BF16) for p in pieces]
        + [pltpu.VMEM((rows, width), BF16), pltpu.SemaphoreType.DMA((len(pieces),))],
        compiler_params=pltpu.CompilerParams(vmem_limit_bytes=32 * MIB),
        cost_estimate=pl.CostEstimate(
            flops=6 * rows * width * down_weight.shape[1], bytes_accessed=6 * MIB, transcendentals=0
        ),
        name="expert_chunk",
    )(where, *pieces, gain, gate_up, down_weight)
    return outs


def swap(x, axis, d):
    size = lax.axis_size(axis)
    return lax.ppermute(x, axis, [(i, i ^ d) for i in range(size)])


def summed(*terms):
    return functools.reduce(lambda p, q: p + q, [t.astype(F32) for t in terms])


def shards(
    states, query_rows, key_rows, value_rows, gate_rows, beta_logit, decay_logit, residual,
    route_ids, route_prob, out_weight, core_gain, moe_gain, gate_up, down_weight, new_home,
):
    requests, heads, hd, _ = states.shape
    steps = query_rows.shape[1]
    width = residual.shape[-1]
    tokens = requests * steps
    lanes = lax.axis_size("ep")
    groups = lax.axis_size("dp")
    my_lane = lax.axis_index("ep")
    my_group = lax.axis_index("dp")
    kw, vw = key_rows.shape[-1], value_rows.shape[-1]
    top = route_ids.shape[-1]

    experts = groups * lanes
    cols = out_weight.shape[1]
    me = my_group * lanes + my_lane

    with jax.named_scope("core"):
        sent = core_rows(
            my_lane.reshape(1), lanes, experts, states, query_rows, key_rows, value_rows,
            gate_rows, beta_logit, decay_logit, core_gain, residual, route_ids, route_prob,
        )
        sent, new_home = lax.optimization_barrier((sent, new_home))
        got = {j: swap(sent[j], "ep", j) for j in range(lanes - 1, 0, -1)}
        got = [sent[0]] + [got[j] for j in range(1, lanes)]
    with jax.named_scope("send_states"):
        packed = pack_states(
            new_home, my_lane.reshape(1), lanes, states, key_rows, value_rows, beta_logit, decay_logit
        )
    with jax.named_scope("attention"):
        got, packed = lax.optimization_barrier((got, packed))
        hidden_cols, marks = project(got, out_weight)
        others = []
        for d in range(2, lanes, 2):
            other = swap(hidden_cols, "ep", d).reshape(lanes, tokens, cols)
            others.append(jnp.concatenate([other[j ^ d] for j in range(lanes)], axis=0))
        held = jnp.concatenate([hidden_cols] + others + [marks], axis=1)
        held, packed = lax.optimization_barrier((held, packed))
    with jax.named_scope("send_states"):
        cap = requests // lanes
        near_states = [packed[0], swap(packed[1], "ep", 1)]
        far_states = []
        for i, piece in enumerate(packed[2:]):
            if i:
                piece, far_states[-1] = lax.optimization_barrier((piece, far_states[-1]))
            far_states.append(swap(piece, "ep", 2 + i // cap))

    gain = moe_gain.reshape(lanes, cols)
    where = jnp.stack([my_lane, me])
    far = groups // 2
    chunks = [0] + [d for d in range(groups - 2, 0, -2) if d != far] + [far]
    tie = lax.optimization_barrier
    own_rows = None
    with jax.named_scope("tokens"):
        near = {d: swap(held, "dp", d) if d else held for d in chunks[:-1]}
        later, near[chunks[1]] = tie((held, near[chunks[1]]))
        across = {d: swap(near[d], "dp", 1) for d in chunks[:-1]}
        near[far] = swap(later, "dp", far)
        pieces = {}
        for d in chunks:
            aside = across.get(d)
            if d == far:
                near[d], pieces[chunks[-2]][2] = tie((near[d], pieces[chunks[-2]][2]))
                aside = swap(near[d], "dp", 1)
            pieces[d] = [near[d], swap(near[d], "ep", 1), aside, swap(aside, "ep", 1)]
        pieces[0], pieces[chunks[1]][2] = tie((pieces[0], pieces[chunks[1]][2]))
        pieces[0], far_states[0] = tie((pieces[0], far_states[0]))
        pieces[far], far_states[1] = tie((pieces[far], far_states[1]))
    sums = {}
    for d in chunks:
        with jax.named_scope("experts"):
            outs = expert_chunk(where, pieces[d], gain, gate_up, down_weight, tokens, experts, d == 0)
            keep_near, keep_across, give = outs[:3]
            if d == 0:
                own_rows = outs[3]
        with jax.named_scope("way_back"):
            taken = swap(give, "ep", 1)
            aside = summed(keep_across, taken[1]).astype(BF16)
            if d == far:
                aside, sums[0], sums[chunks[1]] = tie((aside, sums[0], sums[chunks[1]]))
            back = swap(aside, "dp", 1)
            if d == far:
                back, far_states[2] = tie((back, far_states[2]))
            chunk = summed(keep_near, taken[0], back)
            sums[d] = chunk.astype(BF16) if d else chunk
    with jax.named_scope("landed"):
        sizes = (requests, kw // hd, heads, steps)
        sums[far], arrived = tie((sums[far], near_states + far_states[:-2]))
        moved_out = landed_states(arrived, [], *sizes)
    with jax.named_scope("way_back"):
        sums = [swap(sums[d], "dp", d) if d else sums[d] for d in chunks]
        sums, moved_out = tie((sums, moved_out))
    with jax.named_scope("landed"):
        moved_out = landed_states(far_states[-2:], [moved_out], *sizes)
        moved_out = moved_out.reshape(requests, heads, hd, hd)
    with jax.named_scope("mixed"):
        mixed = summed(own_rows, *[s[0] for s in sums])
        for x in range(1, lanes // 2):
            mixed = mixed + swap(summed(*[s[x] for s in sums]).astype(BF16), "ep", 2 * x).astype(F32)
        mixed_out = mixed.astype(BF16)
    return mixed_out.reshape(requests, steps, width), moved_out


def solution(mesh):
    row = P(("dp", "ep"), None, None)
    placed = (P(("dp", "ep"), None, None, None),) + (row,) * 9 + (
        P(None, "ep"), P(), P(), row, row, P(("dp", "ep")),
    )
    return jax.shard_map(
        shards,
        mesh=mesh,
        in_specs=placed,
        out_specs=(row, P(("dp", "ep"), None, None, None)),
        check_vma=False,
    )
```

```python
import functools

import jax
import jax.numpy as jnp
from jax import lax
from jax.experimental import pallas as pl
from jax.experimental.pallas import tpu as pltpu
from jax.sharding import PartitionSpec as P

EPS = 1e-06
F32 = jnp.float32
BF16 = jnp.bfloat16
MIB = 1 << 20


def row_sum(x):
    return jnp.sum(x, axis=-1, keepdims=True)


def spread_rows(ref, scratch, requests, steps):
    for r in range(requests):
        split_heads(ref[r].astype(F32), scratch, r, steps)


def split_heads(values, scratch, r, steps):
    hd = scratch.shape[-1]
    for h in range(scratch.shape[0]):
        scratch[h, r * steps : (r + 1) * steps, :] = values[:, h * hd : (h + 1) * hd]


def at_step(scratch, t, requests, steps, head=None):
    if head is None:
        return scratch[pl.ds(t, requests, stride=steps), :]
    return scratch[head, pl.ds(t, requests, stride=steps), :]


def recurrence(kh, repeats, steps, requests, hd, k_s, q_s, v_s, a_s, b_s, m_s, emit_out, emit_state):
    per = m_s.shape[1] // requests
    ks = [at_step(k_s, t, requests, steps, kh) for t in range(steps)]
    rk = [lax.rsqrt(row_sum(k * k) + EPS) for k in ks]
    kn = [k * r for k, r in zip(ks, rk)]
    kk = {(i, t): row_sum(kn[i] * kn[t]) for t in range(steps) for i in range(t)}
    if emit_out is not None:
        qs = [at_step(q_s, t, requests, steps, kh) for t in range(steps)]
        rq = [lax.rsqrt(row_sum(q * q) + EPS) * hd**-0.5 for q in qs]
        qn = [q * r for q, r in zip(qs, rq)]
        kq = {(i, t): row_sum(kn[i] * qn[t]) for t in range(steps) for i in range(t + 1)}
    for h in range(kh * repeats, (kh + 1) * repeats):
        decayed = []
        c = None
        for t in range(steps):
            a = at_step(a_s, t, requests, steps)[:, h : h + 1]
            b = at_step(b_s, t, requests, steps)[:, h : h + 1]
            decayed = [w * a for w in decayed]
            c = a if c is None else c * a
            m = (c * rk[t]) * at_step(m_s, t, requests, per, h)
            for i in range(t):
                m = m + kk[i, t] * decayed[i]
            decayed.append((at_step(v_s, t, requests, steps, h) - m) * b)
            if emit_out is not None:
                o = (c * rq[t]) * at_step(m_s, steps + t, requests, per, h)
                for i in range(t + 1):
                    o = o + kq[i, t] * decayed[i]
                emit_out(t, h, o)
        if emit_state is not None:
            emit_state(h, c, [w * r for w, r in zip(decayed, rk)])


def sigmoid_rows(ref, scratch, requests, steps):
    for r in range(requests):
        scratch[r * steps : (r + 1) * steps, : ref.shape[-1]] = jax.nn.sigmoid(ref[r].astype(F32))


def packed_rows(key_heads, heads, steps):
    used = (key_heads + heads + 3) * steps
    return used, -(-used // 16) * 16


def core_kernel(
    lanes, experts, lane_ref, state_ref, q_ref, k_ref, v_ref, g_ref, b_ref, a_ref, gain_ref,
    res_ref, ids_ref, prob_ref, *rest,
):
    outs = rest[:lanes]
    k_s, q_s, v_s, g_s, a_s, b_s, m_s, o_s, r_s, w_s, held, in_sem = rest[lanes:]
    requests, steps, _ = k_ref.shape
    hd = held.shape[-1]
    heads, key_heads = v_s.shape[0], k_s.shape[0]
    repeats = heads // key_heads
    copies = []
    for r in range(requests):
        copies.append(pltpu.make_async_copy(state_ref.at[r], held.at[r], in_sem.at[r]))
        copies[-1].start()
    spread_rows(k_ref, k_s, requests, steps)
    spread_rows(q_ref, q_s, requests, steps)
    spread_rows(v_ref, v_s, requests, steps)
    spread_rows(g_ref, g_s, requests, steps)
    sigmoid_rows(a_ref, a_s, requests, steps)
    sigmoid_rows(b_ref, b_s, requests, steps)
    top = ids_ref.shape[-1]
    place = lax.broadcasted_iota(jnp.int32, (steps, w_s.shape[-1]), 1)
    for r in range(requests):
        rows = slice(r * steps, (r + 1) * steps)
        r_s[rows, :] = res_ref[r].astype(F32)
        prob = prob_ref[r]
        prob = prob / row_sum(prob)
        weight = jnp.zeros(place.shape, F32)
        ids = ids_ref[r]
        for j in range(top):
            high = prob[:, j : j + 1].astype(BF16).astype(F32)
            weight = jnp.where(place == ids[:, j : j + 1], high, weight)
            weight = jnp.where(place == ids[:, j : j + 1] + experts, prob[:, j : j + 1] - high, weight)
        w_s[rows, :] = weight
    for r in range(requests):
        copies[r].wait()
        rows = slice(r * steps, (r + 1) * steps)
        for kh in range(key_heads):
            left = jnp.concatenate([k_s[kh, rows, :], q_s[kh, rows, :]], axis=0).astype(BF16)
            for h in range(kh * repeats, (kh + 1) * repeats):
                m_s[h, r * 2 * steps : (r + 1) * 2 * steps, :] = jnp.dot(
                    left, held[r, h * hd : (h + 1) * hd, :], preferred_element_type=F32
                )
    gain = gain_ref[...]

    def emit(t, h, o):
        gate = at_step(g_s, t, requests, steps, h)
        scaled = o * lax.rsqrt(row_sum(o * o) * (1.0 / hd) + EPS)
        o_s[h, pl.ds(t, requests, stride=steps), :] = scaled * gain * jax.nn.silu(gate)

    for kh in range(key_heads):
        recurrence(kh, repeats, steps, requests, hd, k_s, q_s, v_s, a_s, b_s, m_s, emit, None)
    width = heads * hd
    cols = res_ref.shape[-1] // lanes
    for h in range(heads):
        part = o_s[h].astype(BF16)
        for j in range(lanes):
            outs[j][:, h * hd : (h + 1) * hd] = part
    marks = w_s[...].astype(BF16)
    for j in range(lanes):
        start = pl.multiple_of((lane_ref[0] ^ j) * cols, cols)
        outs[j][:, width : width + cols] = r_s[:, pl.ds(start, cols)].astype(BF16)
        outs[j][:, width + cols :] = marks


def core_rows(
    lane, lanes, experts, states, query_rows, key_rows, value_rows, gate_rows, beta_logit, decay_logit,
    core_gain, residual, route_ids, route_prob,
):
    requests, heads, hd, _ = states.shape
    steps = key_rows.shape[1]
    kw, vw = key_rows.shape[-1], value_rows.shape[-1]
    tokens = requests * steps
    width = residual.shape[-1]
    weight_lanes = -(-2 * experts // 128) * 128
    vmem, hbm = pl.BlockSpec(memory_space=pltpu.VMEM), pl.BlockSpec(memory_space=pl.ANY)
    return pl.pallas_call(
        functools.partial(core_kernel, lanes, experts),
        in_specs=[pl.BlockSpec(memory_space=pltpu.SMEM), hbm] + [vmem] * 10,
        out_specs=[vmem] * lanes,
        out_shape=[jax.ShapeDtypeStruct((tokens, vw + width // lanes + weight_lanes), BF16)] * lanes,
        scratch_shapes=[
            pltpu.VMEM((kw // hd, tokens, hd), F32),
            pltpu.VMEM((kw // hd, tokens, hd), F32),
            pltpu.VMEM((heads, tokens, hd), F32),
            pltpu.VMEM((heads, tokens, hd), F32),
            pltpu.VMEM((tokens, 128), F32),
            pltpu.VMEM((tokens, 128), F32),
            pltpu.VMEM((heads, 2 * tokens, hd), F32),
            pltpu.VMEM((heads, tokens, hd), F32),
            pltpu.VMEM((tokens, width), F32),
            pltpu.VMEM((tokens, weight_lanes), F32),
            pltpu.VMEM((requests, heads * hd, hd), BF16),
            pltpu.SemaphoreType.DMA((requests,)),
        ],
        compiler_params=pltpu.CompilerParams(vmem_limit_bytes=60 * MIB),
        cost_estimate=pl.CostEstimate(flops=20_000_000, bytes_accessed=9 * MIB, transcendentals=100_000),
        name="core_rows",
    )(
        lane, states.reshape(requests, heads * hd, hd), query_rows, key_rows, value_rows, gate_rows,
        beta_logit, decay_logit, core_gain.reshape(1, hd), residual, route_ids, route_prob,
    )


def pack_kernel(lanes, key_heads, home_ref, lane_ref, state_ref, k_ref, v_ref, b_ref, a_ref, *rest):
    outs = rest[:-4]
    held, pay_f, in_sem, out_sem = rest[-4:]
    requests, steps, _ = k_ref.shape
    hd = held.shape[-1]
    heads = v_ref.shape[-1] // hd
    state_rows = heads * hd
    cap = requests // lanes
    copies = []
    for r in range(requests):
        source = state_ref.at[r]
        copies.append(pltpu.make_async_copy(source, held.at[r, pl.ds(0, state_rows)], in_sem.at[r]))
        copies[-1].start()
    target = [lax.rem(lax.div(home_ref[r], requests), lanes) ^ lane_ref[0] for r in range(requests)]
    ranks = [
        sum([(target[p] == target[r]).astype(jnp.int32) for p in range(r)], jnp.int32(0))
        for r in range(requests)
    ]
    pay_f[...] = jnp.zeros_like(pay_f)
    for r in range(requests):
        keys, vals = k_ref[r].astype(F32), v_ref[r].astype(F32)
        for kh in range(key_heads):
            pay_f[kh * steps : (kh + 1) * steps, :] = keys[:, kh * hd : (kh + 1) * hd]
        for h in range(heads):
            at = (key_heads + h) * steps
            pay_f[at : at + steps, :] = vals[:, h * hd : (h + 1) * hd]
        at = (key_heads + heads) * steps
        pay_f[at : at + steps, :heads] = a_ref[r].astype(F32)
        pay_f[at + steps : at + 2 * steps, :heads] = b_ref[r].astype(F32)
        place = lax.rem(home_ref[r], requests).astype(F32)
        pay_f[at + 2 * steps : at + 3 * steps, :] = jnp.full((steps, hd), place, F32)
        held[r, state_rows:, :] = pay_f[...].astype(BF16)
    for r in range(requests):
        copies[r].wait()
        for d in range(lanes):
            for q in range(cap if d > 1 else 1):
                dest = outs[d].at[ranks[r]] if d < 2 else outs[2 + (d - 2) * cap + q].at[0]
                chosen = (target[r] == d) & (ranks[r] == q) if d > 1 else target[r] == d

                @pl.when(chosen)
                def _():
                    pltpu.make_async_copy(held.at[r], dest, out_sem.at[r]).start()

    for r in range(requests):
        pltpu.make_async_copy(held.at[r], outs[0].at[0], out_sem.at[r]).wait()


def pack_states(home, lane, lanes, states, key_rows, value_rows, beta_logit, decay_logit):
    requests, heads, hd, _ = states.shape
    steps = key_rows.shape[1]
    key_heads = key_rows.shape[-1] // hd
    cap = requests // lanes
    _, pay_rows = packed_rows(key_heads, heads, steps)
    all_rows = heads * hd + pay_rows
    vmem, hbm = pl.BlockSpec(memory_space=pltpu.VMEM), pl.BlockSpec(memory_space=pl.ANY)
    smem = pl.BlockSpec(memory_space=pltpu.SMEM)
    sizes = [cap] * 2 + [1] * (cap * (lanes - 2))
    return pl.pallas_call(
        functools.partial(pack_kernel, lanes, key_heads),
        in_specs=[smem, smem, hbm] + [vmem] * 4,
        out_specs=[hbm] * len(sizes),
        out_shape=[jax.ShapeDtypeStruct((n, all_rows, hd), BF16) for n in sizes],
        scratch_shapes=[
            pltpu.VMEM((requests, all_rows, hd), BF16),
            pltpu.VMEM((pay_rows, hd), F32),
            pltpu.SemaphoreType.DMA((requests,)),
            pltpu.SemaphoreType.DMA((requests,)),
        ],
        compiler_params=pltpu.CompilerParams(vmem_limit_bytes=48 * MIB),
        cost_estimate=pl.CostEstimate(flops=0, bytes_accessed=9 * MIB, transcendentals=0),
        name="pack_states",
    )(home, lane, states.reshape(requests, heads * hd, hd), key_rows, value_rows, beta_logit, decay_logit)


def project_kernel(*refs):
    lanes = len(refs) - 3
    weight_ref, out_ref, marks_ref = refs[lanes:]
    depth, cols = weight_ref.shape
    rows = jnp.concatenate([refs[j][...] for j in range(lanes)], axis=0)
    attention = jnp.dot(rows[:, :depth], weight_ref[...], preferred_element_type=F32).astype(BF16)
    before = rows[:, depth : depth + cols].astype(F32)
    out_ref[...] = (before + attention.astype(F32)).astype(BF16)
    marks_ref[...] = rows[:, depth + cols :]


def project(got, out_weight):
    tokens, wide = got[0].shape
    depth, cols = out_weight.shape
    rows = tokens * len(got)
    vmem = pl.BlockSpec(memory_space=pltpu.VMEM)
    return pl.pallas_call(
        project_kernel,
        in_specs=[vmem] * (len(got) + 1),
        out_specs=[vmem] * 2,
        out_shape=[
            jax.ShapeDtypeStruct((rows, cols), BF16),
            jax.ShapeDtypeStruct((rows, wide - depth - cols), BF16),
        ],
        compiler_params=pltpu.CompilerParams(vmem_limit_bytes=24 * MIB),
        cost_estimate=pl.CostEstimate(
            flops=2 * rows * depth * cols, bytes_accessed=3 * MIB, transcendentals=0
        ),
        name="project",
    )(*got, out_weight)


def state_kernel(
    key_heads, heads, steps, count, *rest
):
    arrived = rest[:count]
    out_ref, k_s, v_s, a_s, b_s, m_s, u_s, c_s, held, pay_s, ready, in_sem, pay_sem, out_sem = rest[-14:]
    requests, state_rows, hd = held.shape
    origin = [(a, j) for a in arrived for j in range(a.shape[0])]
    repeats = heads // key_heads
    pays, copies = [], []
    for r in range(requests):
        pays.append(
            pltpu.make_async_copy(
                origin[r][0].at[origin[r][1], pl.ds(state_rows, pay_s.shape[1])], pay_s.at[r], pay_sem.at[r]
            )
        )
        pays[-1].start()
    for r in range(requests):
        copies.append(
            pltpu.make_async_copy(
                origin[r][0].at[origin[r][1], pl.ds(0, state_rows)], held.at[r], in_sem.at[r]
            )
        )
        copies[-1].start()
    places = []
    for r in range(requests):
        pays[r].wait()
        rows = slice(r * steps, (r + 1) * steps)
        pay = pay_s[r].astype(F32)
        for kh in range(key_heads):
            k_s[kh, rows, :] = pay[kh * steps : (kh + 1) * steps]
        for h in range(heads):
            v_s[h, rows, :] = pay[(key_heads + h) * steps : (key_heads + h + 1) * steps]
        at = (key_heads + heads) * steps
        a_s[rows, :] = jax.nn.sigmoid(pay[at : at + steps])
        b_s[rows, :] = jax.nn.sigmoid(pay[at + steps : at + 2 * steps])
        places.append(jnp.max(pay[at + 2 * steps : at + 3 * steps]).astype(jnp.int32))
    for r in range(requests):
        copies[r].wait()
        rows = slice(r * steps, (r + 1) * steps)
        for h in range(heads):
            m_s[h, rows, :] = jnp.dot(
                k_s[h // repeats, rows, :].astype(BF16),
                held[r, h * hd : (h + 1) * hd, :],
                preferred_element_type=F32,
            )

    def emit(h, c, updates):
        c_s[h] = jnp.broadcast_to(c, (requests, hd))
        for t, u in enumerate(updates):
            u_s[h, pl.ds(t, requests, stride=steps), :] = u

    for kh in range(key_heads):
        recurrence(kh, repeats, steps, requests, hd, k_s, None, v_s, a_s, b_s, m_s, None, emit)
    sent = []
    for r in range(requests):
        slot = r % 2
        if r >= 2:
            sent[r - 2].wait()
        rows = slice(r * steps, (r + 1) * steps)
        for h in range(heads):
            k4 = k_s[h // repeats, rows, :]
            k8 = jnp.concatenate([k4, k4], axis=0).astype(BF16)
            u4 = u_s[h, rows, :]
            high = u4.astype(BF16).astype(F32)
            u8 = jnp.concatenate([high, u4 - high], axis=0).astype(BF16)
            added = lax.dot_general(
                k8, u8, (((0,), (0,)), ((), ())), preferred_element_type=F32
            )
            kept = held[r, h * hd : (h + 1) * hd, :].astype(F32) * c_s[h, r : r + 1, :]
            ready[slot, h * hd : (h + 1) * hd, :] = (kept + added).astype(BF16)
        sent.append(pltpu.make_async_copy(ready.at[slot], out_ref.at[places[r]], out_sem.at[slot]))
        sent[-1].start()
    for c in sent[-2:]:
        c.wait()


def landed_states(arrived, before, total, key_heads, heads, steps):
    _, all_rows, hd = arrived[0].shape
    requests = sum(a.shape[0] for a in arrived)
    tokens = requests * steps
    state_rows = heads * hd
    hbm = pl.BlockSpec(memory_space=pl.ANY)
    out = pl.pallas_call(
        functools.partial(state_kernel, key_heads, heads, steps, len(arrived)),
        in_specs=[hbm] * (len(arrived) + len(before)),
        out_specs=hbm,
        out_shape=jax.ShapeDtypeStruct((total, state_rows, hd), BF16),
        input_output_aliases={len(arrived): 0} if before else {},
        scratch_shapes=[
            pltpu.VMEM((key_heads, tokens, hd), F32),
            pltpu.VMEM((heads, tokens, hd), F32),
            pltpu.VMEM((tokens, hd), F32),
            pltpu.VMEM((tokens, hd), F32),
            pltpu.VMEM((heads, tokens, hd), F32),
            pltpu.VMEM((heads, tokens, hd), F32),
            pltpu.VMEM((heads, requests, hd), F32),
            pltpu.VMEM((requests, state_rows, hd), BF16),
            pltpu.VMEM((requests, all_rows - state_rows, hd), BF16),
            pltpu.VMEM((2, state_rows, hd), BF16),
            pltpu.SemaphoreType.DMA((requests,)),
            pltpu.SemaphoreType.DMA((requests,)),
            pltpu.SemaphoreType.DMA((2,)),
        ],
        compiler_params=pltpu.CompilerParams(vmem_limit_bytes=32 * MIB),
        cost_estimate=pl.CostEstimate(flops=20_000_000, bytes_accessed=requests * MIB, transcendentals=10_000),
        name="landed_states",
    )(*arrived, *before)
    return out


def expert_kernel(sides, own_out, experts, where_ref, *rest):
    sources = rest[: 2 * sides]
    gain_ref, up_ref, down_ref = rest[2 * sides : 2 * sides + 3]
    keeps = rest[2 * sides + 3 : 3 * sides + 3]
    give_ref = rest[3 * sides + 3]
    pieces, result_s, sems = rest[-3 - 2 * sides + 1 : -2], rest[-2], rest[-1]
    copies = [pltpu.make_async_copy(a, b, sems.at[i]) for i, (a, b) in enumerate(zip(sources, pieces))]
    for c in copies:
        c.start()
    for c in copies:
        c.wait()
    group_rows = pieces[0].shape[0]
    cols = gain_ref.shape[-1]
    spans = give_ref.shape[1]
    tokens = give_ref.shape[2]
    width = down_ref.shape[-1]
    hidden_units = down_ref.shape[1]
    e = where_ref[0]
    blocks = [(x, c) for x in range(spans) for c in range(2)]
    values = {}
    for x, c in blocks:
        span = slice(x * cols, (x + 1) * cols)
        parts = [
            pieces[2 * y + c][(p ^ c) * tokens : ((p ^ c) + 1) * tokens, span]
            for y in range(sides)
            for p in range(2 * spans)
        ]
        values[x, c] = jnp.concatenate(parts, axis=0).astype(F32)
    total = sum(row_sum(values[b] * values[b]) for b in blocks)
    scale = lax.rsqrt(total * (1.0 / width) + EPS)
    joined = None
    for x, c in blocks:
        block = e ^ (2 * x + c)
        normed = (values[x, c] * scale * gain_ref[pl.ds(block, 1), :]).astype(BF16)
        up = up_ref[0, pl.ds(pl.multiple_of(block * cols, cols), cols), :]
        term = jnp.dot(normed, up, preferred_element_type=F32)
        joined = term if joined is None else joined + term
        if own_out:
            own = values[x, c][:tokens].astype(BF16)
            rest[3 * sides + 4][:, pl.ds(pl.multiple_of(block * cols, cols), cols)] = own
    active = (jax.nn.silu(joined[:, :hidden_units]) * joined[:, hidden_units:]).astype(BF16)
    result = jnp.dot(active, down_ref[0], preferred_element_type=F32).astype(BF16)
    marks = [pieces[2 * y][:, spans * cols :].astype(F32) for y in range(sides)]
    marks = jnp.concatenate(marks, axis=0)
    place = lax.broadcasted_iota(jnp.int32, marks.shape, 1)
    mine = (place == where_ref[1]) | (place == where_ref[1] + experts)
    weight = row_sum(jnp.where(mine, marks, 0.0))
    result_s[...] = (result.astype(F32) * weight).astype(BF16)
    for y in range(sides):
        for x in range(spans):
            for c in range(2):
                start = y * group_rows + (2 * x + c) * tokens
                rows = result_s[start : start + tokens, :]
                if c:
                    give_ref[y, x] = rows
                else:
                    keeps[y][x] = rows


def expert_chunk(where, pieces, gain, gate_up, down_weight, tokens, experts, own_out):
    sides = len(pieces) // 2
    spans, group_rows = gain.shape[0] // 2, pieces[0].shape[0]
    width = down_weight.shape[-1]
    vmem = pl.BlockSpec(memory_space=pltpu.VMEM)
    hbm = pl.BlockSpec(memory_space=pltpu.HBM)
    keep = jax.ShapeDtypeStruct((spans, tokens, width), BF16)
    give = jax.ShapeDtypeStruct((sides, spans, tokens, width), BF16)
    own = [jax.ShapeDtypeStruct((tokens, width), BF16)] if own_out else []
    rows = sides * group_rows
    outs = pl.pallas_call(
        functools.partial(expert_kernel, sides, own_out, experts),
        in_specs=[pl.BlockSpec(memory_space=pltpu.SMEM)] + [hbm] * len(pieces) + [vmem] * 3,
        out_specs=[vmem] * (sides + 1 + len(own)),
        out_shape=[keep] * sides + [give] + own,
        scratch_shapes=[pltpu.VMEM(p.shape, BF16) for p in pieces]
        + [pltpu.VMEM((rows, width), BF16), pltpu.SemaphoreType.DMA((len(pieces),))],
        compiler_params=pltpu.CompilerParams(vmem_limit_bytes=32 * MIB),
        cost_estimate=pl.CostEstimate(
            flops=6 * rows * width * down_weight.shape[1], bytes_accessed=6 * MIB, transcendentals=0
        ),
        name="expert_chunk",
    )(where, *pieces, gain, gate_up, down_weight)
    return outs


def swap(x, axis, d):
    size = lax.axis_size(axis)
    return lax.ppermute(x, axis, [(i, i ^ d) for i in range(size)])


def summed(*terms):
    return functools.reduce(lambda p, q: p + q, [t.astype(F32) for t in terms])


def shards(
    states, query_rows, key_rows, value_rows, gate_rows, beta_logit, decay_logit, residual,
    route_ids, route_prob, out_weight, core_gain, moe_gain, gate_up, down_weight, new_home,
):
    requests, heads, hd, _ = states.shape
    steps = query_rows.shape[1]
    width = residual.shape[-1]
    tokens = requests * steps
    lanes = lax.axis_size("ep")
    groups = lax.axis_size("dp")
    my_lane = lax.axis_index("ep")
    my_group = lax.axis_index("dp")
    kw, vw = key_rows.shape[-1], value_rows.shape[-1]
    top = route_ids.shape[-1]

    experts = groups * lanes
    cols = out_weight.shape[1]
    me = my_group * lanes + my_lane

    with jax.named_scope("core"):
        sent = core_rows(
            my_lane.reshape(1), lanes, experts, states, query_rows, key_rows, value_rows,
            gate_rows, beta_logit, decay_logit, core_gain, residual, route_ids, route_prob,
        )
        sent, new_home = lax.optimization_barrier((sent, new_home))
        got = {j: swap(sent[j], "ep", j) for j in range(lanes - 1, 0, -1)}
        got = [sent[0]] + [got[j] for j in range(1, lanes)]
    with jax.named_scope("send_states"):
        packed = pack_states(
            new_home, my_lane.reshape(1), lanes, states, key_rows, value_rows, beta_logit, decay_logit
        )
    with jax.named_scope("attention"):
        got, packed = lax.optimization_barrier((got, packed))
        hidden_cols, marks = project(got, out_weight)
        others = []
        for d in range(2, lanes, 2):
            other = swap(hidden_cols, "ep", d).reshape(lanes, tokens, cols)
            others.append(jnp.concatenate([other[j ^ d] for j in range(lanes)], axis=0))
        held = jnp.concatenate([hidden_cols] + others + [marks], axis=1)
        held, packed = lax.optimization_barrier((held, packed))
    with jax.named_scope("send_states"):
        cap = requests // lanes
        near_states = [packed[0], swap(packed[1], "ep", 1)]
        far_states = []
        for i, piece in enumerate(packed[2:]):
            if i:
                piece, far_states[-1] = lax.optimization_barrier((piece, far_states[-1]))
            far_states.append(swap(piece, "ep", 2 + i // cap))

    gain = moe_gain.reshape(lanes, cols)
    where = jnp.stack([my_lane, me])
    far = groups // 2
    chunks = [0] + [d for d in range(groups - 2, 0, -2) if d != far] + [far]
    tie = lax.optimization_barrier
    with jax.named_scope("tokens"):
        near = {d: swap(held, "dp", d) if d else held for d in chunks}
        across = {0: swap(held, "dp", 1)}
    sums, keeps, asides, takens = {}, {}, {}, {}
    for i, d in enumerate(chunks):
        with jax.named_scope("tokens"):
            if i == 1:
                near[d], keeps[0] = tie((near[d], keeps[0]))
            if i:
                across[d] = swap(near[d], "dp", 1)
            beside = across[d]
            if d == far:
                beside, keeps = tie((beside, keeps))
            pieces = [near[d], swap(near[d], "ep", 1), across[d], swap(beside, "ep", 1)]
            if i < 2:
                pieces, far_states[i] = tie((pieces, far_states[i]))
        with jax.named_scope("experts"):
            outs = expert_chunk(where, pieces, gain, gate_up, down_weight, tokens, experts, d == 0)
            keeps[d] = outs[0]
            if d == 0:
                own_rows = outs[3]
        with jax.named_scope("way_back"):
            takens[d] = swap(outs[2], "ep", 1)
            asides[d] = summed(outs[1], takens[d][1]).astype(BF16)
    for d in chunks:
        with jax.named_scope("way_back"):
            if d == far:
                asides[d], sums[0] = tie((asides[d], sums[0]))
            back = swap(asides[d], "dp", 1)
            if d == far:
                back, sums[chunks[1]], far_states[2] = tie((back, sums[chunks[1]], far_states[2]))
            chunk = summed(keeps[d], takens[d][0], back)
            sums[d] = chunk.astype(BF16) if d else chunk
    with jax.named_scope("landed"):
        sizes = (requests, kw // hd, heads, steps)
        sums[far], arrived = tie((sums[far], near_states + far_states[:-2]))
        moved_out = landed_states(arrived, [], *sizes)
    with jax.named_scope("way_back"):
        sums = [swap(sums[d], "dp", d) if d else sums[d] for d in chunks]
        sums, moved_out = tie((sums, moved_out))
    with jax.named_scope("landed"):
        moved_out = landed_states(far_states[-2:], [moved_out], *sizes)
        moved_out = moved_out.reshape(requests, heads, hd, hd)
    with jax.named_scope("mixed"):
        mixed = summed(own_rows, *[s[0] for s in sums])
        for x in range(1, lanes // 2):
            mixed = mixed + swap(summed(*[s[x] for s in sums]).astype(BF16), "ep", 2 * x).astype(F32)
        mixed_out = mixed.astype(BF16)
    return mixed_out.reshape(requests, steps, width), moved_out


def solution(mesh):
    row = P(("dp", "ep"), None, None)
    placed = (P(("dp", "ep"), None, None, None),) + (row,) * 9 + (
        P(None, "ep"), P(), P(), row, row, P(("dp", "ep")),
    )
    return jax.shard_map(
        shards,
        mesh=mesh,
        in_specs=placed,
        out_specs=(row, P(("dp", "ep"), None, None, None)),
        check_vma=False,
    )
```

```python
import functools

import jax
import jax.numpy as jnp
from jax import lax
from jax.experimental import pallas as pl
from jax.experimental.pallas import tpu as pltpu
from jax.sharding import PartitionSpec as P

EPS = 1e-06
F32 = jnp.float32
BF16 = jnp.bfloat16
MIB = 1 << 20


def row_sum(x):
    return jnp.sum(x, axis=-1, keepdims=True)


def spread_rows(ref, scratch, requests, steps):
    for r in range(requests):
        split_heads(ref[r].astype(F32), scratch, r, steps)


def split_heads(values, scratch, r, steps):
    hd = scratch.shape[-1]
    for h in range(scratch.shape[0]):
        scratch[h, r * steps : (r + 1) * steps, :] = values[:, h * hd : (h + 1) * hd]


def at_step(scratch, t, requests, steps, head=None):
    if head is None:
        return scratch[pl.ds(t, requests, stride=steps), :]
    return scratch[head, pl.ds(t, requests, stride=steps), :]


def recurrence(kh, repeats, steps, requests, hd, k_s, q_s, v_s, a_s, b_s, m_s, emit_out, emit_state):
    per = m_s.shape[1] // requests
    ks = [at_step(k_s, t, requests, steps, kh) for t in range(steps)]
    rk = [lax.rsqrt(row_sum(k * k) + EPS) for k in ks]
    kn = [k * r for k, r in zip(ks, rk)]
    kk = {(i, t): row_sum(kn[i] * kn[t]) for t in range(steps) for i in range(t)}
    if emit_out is not None:
        qs = [at_step(q_s, t, requests, steps, kh) for t in range(steps)]
        rq = [lax.rsqrt(row_sum(q * q) + EPS) * hd**-0.5 for q in qs]
        qn = [q * r for q, r in zip(qs, rq)]
        kq = {(i, t): row_sum(kn[i] * qn[t]) for t in range(steps) for i in range(t + 1)}
    for h in range(kh * repeats, (kh + 1) * repeats):
        decayed = []
        c = None
        for t in range(steps):
            a = at_step(a_s, t, requests, steps)[:, h : h + 1]
            b = at_step(b_s, t, requests, steps)[:, h : h + 1]
            decayed = [w * a for w in decayed]
            c = a if c is None else c * a
            m = (c * rk[t]) * at_step(m_s, t, requests, per, h)
            for i in range(t):
                m = m + kk[i, t] * decayed[i]
            decayed.append((at_step(v_s, t, requests, steps, h) - m) * b)
            if emit_out is not None:
                o = (c * rq[t]) * at_step(m_s, steps + t, requests, per, h)
                for i in range(t + 1):
                    o = o + kq[i, t] * decayed[i]
                emit_out(t, h, o)
        if emit_state is not None:
            emit_state(h, c, [w * r for w, r in zip(decayed, rk)])


def sigmoid_rows(ref, scratch, requests, steps):
    for r in range(requests):
        scratch[r * steps : (r + 1) * steps, : ref.shape[-1]] = jax.nn.sigmoid(ref[r].astype(F32))


def packed_rows(key_heads, heads, steps):
    used = (key_heads + heads + 3) * steps
    return used, -(-used // 16) * 16


def core_kernel(
    lanes, experts, lane_ref, state_ref, q_ref, k_ref, v_ref, g_ref, b_ref, a_ref, gain_ref,
    res_ref, ids_ref, prob_ref, *rest,
):
    outs = rest[:lanes]
    k_s, q_s, v_s, g_s, a_s, b_s, m_s, o_s, r_s, w_s, held, in_sem = rest[lanes:]
    requests, steps, _ = k_ref.shape
    hd = held.shape[-1]
    heads, key_heads = v_s.shape[0], k_s.shape[0]
    repeats = heads // key_heads
    copies = []
    for r in range(requests):
        copies.append(pltpu.make_async_copy(state_ref.at[r], held.at[r], in_sem.at[r]))
        copies[-1].start()
    spread_rows(k_ref, k_s, requests, steps)
    spread_rows(q_ref, q_s, requests, steps)
    spread_rows(v_ref, v_s, requests, steps)
    spread_rows(g_ref, g_s, requests, steps)
    sigmoid_rows(a_ref, a_s, requests, steps)
    sigmoid_rows(b_ref, b_s, requests, steps)
    top = ids_ref.shape[-1]
    place = lax.broadcasted_iota(jnp.int32, (steps, w_s.shape[-1]), 1)
    for r in range(requests):
        rows = slice(r * steps, (r + 1) * steps)
        r_s[rows, :] = res_ref[r].astype(F32)
        prob = prob_ref[r]
        prob = prob / row_sum(prob)
        weight = jnp.zeros(place.shape, F32)
        ids = ids_ref[r]
        for j in range(top):
            high = prob[:, j : j + 1].astype(BF16).astype(F32)
            weight = jnp.where(place == ids[:, j : j + 1], high, weight)
            weight = jnp.where(place == ids[:, j : j + 1] + experts, prob[:, j : j + 1] - high, weight)
        w_s[rows, :] = weight
    for r in range(requests):
        copies[r].wait()
        rows = slice(r * steps, (r + 1) * steps)
        for kh in range(key_heads):
            left = jnp.concatenate([k_s[kh, rows, :], q_s[kh, rows, :]], axis=0).astype(BF16)
            for h in range(kh * repeats, (kh + 1) * repeats):
                m_s[h, r * 2 * steps : (r + 1) * 2 * steps, :] = jnp.dot(
                    left, held[r, h * hd : (h + 1) * hd, :], preferred_element_type=F32
                )
    gain = gain_ref[...]

    def emit(t, h, o):
        gate = at_step(g_s, t, requests, steps, h)
        scaled = o * lax.rsqrt(row_sum(o * o) * (1.0 / hd) + EPS)
        o_s[h, pl.ds(t, requests, stride=steps), :] = scaled * gain * jax.nn.silu(gate)

    for kh in range(key_heads):
        recurrence(kh, repeats, steps, requests, hd, k_s, q_s, v_s, a_s, b_s, m_s, emit, None)
    width = heads * hd
    cols = res_ref.shape[-1] // lanes
    for h in range(heads):
        part = o_s[h].astype(BF16)
        for j in range(lanes):
            outs[j][:, h * hd : (h + 1) * hd] = part
    marks = w_s[...].astype(BF16)
    for j in range(lanes):
        start = pl.multiple_of((lane_ref[0] ^ j) * cols, cols)
        outs[j][:, width : width + cols] = r_s[:, pl.ds(start, cols)].astype(BF16)
        outs[j][:, width + cols :] = marks


def core_rows(
    lane, lanes, experts, states, query_rows, key_rows, value_rows, gate_rows, beta_logit, decay_logit,
    core_gain, residual, route_ids, route_prob,
):
    requests, heads, hd, _ = states.shape
    steps = key_rows.shape[1]
    kw, vw = key_rows.shape[-1], value_rows.shape[-1]
    tokens = requests * steps
    width = residual.shape[-1]
    weight_lanes = -(-2 * experts // 128) * 128
    vmem, hbm = pl.BlockSpec(memory_space=pltpu.VMEM), pl.BlockSpec(memory_space=pl.ANY)
    return pl.pallas_call(
        functools.partial(core_kernel, lanes, experts),
        in_specs=[pl.BlockSpec(memory_space=pltpu.SMEM), hbm] + [vmem] * 10,
        out_specs=[vmem] * lanes,
        out_shape=[jax.ShapeDtypeStruct((tokens, vw + width // lanes + weight_lanes), BF16)] * lanes,
        scratch_shapes=[
            pltpu.VMEM((kw // hd, tokens, hd), F32),
            pltpu.VMEM((kw // hd, tokens, hd), F32),
            pltpu.VMEM((heads, tokens, hd), F32),
            pltpu.VMEM((heads, tokens, hd), F32),
            pltpu.VMEM((tokens, 128), F32),
            pltpu.VMEM((tokens, 128), F32),
            pltpu.VMEM((heads, 2 * tokens, hd), F32),
            pltpu.VMEM((heads, tokens, hd), F32),
            pltpu.VMEM((tokens, width), F32),
            pltpu.VMEM((tokens, weight_lanes), F32),
            pltpu.VMEM((requests, heads * hd, hd), BF16),
            pltpu.SemaphoreType.DMA((requests,)),
        ],
        compiler_params=pltpu.CompilerParams(vmem_limit_bytes=60 * MIB),
        cost_estimate=pl.CostEstimate(flops=20_000_000, bytes_accessed=9 * MIB, transcendentals=100_000),
        name="core_rows",
    )(
        lane, states.reshape(requests, heads * hd, hd), query_rows, key_rows, value_rows, gate_rows,
        beta_logit, decay_logit, core_gain.reshape(1, hd), residual, route_ids, route_prob,
    )


def pack_kernel(lanes, key_heads, home_ref, lane_ref, state_ref, k_ref, v_ref, b_ref, a_ref, *rest):
    outs = rest[:-4]
    held, pay_f, in_sem, out_sem = rest[-4:]
    requests, steps, _ = k_ref.shape
    hd = held.shape[-1]
    heads = v_ref.shape[-1] // hd
    state_rows = heads * hd
    cap = requests // lanes
    copies = []
    for r in range(requests):
        source = state_ref.at[r]
        copies.append(pltpu.make_async_copy(source, held.at[r, pl.ds(0, state_rows)], in_sem.at[r]))
        copies[-1].start()
    target = [lax.rem(lax.div(home_ref[r], requests), lanes) ^ lane_ref[0] for r in range(requests)]
    ranks = [
        sum([(target[p] == target[r]).astype(jnp.int32) for p in range(r)], jnp.int32(0))
        for r in range(requests)
    ]
    pay_f[...] = jnp.zeros_like(pay_f)
    for r in range(requests):
        keys, vals = k_ref[r].astype(F32), v_ref[r].astype(F32)
        for kh in range(key_heads):
            pay_f[kh * steps : (kh + 1) * steps, :] = keys[:, kh * hd : (kh + 1) * hd]
        for h in range(heads):
            at = (key_heads + h) * steps
            pay_f[at : at + steps, :] = vals[:, h * hd : (h + 1) * hd]
        at = (key_heads + heads) * steps
        pay_f[at : at + steps, :heads] = a_ref[r].astype(F32)
        pay_f[at + steps : at + 2 * steps, :heads] = b_ref[r].astype(F32)
        place = lax.rem(home_ref[r], requests).astype(F32)
        pay_f[at + 2 * steps : at + 3 * steps, :] = jnp.full((steps, hd), place, F32)
        held[r, state_rows:, :] = pay_f[...].astype(BF16)
    for r in range(requests):
        copies[r].wait()
        for d in range(lanes):
            for q in range(cap if d > 1 else 1):
                dest = outs[d].at[ranks[r]] if d < 2 else outs[2 + (d - 2) * cap + q].at[0]
                chosen = (target[r] == d) & (ranks[r] == q) if d > 1 else target[r] == d

                @pl.when(chosen)
                def _():
                    pltpu.make_async_copy(held.at[r], dest, out_sem.at[r]).start()

    for r in range(requests):
        pltpu.make_async_copy(held.at[r], outs[0].at[0], out_sem.at[r]).wait()


def pack_states(home, lane, lanes, states, key_rows, value_rows, beta_logit, decay_logit):
    requests, heads, hd, _ = states.shape
    steps = key_rows.shape[1]
    key_heads = key_rows.shape[-1] // hd
    cap = requests // lanes
    _, pay_rows = packed_rows(key_heads, heads, steps)
    all_rows = heads * hd + pay_rows
    vmem, hbm = pl.BlockSpec(memory_space=pltpu.VMEM), pl.BlockSpec(memory_space=pl.ANY)
    smem = pl.BlockSpec(memory_space=pltpu.SMEM)
    sizes = [cap] * 2 + [1] * (cap * (lanes - 2))
    return pl.pallas_call(
        functools.partial(pack_kernel, lanes, key_heads),
        in_specs=[smem, smem, hbm] + [vmem] * 4,
        out_specs=[hbm] * len(sizes),
        out_shape=[jax.ShapeDtypeStruct((n, all_rows, hd), BF16) for n in sizes],
        scratch_shapes=[
            pltpu.VMEM((requests, all_rows, hd), BF16),
            pltpu.VMEM((pay_rows, hd), F32),
            pltpu.SemaphoreType.DMA((requests,)),
            pltpu.SemaphoreType.DMA((requests,)),
        ],
        compiler_params=pltpu.CompilerParams(vmem_limit_bytes=48 * MIB),
        cost_estimate=pl.CostEstimate(flops=0, bytes_accessed=9 * MIB, transcendentals=0),
        name="pack_states",
    )(home, lane, states.reshape(requests, heads * hd, hd), key_rows, value_rows, beta_logit, decay_logit)


def project_kernel(*refs):
    lanes = len(refs) - 3
    weight_ref, out_ref, marks_ref = refs[lanes:]
    depth, cols = weight_ref.shape
    rows = jnp.concatenate([refs[j][...] for j in range(lanes)], axis=0)
    attention = jnp.dot(rows[:, :depth], weight_ref[...], preferred_element_type=F32).astype(BF16)
    before = rows[:, depth : depth + cols].astype(F32)
    out_ref[...] = (before + attention.astype(F32)).astype(BF16)
    marks_ref[...] = rows[:, depth + cols :]


def project(got, out_weight):
    tokens, wide = got[0].shape
    depth, cols = out_weight.shape
    rows = tokens * len(got)
    vmem = pl.BlockSpec(memory_space=pltpu.VMEM)
    return pl.pallas_call(
        project_kernel,
        in_specs=[vmem] * (len(got) + 1),
        out_specs=[vmem] * 2,
        out_shape=[
            jax.ShapeDtypeStruct((rows, cols), BF16),
            jax.ShapeDtypeStruct((rows, wide - depth - cols), BF16),
        ],
        compiler_params=pltpu.CompilerParams(vmem_limit_bytes=24 * MIB),
        cost_estimate=pl.CostEstimate(
            flops=2 * rows * depth * cols, bytes_accessed=3 * MIB, transcendentals=0
        ),
        name="project",
    )(*got, out_weight)


def state_kernel(
    key_heads, heads, steps, count, *rest
):
    arrived = rest[:count]
    out_ref, k_s, v_s, a_s, b_s, m_s, u_s, c_s, held, pay_s, ready, in_sem, pay_sem, out_sem = rest[-14:]
    requests, state_rows, hd = held.shape
    origin = [(a, j) for a in arrived for j in range(a.shape[0])]
    repeats = heads // key_heads
    pays, copies = [], []
    for r in range(requests):
        pays.append(
            pltpu.make_async_copy(
                origin[r][0].at[origin[r][1], pl.ds(state_rows, pay_s.shape[1])], pay_s.at[r], pay_sem.at[r]
            )
        )
        pays[-1].start()
    for r in range(requests):
        copies.append(
            pltpu.make_async_copy(
                origin[r][0].at[origin[r][1], pl.ds(0, state_rows)], held.at[r], in_sem.at[r]
            )
        )
        copies[-1].start()
    places = []
    for r in range(requests):
        pays[r].wait()
        rows = slice(r * steps, (r + 1) * steps)
        pay = pay_s[r].astype(F32)
        for kh in range(key_heads):
            k_s[kh, rows, :] = pay[kh * steps : (kh + 1) * steps]
        for h in range(heads):
            v_s[h, rows, :] = pay[(key_heads + h) * steps : (key_heads + h + 1) * steps]
        at = (key_heads + heads) * steps
        a_s[rows, :] = jax.nn.sigmoid(pay[at : at + steps])
        b_s[rows, :] = jax.nn.sigmoid(pay[at + steps : at + 2 * steps])
        places.append(jnp.max(pay[at + 2 * steps : at + 3 * steps]).astype(jnp.int32))
    for r in range(requests):
        copies[r].wait()
        rows = slice(r * steps, (r + 1) * steps)
        for h in range(heads):
            m_s[h, rows, :] = jnp.dot(
                k_s[h // repeats, rows, :].astype(BF16),
                held[r, h * hd : (h + 1) * hd, :],
                preferred_element_type=F32,
            )

    def emit(h, c, updates):
        c_s[h] = jnp.broadcast_to(c, (requests, hd))
        for t, u in enumerate(updates):
            u_s[h, pl.ds(t, requests, stride=steps), :] = u

    for kh in range(key_heads):
        recurrence(kh, repeats, steps, requests, hd, k_s, None, v_s, a_s, b_s, m_s, None, emit)
    sent = []
    for r in range(requests):
        slot = r % 2
        if r >= 2:
            sent[r - 2].wait()
        rows = slice(r * steps, (r + 1) * steps)
        for h in range(heads):
            k4 = k_s[h // repeats, rows, :]
            k8 = jnp.concatenate([k4, k4], axis=0).astype(BF16)
            u4 = u_s[h, rows, :]
            high = u4.astype(BF16).astype(F32)
            u8 = jnp.concatenate([high, u4 - high], axis=0).astype(BF16)
            added = lax.dot_general(
                k8, u8, (((0,), (0,)), ((), ())), preferred_element_type=F32
            )
            kept = held[r, h * hd : (h + 1) * hd, :].astype(F32) * c_s[h, r : r + 1, :]
            ready[slot, h * hd : (h + 1) * hd, :] = (kept + added).astype(BF16)
        sent.append(pltpu.make_async_copy(ready.at[slot], out_ref.at[places[r]], out_sem.at[slot]))
        sent[-1].start()
    for c in sent[-2:]:
        c.wait()


def landed_states(arrived, before, total, key_heads, heads, steps):
    _, all_rows, hd = arrived[0].shape
    requests = sum(a.shape[0] for a in arrived)
    tokens = requests * steps
    state_rows = heads * hd
    hbm = pl.BlockSpec(memory_space=pl.ANY)
    out = pl.pallas_call(
        functools.partial(state_kernel, key_heads, heads, steps, len(arrived)),
        in_specs=[hbm] * (len(arrived) + len(before)),
        out_specs=hbm,
        out_shape=jax.ShapeDtypeStruct((total, state_rows, hd), BF16),
        input_output_aliases={len(arrived): 0} if before else {},
        scratch_shapes=[
            pltpu.VMEM((key_heads, tokens, hd), F32),
            pltpu.VMEM((heads, tokens, hd), F32),
            pltpu.VMEM((tokens, hd), F32),
            pltpu.VMEM((tokens, hd), F32),
            pltpu.VMEM((heads, tokens, hd), F32),
            pltpu.VMEM((heads, tokens, hd), F32),
            pltpu.VMEM((heads, requests, hd), F32),
            pltpu.VMEM((requests, state_rows, hd), BF16),
            pltpu.VMEM((requests, all_rows - state_rows, hd), BF16),
            pltpu.VMEM((2, state_rows, hd), BF16),
            pltpu.SemaphoreType.DMA((requests,)),
            pltpu.SemaphoreType.DMA((requests,)),
            pltpu.SemaphoreType.DMA((2,)),
        ],
        compiler_params=pltpu.CompilerParams(vmem_limit_bytes=32 * MIB),
        cost_estimate=pl.CostEstimate(flops=20_000_000, bytes_accessed=requests * MIB, transcendentals=10_000),
        name="landed_states",
    )(*arrived, *before)
    return out


def expert_kernel(sides, own_out, experts, where_ref, *rest):
    sources = rest[: 2 * sides]
    gain_ref, up_ref, down_ref = rest[2 * sides : 2 * sides + 3]
    keeps = rest[2 * sides + 3 : 3 * sides + 3]
    give_ref = rest[3 * sides + 3]
    pieces, result_s, sems = rest[-3 - 2 * sides + 1 : -2], rest[-2], rest[-1]
    copies = [pltpu.make_async_copy(a, b, sems.at[i]) for i, (a, b) in enumerate(zip(sources, pieces))]
    for c in copies:
        c.start()
    for c in copies:
        c.wait()
    group_rows = pieces[0].shape[0]
    cols = gain_ref.shape[-1]
    spans = give_ref.shape[1]
    tokens = give_ref.shape[2]
    width = down_ref.shape[-1]
    hidden_units = down_ref.shape[1]
    e = where_ref[0]
    blocks = [(x, c) for x in range(spans) for c in range(2)]
    values = {}
    for x, c in blocks:
        span = slice(x * cols, (x + 1) * cols)
        parts = [
            pieces[2 * y + c][(p ^ c) * tokens : ((p ^ c) + 1) * tokens, span]
            for y in range(sides)
            for p in range(2 * spans)
        ]
        values[x, c] = jnp.concatenate(parts, axis=0).astype(F32)
    total = sum(row_sum(values[b] * values[b]) for b in blocks)
    scale = lax.rsqrt(total * (1.0 / width) + EPS)
    joined = None
    for x, c in blocks:
        block = e ^ (2 * x + c)
        normed = (values[x, c] * scale * gain_ref[pl.ds(block, 1), :]).astype(BF16)
        up = up_ref[0, pl.ds(pl.multiple_of(block * cols, cols), cols), :]
        term = jnp.dot(normed, up, preferred_element_type=F32)
        joined = term if joined is None else joined + term
        if own_out:
            own = values[x, c][:tokens].astype(BF16)
            rest[3 * sides + 4][:, pl.ds(pl.multiple_of(block * cols, cols), cols)] = own
    active = (jax.nn.silu(joined[:, :hidden_units]) * joined[:, hidden_units:]).astype(BF16)
    result = jnp.dot(active, down_ref[0], preferred_element_type=F32).astype(BF16)
    marks = [pieces[2 * y][:, spans * cols :].astype(F32) for y in range(sides)]
    marks = jnp.concatenate(marks, axis=0)
    place = lax.broadcasted_iota(jnp.int32, marks.shape, 1)
    mine = (place == where_ref[1]) | (place == where_ref[1] + experts)
    weight = row_sum(jnp.where(mine, marks, 0.0))
    result_s[...] = (result.astype(F32) * weight).astype(BF16)
    for y in range(sides):
        for x in range(spans):
            for c in range(2):
                start = y * group_rows + (2 * x + c) * tokens
                rows = result_s[start : start + tokens, :]
                if c:
                    give_ref[y, x] = rows
                else:
                    keeps[y][x] = rows


def expert_chunk(where, pieces, gain, gate_up, down_weight, tokens, experts, own_out):
    sides = len(pieces) // 2
    spans, group_rows = gain.shape[0] // 2, pieces[0].shape[0]
    width = down_weight.shape[-1]
    vmem = pl.BlockSpec(memory_space=pltpu.VMEM)
    hbm = pl.BlockSpec(memory_space=pltpu.HBM)
    keep = jax.ShapeDtypeStruct((spans, tokens, width), BF16)
    give = jax.ShapeDtypeStruct((sides, spans, tokens, width), BF16)
    own = [jax.ShapeDtypeStruct((tokens, width), BF16)] if own_out else []
    rows = sides * group_rows
    outs = pl.pallas_call(
        functools.partial(expert_kernel, sides, own_out, experts),
        in_specs=[pl.BlockSpec(memory_space=pltpu.SMEM)] + [hbm] * len(pieces) + [vmem] * 3,
        out_specs=[vmem] * (sides + 1 + len(own)),
        out_shape=[keep] * sides + [give] + own,
        scratch_shapes=[pltpu.VMEM(p.shape, BF16) for p in pieces]
        + [pltpu.VMEM((rows, width), BF16), pltpu.SemaphoreType.DMA((len(pieces),))],
        compiler_params=pltpu.CompilerParams(vmem_limit_bytes=32 * MIB),
        cost_estimate=pl.CostEstimate(
            flops=6 * rows * width * down_weight.shape[1], bytes_accessed=6 * MIB, transcendentals=0
        ),
        name="expert_chunk",
    )(where, *pieces, gain, gate_up, down_weight)
    return outs


def swap(x, axis, d):
    size = lax.axis_size(axis)
    return lax.ppermute(x, axis, [(i, i ^ d) for i in range(size)])


def summed(*terms):
    return functools.reduce(lambda p, q: p + q, [t.astype(F32) for t in terms])


def shards(
    states, query_rows, key_rows, value_rows, gate_rows, beta_logit, decay_logit, residual,
    route_ids, route_prob, out_weight, core_gain, moe_gain, gate_up, down_weight, new_home,
):
    requests, heads, hd, _ = states.shape
    steps = query_rows.shape[1]
    width = residual.shape[-1]
    tokens = requests * steps
    lanes = lax.axis_size("ep")
    groups = lax.axis_size("dp")
    my_lane = lax.axis_index("ep")
    my_group = lax.axis_index("dp")
    kw, vw = key_rows.shape[-1], value_rows.shape[-1]
    top = route_ids.shape[-1]

    experts = groups * lanes
    cols = out_weight.shape[1]
    me = my_group * lanes + my_lane

    with jax.named_scope("core"):
        sent = core_rows(
            my_lane.reshape(1), lanes, experts, states, query_rows, key_rows, value_rows,
            gate_rows, beta_logit, decay_logit, core_gain, residual, route_ids, route_prob,
        )
        sent, new_home = lax.optimization_barrier((sent, new_home))
        got = {j: swap(sent[j], "ep", j) for j in range(lanes - 1, 0, -1)}
        got = [sent[0]] + [got[j] for j in range(1, lanes)]
    with jax.named_scope("send_states"):
        packed = pack_states(
            new_home, my_lane.reshape(1), lanes, states, key_rows, value_rows, beta_logit, decay_logit
        )
    with jax.named_scope("attention"):
        got, packed = lax.optimization_barrier((got, packed))
        hidden_cols, marks = project(got, out_weight)
        others = []
        for d in range(2, lanes, 2):
            other = swap(hidden_cols, "ep", d).reshape(lanes, tokens, cols)
            others.append(jnp.concatenate([other[j ^ d] for j in range(lanes)], axis=0))
        held = jnp.concatenate([hidden_cols] + others + [marks], axis=1)
        held, packed = lax.optimization_barrier((held, packed))
    with jax.named_scope("send_states"):
        cap = requests // lanes
        near_states = [packed[0], swap(packed[1], "ep", 1)]
        far_states = []
        for i, piece in enumerate(packed[2:]):
            if i:
                piece, far_states[-1] = lax.optimization_barrier((piece, far_states[-1]))
            far_states.append(swap(piece, "ep", 2 + i // cap))

    gain = moe_gain.reshape(lanes, cols)
    where = jnp.stack([my_lane, me])
    far = groups // 2
    chunks = [0] + [d for d in range(groups - 2, 0, -2) if d != far] + [far]
    tie = lax.optimization_barrier
    mid = chunks[1:-1]
    first, last = mid[0], mid[-1]
    across, keeps, asides, takens, backs, sums = {}, {}, {}, {}, {}, {}

    def expert(d):
        with jax.named_scope("experts"):
            pieces = [near[d], swap(near[d], "ep", 1), across[d], swap(across[d], "ep", 1)]
            outs = expert_chunk(where, pieces, gain, gate_up, down_weight, tokens, experts, d == 0)
            keeps[d] = outs[0]
        with jax.named_scope("way_back"):
            takens[d] = swap(outs[2], "ep", 1)
            asides[d] = summed(outs[1], takens[d][1]).astype(BF16)
        return outs[3:]

    def over(d):
        with jax.named_scope("tokens"):
            across[d] = swap(near[d], "dp", 1)

    def back(d):
        with jax.named_scope("way_back"):
            backs[d] = swap(asides[d], "dp", 1)

    def total(d):
        with jax.named_scope("way_back"):
            chunk = summed(keeps[d], takens[d][0], backs[d])
            sums[d] = chunk.astype(BF16) if d else chunk

    with jax.named_scope("tokens"):
        near = {d: swap(held, "dp", d) if d else held for d in [0] + mid}
    over(0)
    near, across = tie((near, across))
    with jax.named_scope("tokens"):
        half = near[0].shape[0] // 2
        upper = swap(near[0][:half], "dp", far)
        lower = swap(near[0][half:], "dp", far)
    for d in mid:
        over(d)
    near[0], upper = tie((near[0], upper))
    (own_rows,) = expert(0)
    for d in mid[:-1]:
        expert(d)
    with jax.named_scope("tokens"):
        near[far] = jnp.concatenate([upper, lower], axis=0)
    near[far], across[last], keeps, far_states[0] = tie((near[far], across[last], keeps, far_states[0]))
    over(far)
    if last not in keeps:
        expert(last)
    across[far], keeps, asides[first], far_states[1] = tie(
        (across[far], keeps, asides[first], far_states[1])
    )
    expert(far)
    back(first)
    asides[far], backs[first] = tie((asides[far], backs[first]))
    back(far)
    total(first)
    with jax.named_scope("way_back"):
        sums[first] = swap(sums[first], "dp", first)
    total(far)
    sums[far], sums[first] = tie((sums[far], sums[first]))
    for d in mid[1:] + [0]:
        back(d)
        total(d)
    with jax.named_scope("landed"):
        sizes = (requests, kw // hd, heads, steps)
        sums[far], arrived = tie((sums[far], near_states + far_states[:-2]))
        moved_out = landed_states(arrived, [], *sizes)
    with jax.named_scope("way_back"):
        sums = [swap(sums[d], "dp", d) if d not in (0, first) else sums[d] for d in chunks]
        sums, moved_out = tie((sums, moved_out))
    with jax.named_scope("landed"):
        moved_out = landed_states(far_states[-2:], [moved_out], *sizes)
        moved_out = moved_out.reshape(requests, heads, hd, hd)
    with jax.named_scope("mixed"):
        mixed = summed(own_rows, *[s[0] for s in sums])
        for x in range(1, lanes // 2):
            mixed = mixed + swap(summed(*[s[x] for s in sums]).astype(BF16), "ep", 2 * x).astype(F32)
        mixed_out = mixed.astype(BF16)
    return mixed_out.reshape(requests, steps, width), moved_out


def solution(mesh):
    row = P(("dp", "ep"), None, None)
    placed = (P(("dp", "ep"), None, None, None),) + (row,) * 9 + (
        P(None, "ep"), P(), P(), row, row, P(("dp", "ep")),
    )
    return jax.shard_map(
        shards,
        mesh=mesh,
        in_specs=placed,
        out_specs=(row, P(("dp", "ep"), None, None, None)),
        check_vma=False,
    )
```

```python
import functools

import jax
import jax.numpy as jnp
from jax import lax
from jax.experimental import pallas as pl
from jax.experimental.pallas import tpu as pltpu
from jax.sharding import PartitionSpec as P

EPS = 1e-06
F32 = jnp.float32
BF16 = jnp.bfloat16
MIB = 1 << 20


def row_sum(x):
    return jnp.sum(x, axis=-1, keepdims=True)


def spread_rows(ref, scratch, requests, steps):
    for r in range(requests):
        split_heads(ref[r].astype(F32), scratch, r, steps)


def split_heads(values, scratch, r, steps):
    hd = scratch.shape[-1]
    for h in range(scratch.shape[0]):
        scratch[h, r * steps : (r + 1) * steps, :] = values[:, h * hd : (h + 1) * hd]


def at_step(scratch, t, requests, steps, head=None):
    if head is None:
        return scratch[pl.ds(t, requests, stride=steps), :]
    return scratch[head, pl.ds(t, requests, stride=steps), :]


def recurrence(kh, repeats, steps, requests, hd, k_s, q_s, v_s, a_s, b_s, m_s, emit_out, emit_state):
    per = m_s.shape[1] // requests
    ks = [at_step(k_s, t, requests, steps, kh) for t in range(steps)]
    rk = [lax.rsqrt(row_sum(k * k) + EPS) for k in ks]
    kn = [k * r for k, r in zip(ks, rk)]
    kk = {(i, t): row_sum(kn[i] * kn[t]) for t in range(steps) for i in range(t)}
    if emit_out is not None:
        qs = [at_step(q_s, t, requests, steps, kh) for t in range(steps)]
        rq = [lax.rsqrt(row_sum(q * q) + EPS) * hd**-0.5 for q in qs]
        qn = [q * r for q, r in zip(qs, rq)]
        kq = {(i, t): row_sum(kn[i] * qn[t]) for t in range(steps) for i in range(t + 1)}
    for h in range(kh * repeats, (kh + 1) * repeats):
        decayed = []
        c = None
        for t in range(steps):
            a = at_step(a_s, t, requests, steps)[:, h : h + 1]
            b = at_step(b_s, t, requests, steps)[:, h : h + 1]
            decayed = [w * a for w in decayed]
            c = a if c is None else c * a
            m = (c * rk[t]) * at_step(m_s, t, requests, per, h)
            for i in range(t):
                m = m + kk[i, t] * decayed[i]
            decayed.append((at_step(v_s, t, requests, steps, h) - m) * b)
            if emit_out is not None:
                o = (c * rq[t]) * at_step(m_s, steps + t, requests, per, h)
                for i in range(t + 1):
                    o = o + kq[i, t] * decayed[i]
                emit_out(t, h, o)
        if emit_state is not None:
            emit_state(h, c, [w * r for w, r in zip(decayed, rk)])


def sigmoid_rows(ref, scratch, requests, steps):
    for r in range(requests):
        scratch[r * steps : (r + 1) * steps, : ref.shape[-1]] = jax.nn.sigmoid(ref[r].astype(F32))


def packed_rows(key_heads, heads, steps):
    used = (key_heads + heads + 3) * steps
    return used, -(-used // 16) * 16


def core_kernel(
    lanes, experts, lane_ref, state_ref, q_ref, k_ref, v_ref, g_ref, b_ref, a_ref, gain_ref,
    res_ref, ids_ref, prob_ref, *rest,
):
    outs = rest[:lanes]
    k_s, q_s, v_s, g_s, a_s, b_s, m_s, o_s, r_s, w_s, held, in_sem = rest[lanes:]
    requests, steps, _ = k_ref.shape
    hd = held.shape[-1]
    heads, key_heads = v_s.shape[0], k_s.shape[0]
    repeats = heads // key_heads
    copies = []
    for r in range(requests):
        copies.append(pltpu.make_async_copy(state_ref.at[r], held.at[r], in_sem.at[r]))
        copies[-1].start()
    spread_rows(k_ref, k_s, requests, steps)
    spread_rows(q_ref, q_s, requests, steps)
    spread_rows(v_ref, v_s, requests, steps)
    spread_rows(g_ref, g_s, requests, steps)
    sigmoid_rows(a_ref, a_s, requests, steps)
    sigmoid_rows(b_ref, b_s, requests, steps)
    top = ids_ref.shape[-1]
    place = lax.broadcasted_iota(jnp.int32, (steps, w_s.shape[-1]), 1)
    for r in range(requests):
        rows = slice(r * steps, (r + 1) * steps)
        r_s[rows, :] = res_ref[r].astype(F32)
        prob = prob_ref[r]
        prob = prob / row_sum(prob)
        weight = jnp.zeros(place.shape, F32)
        ids = ids_ref[r]
        for j in range(top):
            high = prob[:, j : j + 1].astype(BF16).astype(F32)
            weight = jnp.where(place == ids[:, j : j + 1], high, weight)
            weight = jnp.where(place == ids[:, j : j + 1] + experts, prob[:, j : j + 1] - high, weight)
        w_s[rows, :] = weight
    for r in range(requests):
        copies[r].wait()
        rows = slice(r * steps, (r + 1) * steps)
        for kh in range(key_heads):
            left = jnp.concatenate([k_s[kh, rows, :], q_s[kh, rows, :]], axis=0).astype(BF16)
            for h in range(kh * repeats, (kh + 1) * repeats):
                m_s[h, r * 2 * steps : (r + 1) * 2 * steps, :] = jnp.dot(
                    left, held[r, h * hd : (h + 1) * hd, :], preferred_element_type=F32
                )
    gain = gain_ref[...]

    def emit(t, h, o):
        gate = at_step(g_s, t, requests, steps, h)
        scaled = o * lax.rsqrt(row_sum(o * o) * (1.0 / hd) + EPS)
        o_s[h, pl.ds(t, requests, stride=steps), :] = scaled * gain * jax.nn.silu(gate)

    for kh in range(key_heads):
        recurrence(kh, repeats, steps, requests, hd, k_s, q_s, v_s, a_s, b_s, m_s, emit, None)
    width = heads * hd
    cols = res_ref.shape[-1] // lanes
    for h in range(heads):
        part = o_s[h].astype(BF16)
        for j in range(lanes):
            outs[j][:, h * hd : (h + 1) * hd] = part
    marks = w_s[...].astype(BF16)
    for j in range(lanes):
        start = pl.multiple_of((lane_ref[0] ^ j) * cols, cols)
        outs[j][:, width : width + cols] = r_s[:, pl.ds(start, cols)].astype(BF16)
        outs[j][:, width + cols :] = marks


def core_rows(
    lane, lanes, experts, states, query_rows, key_rows, value_rows, gate_rows, beta_logit, decay_logit,
    core_gain, residual, route_ids, route_prob,
):
    requests, heads, hd, _ = states.shape
    steps = key_rows.shape[1]
    kw, vw = key_rows.shape[-1], value_rows.shape[-1]
    tokens = requests * steps
    width = residual.shape[-1]
    weight_lanes = -(-2 * experts // 128) * 128
    vmem, hbm = pl.BlockSpec(memory_space=pltpu.VMEM), pl.BlockSpec(memory_space=pl.ANY)
    return pl.pallas_call(
        functools.partial(core_kernel, lanes, experts),
        in_specs=[pl.BlockSpec(memory_space=pltpu.SMEM), hbm] + [vmem] * 10,
        out_specs=[vmem] * lanes,
        out_shape=[jax.ShapeDtypeStruct((tokens, vw + width // lanes + weight_lanes), BF16)] * lanes,
        scratch_shapes=[
            pltpu.VMEM((kw // hd, tokens, hd), F32),
            pltpu.VMEM((kw // hd, tokens, hd), F32),
            pltpu.VMEM((heads, tokens, hd), F32),
            pltpu.VMEM((heads, tokens, hd), F32),
            pltpu.VMEM((tokens, 128), F32),
            pltpu.VMEM((tokens, 128), F32),
            pltpu.VMEM((heads, 2 * tokens, hd), F32),
            pltpu.VMEM((heads, tokens, hd), F32),
            pltpu.VMEM((tokens, width), F32),
            pltpu.VMEM((tokens, weight_lanes), F32),
            pltpu.VMEM((requests, heads * hd, hd), BF16),
            pltpu.SemaphoreType.DMA((requests,)),
        ],
        compiler_params=pltpu.CompilerParams(vmem_limit_bytes=60 * MIB),
        cost_estimate=pl.CostEstimate(flops=20_000_000, bytes_accessed=9 * MIB, transcendentals=100_000),
        name="core_rows",
    )(
        lane, states.reshape(requests, heads * hd, hd), query_rows, key_rows, value_rows, gate_rows,
        beta_logit, decay_logit, core_gain.reshape(1, hd), residual, route_ids, route_prob,
    )


def pack_kernel(lanes, key_heads, home_ref, lane_ref, state_ref, k_ref, v_ref, b_ref, a_ref, *rest):
    outs = rest[:-4]
    held, pay_f, in_sem, out_sem = rest[-4:]
    requests, steps, _ = k_ref.shape
    hd = held.shape[-1]
    heads = v_ref.shape[-1] // hd
    state_rows = heads * hd
    cap = requests // lanes
    copies = []
    for r in range(requests):
        source = state_ref.at[r]
        copies.append(pltpu.make_async_copy(source, held.at[r, pl.ds(0, state_rows)], in_sem.at[r]))
        copies[-1].start()
    target = [lax.rem(lax.div(home_ref[r], requests), lanes) ^ lane_ref[0] for r in range(requests)]
    ranks = [
        sum([(target[p] == target[r]).astype(jnp.int32) for p in range(r)], jnp.int32(0))
        for r in range(requests)
    ]
    pay_f[...] = jnp.zeros_like(pay_f)
    for r in range(requests):
        keys, vals = k_ref[r].astype(F32), v_ref[r].astype(F32)
        for kh in range(key_heads):
            pay_f[kh * steps : (kh + 1) * steps, :] = keys[:, kh * hd : (kh + 1) * hd]
        for h in range(heads):
            at = (key_heads + h) * steps
            pay_f[at : at + steps, :] = vals[:, h * hd : (h + 1) * hd]
        at = (key_heads + heads) * steps
        pay_f[at : at + steps, :heads] = a_ref[r].astype(F32)
        pay_f[at + steps : at + 2 * steps, :heads] = b_ref[r].astype(F32)
        place = lax.rem(home_ref[r], requests).astype(F32)
        pay_f[at + 2 * steps : at + 3 * steps, :] = jnp.full((steps, hd), place, F32)
        held[r, state_rows:, :] = pay_f[...].astype(BF16)
    for r in range(requests):
        copies[r].wait()
        for d in range(lanes):
            for q in range(cap if d > 1 else 1):
                dest = outs[d].at[ranks[r]] if d < 2 else outs[2 + (d - 2) * cap + q].at[0]
                chosen = (target[r] == d) & (ranks[r] == q) if d > 1 else target[r] == d

                @pl.when(chosen)
                def _():
                    pltpu.make_async_copy(held.at[r], dest, out_sem.at[r]).start()

    for r in range(requests):
        pltpu.make_async_copy(held.at[r], outs[0].at[0], out_sem.at[r]).wait()


def pack_states(home, lane, lanes, states, key_rows, value_rows, beta_logit, decay_logit):
    requests, heads, hd, _ = states.shape
    steps = key_rows.shape[1]
    key_heads = key_rows.shape[-1] // hd
    cap = requests // lanes
    _, pay_rows = packed_rows(key_heads, heads, steps)
    all_rows = heads * hd + pay_rows
    vmem, hbm = pl.BlockSpec(memory_space=pltpu.VMEM), pl.BlockSpec(memory_space=pl.ANY)
    smem = pl.BlockSpec(memory_space=pltpu.SMEM)
    sizes = [cap] * 2 + [1] * (cap * (lanes - 2))
    return pl.pallas_call(
        functools.partial(pack_kernel, lanes, key_heads),
        in_specs=[smem, smem, hbm] + [vmem] * 4,
        out_specs=[hbm] * len(sizes),
        out_shape=[jax.ShapeDtypeStruct((n, all_rows, hd), BF16) for n in sizes],
        scratch_shapes=[
            pltpu.VMEM((requests, all_rows, hd), BF16),
            pltpu.VMEM((pay_rows, hd), F32),
            pltpu.SemaphoreType.DMA((requests,)),
            pltpu.SemaphoreType.DMA((requests,)),
        ],
        compiler_params=pltpu.CompilerParams(vmem_limit_bytes=48 * MIB),
        cost_estimate=pl.CostEstimate(flops=0, bytes_accessed=9 * MIB, transcendentals=0),
        name="pack_states",
    )(home, lane, states.reshape(requests, heads * hd, hd), key_rows, value_rows, beta_logit, decay_logit)


def project_kernel(*refs):
    lanes = len(refs) - 3
    weight_ref, out_ref, marks_ref = refs[lanes:]
    depth, cols = weight_ref.shape
    rows = jnp.concatenate([refs[j][...] for j in range(lanes)], axis=0)
    attention = jnp.dot(rows[:, :depth], weight_ref[...], preferred_element_type=F32).astype(BF16)
    before = rows[:, depth : depth + cols].astype(F32)
    out_ref[...] = (before + attention.astype(F32)).astype(BF16)
    marks_ref[...] = rows[:, depth + cols :]


def project(got, out_weight):
    tokens, wide = got[0].shape
    depth, cols = out_weight.shape
    rows = tokens * len(got)
    vmem = pl.BlockSpec(memory_space=pltpu.VMEM)
    return pl.pallas_call(
        project_kernel,
        in_specs=[vmem] * (len(got) + 1),
        out_specs=[vmem] * 2,
        out_shape=[
            jax.ShapeDtypeStruct((rows, cols), BF16),
            jax.ShapeDtypeStruct((rows, wide - depth - cols), BF16),
        ],
        compiler_params=pltpu.CompilerParams(vmem_limit_bytes=24 * MIB),
        cost_estimate=pl.CostEstimate(
            flops=2 * rows * depth * cols, bytes_accessed=3 * MIB, transcendentals=0
        ),
        name="project",
    )(*got, out_weight)


def state_kernel(
    key_heads, heads, steps, count, *rest
):
    arrived = rest[:count]
    out_ref, k_s, v_s, a_s, b_s, m_s, u_s, c_s, held, pay_s, ready, in_sem, pay_sem, out_sem = rest[-14:]
    requests, state_rows, hd = held.shape
    origin = [(a, j) for a in arrived for j in range(a.shape[0])]
    repeats = heads // key_heads
    pays, copies = [], []
    for r in range(requests):
        pays.append(
            pltpu.make_async_copy(
                origin[r][0].at[origin[r][1], pl.ds(state_rows, pay_s.shape[1])], pay_s.at[r], pay_sem.at[r]
            )
        )
        pays[-1].start()
    for r in range(requests):
        copies.append(
            pltpu.make_async_copy(
                origin[r][0].at[origin[r][1], pl.ds(0, state_rows)], held.at[r], in_sem.at[r]
            )
        )
        copies[-1].start()
    places = []
    for r in range(requests):
        pays[r].wait()
        rows = slice(r * steps, (r + 1) * steps)
        pay = pay_s[r].astype(F32)
        for kh in range(key_heads):
            k_s[kh, rows, :] = pay[kh * steps : (kh + 1) * steps]
        for h in range(heads):
            v_s[h, rows, :] = pay[(key_heads + h) * steps : (key_heads + h + 1) * steps]
        at = (key_heads + heads) * steps
        a_s[rows, :] = jax.nn.sigmoid(pay[at : at + steps])
        b_s[rows, :] = jax.nn.sigmoid(pay[at + steps : at + 2 * steps])
        places.append(jnp.max(pay[at + 2 * steps : at + 3 * steps]).astype(jnp.int32))
    for r in range(requests):
        copies[r].wait()
        rows = slice(r * steps, (r + 1) * steps)
        for h in range(heads):
            m_s[h, rows, :] = jnp.dot(
                k_s[h // repeats, rows, :].astype(BF16),
                held[r, h * hd : (h + 1) * hd, :],
                preferred_element_type=F32,
            )

    def emit(h, c, updates):
        c_s[h] = jnp.broadcast_to(c, (requests, hd))
        for t, u in enumerate(updates):
            u_s[h, pl.ds(t, requests, stride=steps), :] = u

    for kh in range(key_heads):
        recurrence(kh, repeats, steps, requests, hd, k_s, None, v_s, a_s, b_s, m_s, None, emit)
    sent = []
    for r in range(requests):
        slot = r % 2
        if r >= 2:
            sent[r - 2].wait()
        rows = slice(r * steps, (r + 1) * steps)
        for h in range(heads):
            k4 = k_s[h // repeats, rows, :]
            k8 = jnp.concatenate([k4, k4], axis=0).astype(BF16)
            u4 = u_s[h, rows, :]
            high = u4.astype(BF16).astype(F32)
            u8 = jnp.concatenate([high, u4 - high], axis=0).astype(BF16)
            added = lax.dot_general(
                k8, u8, (((0,), (0,)), ((), ())), preferred_element_type=F32
            )
            kept = held[r, h * hd : (h + 1) * hd, :].astype(F32) * c_s[h, r : r + 1, :]
            ready[slot, h * hd : (h + 1) * hd, :] = (kept + added).astype(BF16)
        sent.append(pltpu.make_async_copy(ready.at[slot], out_ref.at[places[r]], out_sem.at[slot]))
        sent[-1].start()
    for c in sent[-2:]:
        c.wait()


def landed_states(arrived, before, total, key_heads, heads, steps):
    _, all_rows, hd = arrived[0].shape
    requests = sum(a.shape[0] for a in arrived)
    tokens = requests * steps
    state_rows = heads * hd
    hbm = pl.BlockSpec(memory_space=pl.ANY)
    out = pl.pallas_call(
        functools.partial(state_kernel, key_heads, heads, steps, len(arrived)),
        in_specs=[hbm] * (len(arrived) + len(before)),
        out_specs=hbm,
        out_shape=jax.ShapeDtypeStruct((total, state_rows, hd), BF16),
        input_output_aliases={len(arrived): 0} if before else {},
        scratch_shapes=[
            pltpu.VMEM((key_heads, tokens, hd), F32),
            pltpu.VMEM((heads, tokens, hd), F32),
            pltpu.VMEM((tokens, hd), F32),
            pltpu.VMEM((tokens, hd), F32),
            pltpu.VMEM((heads, tokens, hd), F32),
            pltpu.VMEM((heads, tokens, hd), F32),
            pltpu.VMEM((heads, requests, hd), F32),
            pltpu.VMEM((requests, state_rows, hd), BF16),
            pltpu.VMEM((requests, all_rows - state_rows, hd), BF16),
            pltpu.VMEM((2, state_rows, hd), BF16),
            pltpu.SemaphoreType.DMA((requests,)),
            pltpu.SemaphoreType.DMA((requests,)),
            pltpu.SemaphoreType.DMA((2,)),
        ],
        compiler_params=pltpu.CompilerParams(vmem_limit_bytes=32 * MIB),
        cost_estimate=pl.CostEstimate(flops=20_000_000, bytes_accessed=requests * MIB, transcendentals=10_000),
        name="landed_states",
    )(*arrived, *before)
    return out


def expert_kernel(sides, own_out, experts, where_ref, *rest):
    sources = rest[: 2 * sides]
    gain_ref, up_ref, down_ref = rest[2 * sides : 2 * sides + 3]
    keeps = rest[2 * sides + 3 : 3 * sides + 3]
    give_ref = rest[3 * sides + 3]
    pieces, result_s, sems = rest[-3 - 2 * sides + 1 : -2], rest[-2], rest[-1]
    copies = [pltpu.make_async_copy(a, b, sems.at[i]) for i, (a, b) in enumerate(zip(sources, pieces))]
    for c in copies:
        c.start()
    for c in copies:
        c.wait()
    group_rows = pieces[0].shape[0]
    cols = gain_ref.shape[-1]
    spans = give_ref.shape[1]
    tokens = give_ref.shape[2]
    width = down_ref.shape[-1]
    hidden_units = down_ref.shape[1]
    e = where_ref[0]
    blocks = [(x, c) for x in range(spans) for c in range(2)]
    values = {}
    for x, c in blocks:
        span = slice(x * cols, (x + 1) * cols)
        parts = [
            pieces[2 * y + c][(p ^ c) * tokens : ((p ^ c) + 1) * tokens, span]
            for y in range(sides)
            for p in range(2 * spans)
        ]
        values[x, c] = jnp.concatenate(parts, axis=0).astype(F32)
    total = sum(row_sum(values[b] * values[b]) for b in blocks)
    scale = lax.rsqrt(total * (1.0 / width) + EPS)
    joined = None
    for x, c in blocks:
        block = e ^ (2 * x + c)
        normed = (values[x, c] * scale * gain_ref[pl.ds(block, 1), :]).astype(BF16)
        up = up_ref[0, pl.ds(pl.multiple_of(block * cols, cols), cols), :]
        term = jnp.dot(normed, up, preferred_element_type=F32)
        joined = term if joined is None else joined + term
        if own_out:
            own = values[x, c][:tokens].astype(BF16)
            rest[3 * sides + 4][:, pl.ds(pl.multiple_of(block * cols, cols), cols)] = own
    active = (jax.nn.silu(joined[:, :hidden_units]) * joined[:, hidden_units:]).astype(BF16)
    result = jnp.dot(active, down_ref[0], preferred_element_type=F32).astype(BF16)
    marks = [pieces[2 * y][:, spans * cols :].astype(F32) for y in range(sides)]
    marks = jnp.concatenate(marks, axis=0)
    place = lax.broadcasted_iota(jnp.int32, marks.shape, 1)
    mine = (place == where_ref[1]) | (place == where_ref[1] + experts)
    weight = row_sum(jnp.where(mine, marks, 0.0))
    result_s[...] = (result.astype(F32) * weight).astype(BF16)
    for y in range(sides):
        for x in range(spans):
            for c in range(2):
                start = y * group_rows + (2 * x + c) * tokens
                rows = result_s[start : start + tokens, :]
                if c:
                    give_ref[y, x] = rows
                else:
                    keeps[y][x] = rows


def expert_chunk(where, pieces, gain, gate_up, down_weight, tokens, experts, own_out):
    sides = len(pieces) // 2
    spans, group_rows = gain.shape[0] // 2, pieces[0].shape[0]
    width = down_weight.shape[-1]
    vmem = pl.BlockSpec(memory_space=pltpu.VMEM)
    hbm = pl.BlockSpec(memory_space=pltpu.HBM)
    keep = jax.ShapeDtypeStruct((spans, tokens, width), BF16)
    give = jax.ShapeDtypeStruct((sides, spans, tokens, width), BF16)
    own = [jax.ShapeDtypeStruct((tokens, width), BF16)] if own_out else []
    rows = sides * group_rows
    outs = pl.pallas_call(
        functools.partial(expert_kernel, sides, own_out, experts),
        in_specs=[pl.BlockSpec(memory_space=pltpu.SMEM)] + [hbm] * len(pieces) + [vmem] * 3,
        out_specs=[vmem] * (sides + 1 + len(own)),
        out_shape=[keep] * sides + [give] + own,
        scratch_shapes=[pltpu.VMEM(p.shape, BF16) for p in pieces]
        + [pltpu.VMEM((rows, width), BF16), pltpu.SemaphoreType.DMA((len(pieces),))],
        compiler_params=pltpu.CompilerParams(vmem_limit_bytes=32 * MIB),
        cost_estimate=pl.CostEstimate(
            flops=6 * rows * width * down_weight.shape[1], bytes_accessed=6 * MIB, transcendentals=0
        ),
        name="expert_chunk",
    )(where, *pieces, gain, gate_up, down_weight)
    return outs


def swap(x, axis, d):
    size = lax.axis_size(axis)
    return lax.ppermute(x, axis, [(i, i ^ d) for i in range(size)])


def summed(*terms):
    return functools.reduce(lambda p, q: p + q, [t.astype(F32) for t in terms])


def shards(
    states, query_rows, key_rows, value_rows, gate_rows, beta_logit, decay_logit, residual,
    route_ids, route_prob, out_weight, core_gain, moe_gain, gate_up, down_weight, new_home,
):
    requests, heads, hd, _ = states.shape
    steps = query_rows.shape[1]
    width = residual.shape[-1]
    tokens = requests * steps
    lanes = lax.axis_size("ep")
    groups = lax.axis_size("dp")
    my_lane = lax.axis_index("ep")
    my_group = lax.axis_index("dp")
    kw, vw = key_rows.shape[-1], value_rows.shape[-1]
    top = route_ids.shape[-1]

    experts = groups * lanes
    cols = out_weight.shape[1]
    me = my_group * lanes + my_lane

    with jax.named_scope("core"):
        sent = core_rows(
            my_lane.reshape(1), lanes, experts, states, query_rows, key_rows, value_rows,
            gate_rows, beta_logit, decay_logit, core_gain, residual, route_ids, route_prob,
        )
        sent, new_home = lax.optimization_barrier((sent, new_home))
        got = {j: swap(sent[j], "ep", j) for j in range(lanes - 1, 0, -1)}
        got = [sent[0]] + [got[j] for j in range(1, lanes)]
    with jax.named_scope("send_states"):
        packed = pack_states(
            new_home, my_lane.reshape(1), lanes, states, key_rows, value_rows, beta_logit, decay_logit
        )
    with jax.named_scope("attention"):
        got, packed = lax.optimization_barrier((got, packed))
        hidden_cols, marks = project(got, out_weight)
        others = []
        for d in range(2, lanes, 2):
            other = swap(hidden_cols, "ep", d).reshape(lanes, tokens, cols)
            others.append(jnp.concatenate([other[j ^ d] for j in range(lanes)], axis=0))
        held = jnp.concatenate([hidden_cols] + others + [marks], axis=1)
        held, packed = lax.optimization_barrier((held, packed))
    with jax.named_scope("send_states"):
        cap = requests // lanes
        near_states = [packed[0], swap(packed[1], "ep", 1)]
        far_states = []
        for i, piece in enumerate(packed[2:]):
            if i:
                piece, far_states[-1] = lax.optimization_barrier((piece, far_states[-1]))
            far_states.append(swap(piece, "ep", 2 + i // cap))

    gain = moe_gain.reshape(lanes, cols)
    where = jnp.stack([my_lane, me])
    far = groups // 2
    chunks = [0] + [d for d in range(groups - 2, 0, -2) if d != far] + [far]
    tie = lax.optimization_barrier
    own_rows = None
    with jax.named_scope("tokens"):
        near = {d: swap(held, "dp", d) if d else held for d in chunks[:-1]}
        later, near[chunks[1]] = tie((held, near[chunks[1]]))
        across = {d: swap(near[d], "dp", 1) for d in chunks[:-1]}
        near[far] = swap(later, "dp", far)
        pieces = {}
        for d in chunks:
            aside = across.get(d)
            if d == far:
                near[d], pieces[chunks[-2]][2] = tie((near[d], pieces[chunks[-2]][2]))
                aside = swap(near[d], "dp", 1)
                last_across = aside
            else:
                pieces[d] = [near[d], swap(near[d], "ep", 1), aside, swap(aside, "ep", 1)]
        pieces[0], pieces[chunks[1]][2] = tie((pieces[0], pieces[chunks[1]][2]))
        pieces[0], far_states[0] = tie((pieces[0], far_states[0]))
    sums, keeps, parts = {}, {}, {}
    for d in chunks:
        if d == far:
            with jax.named_scope("tokens"):
                beside, keeps = tie((last_across, keeps))
                pieces[d] = [near[d], swap(near[d], "ep", 1), last_across, swap(beside, "ep", 1)]
                pieces[d], far_states[1] = tie((pieces[d], far_states[1]))
        with jax.named_scope("experts"):
            outs = expert_chunk(where, pieces[d], gain, gate_up, down_weight, tokens, experts, d == 0)
            keep_near, keep_across, give = outs[:3]
            if d == 0:
                own_rows = outs[3]
        with jax.named_scope("way_back"):
            taken = swap(give, "ep", 1)
            aside = summed(keep_across, taken[1]).astype(BF16)
            parts[d] = (taken, swap(aside, "dp", 1))
            keeps[d] = keep_near
    for d in chunks:
        with jax.named_scope("way_back"):
            taken, back = parts[d]
            chunk = summed(keeps[d], taken[0], back)
            sums[d] = chunk.astype(BF16) if d else chunk
    with jax.named_scope("landed"):
        sizes = (requests, kw // hd, heads, steps)
        sums[far], arrived = tie((sums[far], near_states + far_states[:-2]))
        moved_out = landed_states(arrived, [], *sizes)
    with jax.named_scope("way_back"):
        sums = [swap(sums[d], "dp", d) if d else sums[d] for d in chunks]
        sums, moved_out = tie((sums, moved_out))
    with jax.named_scope("landed"):
        moved_out = landed_states(far_states[-2:], [moved_out], *sizes)
        moved_out = moved_out.reshape(requests, heads, hd, hd)
    with jax.named_scope("mixed"):
        mixed = summed(own_rows, *[s[0] for s in sums])
        for x in range(1, lanes // 2):
            mixed = mixed + swap(summed(*[s[x] for s in sums]).astype(BF16), "ep", 2 * x).astype(F32)
        mixed_out = mixed.astype(BF16)
    return mixed_out.reshape(requests, steps, width), moved_out


def solution(mesh):
    row = P(("dp", "ep"), None, None)
    placed = (P(("dp", "ep"), None, None, None),) + (row,) * 9 + (
        P(None, "ep"), P(), P(), row, row, P(("dp", "ep")),
    )
    return jax.shard_map(
        shards,
        mesh=mesh,
        in_specs=placed,
        out_specs=(row, P(("dp", "ep"), None, None, None)),
        check_vma=False,
    )
```

```python
import functools

import jax
import jax.numpy as jnp
from jax import lax
from jax.experimental import pallas as pl
from jax.experimental.pallas import tpu as pltpu
from jax.sharding import PartitionSpec as P

EPS = 1e-06
F32 = jnp.float32
BF16 = jnp.bfloat16
MIB = 1 << 20


def row_sum(x):
    return jnp.sum(x, axis=-1, keepdims=True)


def spread_rows(ref, scratch, requests, steps):
    for r in range(requests):
        split_heads(ref[r].astype(F32), scratch, r, steps)


def split_heads(values, scratch, r, steps):
    hd = scratch.shape[-1]
    for h in range(scratch.shape[0]):
        scratch[h, r * steps : (r + 1) * steps, :] = values[:, h * hd : (h + 1) * hd]


def at_step(scratch, t, requests, steps, head=None):
    if head is None:
        return scratch[pl.ds(t, requests, stride=steps), :]
    return scratch[head, pl.ds(t, requests, stride=steps), :]


def recurrence(kh, repeats, steps, requests, hd, k_s, q_s, v_s, a_s, b_s, m_s, emit_out, emit_state):
    per = m_s.shape[1] // requests
    ks = [at_step(k_s, t, requests, steps, kh) for t in range(steps)]
    rk = [lax.rsqrt(row_sum(k * k) + EPS) for k in ks]
    kn = [k * r for k, r in zip(ks, rk)]
    kk = {(i, t): row_sum(kn[i] * kn[t]) for t in range(steps) for i in range(t)}
    if emit_out is not None:
        qs = [at_step(q_s, t, requests, steps, kh) for t in range(steps)]
        rq = [lax.rsqrt(row_sum(q * q) + EPS) * hd**-0.5 for q in qs]
        qn = [q * r for q, r in zip(qs, rq)]
        kq = {(i, t): row_sum(kn[i] * qn[t]) for t in range(steps) for i in range(t + 1)}
    for h in range(kh * repeats, (kh + 1) * repeats):
        decayed = []
        c = None
        for t in range(steps):
            a = at_step(a_s, t, requests, steps)[:, h : h + 1]
            b = at_step(b_s, t, requests, steps)[:, h : h + 1]
            decayed = [w * a for w in decayed]
            c = a if c is None else c * a
            m = (c * rk[t]) * at_step(m_s, t, requests, per, h)
            for i in range(t):
                m = m + kk[i, t] * decayed[i]
            decayed.append((at_step(v_s, t, requests, steps, h) - m) * b)
            if emit_out is not None:
                o = (c * rq[t]) * at_step(m_s, steps + t, requests, per, h)
                for i in range(t + 1):
                    o = o + kq[i, t] * decayed[i]
                emit_out(t, h, o)
        if emit_state is not None:
            emit_state(h, c, [w * r for w, r in zip(decayed, rk)])


def sigmoid_rows(ref, scratch, requests, steps):
    for r in range(requests):
        scratch[r * steps : (r + 1) * steps, : ref.shape[-1]] = jax.nn.sigmoid(ref[r].astype(F32))


def packed_rows(key_heads, heads, steps):
    used = (key_heads + heads + 3) * steps
    return used, -(-used // 16) * 16


def core_kernel(
    lanes, experts, lane_ref, state_ref, q_ref, k_ref, v_ref, g_ref, b_ref, a_ref, gain_ref,
    res_ref, ids_ref, prob_ref, *rest,
):
    outs = rest[:lanes]
    k_s, q_s, v_s, g_s, a_s, b_s, m_s, o_s, r_s, w_s, held, in_sem = rest[lanes:]
    requests, steps, _ = k_ref.shape
    hd = held.shape[-1]
    heads, key_heads = v_s.shape[0], k_s.shape[0]
    repeats = heads // key_heads
    copies = []
    for r in range(requests):
        copies.append(pltpu.make_async_copy(state_ref.at[r], held.at[r], in_sem.at[r]))
        copies[-1].start()
    spread_rows(k_ref, k_s, requests, steps)
    spread_rows(q_ref, q_s, requests, steps)
    spread_rows(v_ref, v_s, requests, steps)
    spread_rows(g_ref, g_s, requests, steps)
    sigmoid_rows(a_ref, a_s, requests, steps)
    sigmoid_rows(b_ref, b_s, requests, steps)
    top = ids_ref.shape[-1]
    place = lax.broadcasted_iota(jnp.int32, (steps, w_s.shape[-1]), 1)
    for r in range(requests):
        rows = slice(r * steps, (r + 1) * steps)
        r_s[rows, :] = res_ref[r].astype(F32)
        prob = prob_ref[r]
        prob = prob / row_sum(prob)
        weight = jnp.zeros(place.shape, F32)
        ids = ids_ref[r]
        for j in range(top):
            high = prob[:, j : j + 1].astype(BF16).astype(F32)
            weight = jnp.where(place == ids[:, j : j + 1], high, weight)
            weight = jnp.where(place == ids[:, j : j + 1] + experts, prob[:, j : j + 1] - high, weight)
        w_s[rows, :] = weight
    for r in range(requests):
        copies[r].wait()
        rows = slice(r * steps, (r + 1) * steps)
        for kh in range(key_heads):
            left = jnp.concatenate([k_s[kh, rows, :], q_s[kh, rows, :]], axis=0).astype(BF16)
            for h in range(kh * repeats, (kh + 1) * repeats):
                m_s[h, r * 2 * steps : (r + 1) * 2 * steps, :] = jnp.dot(
                    left, held[r, h * hd : (h + 1) * hd, :], preferred_element_type=F32
                )
    gain = gain_ref[...]

    def emit(t, h, o):
        gate = at_step(g_s, t, requests, steps, h)
        scaled = o * lax.rsqrt(row_sum(o * o) * (1.0 / hd) + EPS)
        o_s[h, pl.ds(t, requests, stride=steps), :] = scaled * gain * jax.nn.silu(gate)

    for kh in range(key_heads):
        recurrence(kh, repeats, steps, requests, hd, k_s, q_s, v_s, a_s, b_s, m_s, emit, None)
    width = heads * hd
    cols = res_ref.shape[-1] // lanes
    for h in range(heads):
        part = o_s[h].astype(BF16)
        for j in range(lanes):
            outs[j][:, h * hd : (h + 1) * hd] = part
    marks = w_s[...].astype(BF16)
    for j in range(lanes):
        start = pl.multiple_of((lane_ref[0] ^ j) * cols, cols)
        outs[j][:, width : width + cols] = r_s[:, pl.ds(start, cols)].astype(BF16)
        outs[j][:, width + cols :] = marks


def core_rows(
    lane, lanes, experts, states, query_rows, key_rows, value_rows, gate_rows, beta_logit, decay_logit,
    core_gain, residual, route_ids, route_prob,
):
    requests, heads, hd, _ = states.shape
    steps = key_rows.shape[1]
    kw, vw = key_rows.shape[-1], value_rows.shape[-1]
    tokens = requests * steps
    width = residual.shape[-1]
    weight_lanes = -(-2 * experts // 128) * 128
    vmem, hbm = pl.BlockSpec(memory_space=pltpu.VMEM), pl.BlockSpec(memory_space=pl.ANY)
    return pl.pallas_call(
        functools.partial(core_kernel, lanes, experts),
        in_specs=[pl.BlockSpec(memory_space=pltpu.SMEM), hbm] + [vmem] * 10,
        out_specs=[vmem] * lanes,
        out_shape=[jax.ShapeDtypeStruct((tokens, vw + width // lanes + weight_lanes), BF16)] * lanes,
        scratch_shapes=[
            pltpu.VMEM((kw // hd, tokens, hd), F32),
            pltpu.VMEM((kw // hd, tokens, hd), F32),
            pltpu.VMEM((heads, tokens, hd), F32),
            pltpu.VMEM((heads, tokens, hd), F32),
            pltpu.VMEM((tokens, 128), F32),
            pltpu.VMEM((tokens, 128), F32),
            pltpu.VMEM((heads, 2 * tokens, hd), F32),
            pltpu.VMEM((heads, tokens, hd), F32),
            pltpu.VMEM((tokens, width), F32),
            pltpu.VMEM((tokens, weight_lanes), F32),
            pltpu.VMEM((requests, heads * hd, hd), BF16),
            pltpu.SemaphoreType.DMA((requests,)),
        ],
        compiler_params=pltpu.CompilerParams(vmem_limit_bytes=60 * MIB),
        cost_estimate=pl.CostEstimate(flops=20_000_000, bytes_accessed=9 * MIB, transcendentals=100_000),
        name="core_rows",
    )(
        lane, states.reshape(requests, heads * hd, hd), query_rows, key_rows, value_rows, gate_rows,
        beta_logit, decay_logit, core_gain.reshape(1, hd), residual, route_ids, route_prob,
    )


def pack_kernel(lanes, key_heads, home_ref, lane_ref, state_ref, k_ref, v_ref, b_ref, a_ref, *rest):
    outs = rest[:-4]
    held, pay_f, in_sem, out_sem = rest[-4:]
    requests, steps, _ = k_ref.shape
    hd = held.shape[-1]
    heads = v_ref.shape[-1] // hd
    state_rows = heads * hd
    cap = requests // lanes
    copies = []
    for r in range(requests):
        source = state_ref.at[r]
        copies.append(pltpu.make_async_copy(source, held.at[r, pl.ds(0, state_rows)], in_sem.at[r]))
        copies[-1].start()
    target = [lax.rem(lax.div(home_ref[r], requests), lanes) ^ lane_ref[0] for r in range(requests)]
    ranks = [
        sum([(target[p] == target[r]).astype(jnp.int32) for p in range(r)], jnp.int32(0))
        for r in range(requests)
    ]
    pay_f[...] = jnp.zeros_like(pay_f)
    for r in range(requests):
        keys, vals = k_ref[r].astype(F32), v_ref[r].astype(F32)
        for kh in range(key_heads):
            pay_f[kh * steps : (kh + 1) * steps, :] = keys[:, kh * hd : (kh + 1) * hd]
        for h in range(heads):
            at = (key_heads + h) * steps
            pay_f[at : at + steps, :] = vals[:, h * hd : (h + 1) * hd]
        at = (key_heads + heads) * steps
        pay_f[at : at + steps, :heads] = a_ref[r].astype(F32)
        pay_f[at + steps : at + 2 * steps, :heads] = b_ref[r].astype(F32)
        place = lax.rem(home_ref[r], requests).astype(F32)
        pay_f[at + 2 * steps : at + 3 * steps, :] = jnp.full((steps, hd), place, F32)
        held[r, state_rows:, :] = pay_f[...].astype(BF16)
    for r in range(requests):
        copies[r].wait()
        for d in range(lanes):
            for q in range(cap if d > 1 else 1):
                dest = outs[d].at[ranks[r]] if d < 2 else outs[2 + (d - 2) * cap + q].at[0]
                chosen = (target[r] == d) & (ranks[r] == q) if d > 1 else target[r] == d

                @pl.when(chosen)
                def _():
                    pltpu.make_async_copy(held.at[r], dest, out_sem.at[r]).start()

    for r in range(requests):
        pltpu.make_async_copy(held.at[r], outs[0].at[0], out_sem.at[r]).wait()


def pack_states(home, lane, lanes, states, key_rows, value_rows, beta_logit, decay_logit):
    requests, heads, hd, _ = states.shape
    steps = key_rows.shape[1]
    key_heads = key_rows.shape[-1] // hd
    cap = requests // lanes
    _, pay_rows = packed_rows(key_heads, heads, steps)
    all_rows = heads * hd + pay_rows
    vmem, hbm = pl.BlockSpec(memory_space=pltpu.VMEM), pl.BlockSpec(memory_space=pl.ANY)
    smem = pl.BlockSpec(memory_space=pltpu.SMEM)
    sizes = [cap] * 2 + [1] * (cap * (lanes - 2))
    return pl.pallas_call(
        functools.partial(pack_kernel, lanes, key_heads),
        in_specs=[smem, smem, hbm] + [vmem] * 4,
        out_specs=[hbm] * len(sizes),
        out_shape=[jax.ShapeDtypeStruct((n, all_rows, hd), BF16) for n in sizes],
        scratch_shapes=[
            pltpu.VMEM((requests, all_rows, hd), BF16),
            pltpu.VMEM((pay_rows, hd), F32),
            pltpu.SemaphoreType.DMA((requests,)),
            pltpu.SemaphoreType.DMA((requests,)),
        ],
        compiler_params=pltpu.CompilerParams(vmem_limit_bytes=48 * MIB),
        cost_estimate=pl.CostEstimate(flops=0, bytes_accessed=9 * MIB, transcendentals=0),
        name="pack_states",
    )(home, lane, states.reshape(requests, heads * hd, hd), key_rows, value_rows, beta_logit, decay_logit)


def project_kernel(*refs):
    lanes = len(refs) - 3
    weight_ref, out_ref, marks_ref = refs[lanes:]
    depth, cols = weight_ref.shape
    rows = jnp.concatenate([refs[j][...] for j in range(lanes)], axis=0)
    attention = jnp.dot(rows[:, :depth], weight_ref[...], preferred_element_type=F32).astype(BF16)
    before = rows[:, depth : depth + cols].astype(F32)
    out_ref[...] = (before + attention.astype(F32)).astype(BF16)
    marks_ref[...] = rows[:, depth + cols :]


def project(got, out_weight):
    tokens, wide = got[0].shape
    depth, cols = out_weight.shape
    rows = tokens * len(got)
    vmem = pl.BlockSpec(memory_space=pltpu.VMEM)
    return pl.pallas_call(
        project_kernel,
        in_specs=[vmem] * (len(got) + 1),
        out_specs=[vmem] * 2,
        out_shape=[
            jax.ShapeDtypeStruct((rows, cols), BF16),
            jax.ShapeDtypeStruct((rows, wide - depth - cols), BF16),
        ],
        compiler_params=pltpu.CompilerParams(vmem_limit_bytes=24 * MIB),
        cost_estimate=pl.CostEstimate(
            flops=2 * rows * depth * cols, bytes_accessed=3 * MIB, transcendentals=0
        ),
        name="project",
    )(*got, out_weight)


def state_kernel(
    key_heads, heads, steps, count, *rest
):
    arrived = rest[:count]
    out_ref, k_s, v_s, a_s, b_s, m_s, u_s, c_s, held, pay_s, ready, in_sem, pay_sem, out_sem = rest[-14:]
    requests, state_rows, hd = held.shape
    origin = [(a, j) for a in arrived for j in range(a.shape[0])]
    repeats = heads // key_heads
    pays, copies = [], []
    for r in range(requests):
        pays.append(
            pltpu.make_async_copy(
                origin[r][0].at[origin[r][1], pl.ds(state_rows, pay_s.shape[1])], pay_s.at[r], pay_sem.at[r]
            )
        )
        pays[-1].start()
    for r in range(requests):
        copies.append(
            pltpu.make_async_copy(
                origin[r][0].at[origin[r][1], pl.ds(0, state_rows)], held.at[r], in_sem.at[r]
            )
        )
        copies[-1].start()
    places = []
    for r in range(requests):
        pays[r].wait()
        rows = slice(r * steps, (r + 1) * steps)
        pay = pay_s[r].astype(F32)
        for kh in range(key_heads):
            k_s[kh, rows, :] = pay[kh * steps : (kh + 1) * steps]
        for h in range(heads):
            v_s[h, rows, :] = pay[(key_heads + h) * steps : (key_heads + h + 1) * steps]
        at = (key_heads + heads) * steps
        a_s[rows, :] = jax.nn.sigmoid(pay[at : at + steps])
        b_s[rows, :] = jax.nn.sigmoid(pay[at + steps : at + 2 * steps])
        places.append(jnp.max(pay[at + 2 * steps : at + 3 * steps]).astype(jnp.int32))
    for r in range(requests):
        copies[r].wait()
        rows = slice(r * steps, (r + 1) * steps)
        for h in range(heads):
            m_s[h, rows, :] = jnp.dot(
                k_s[h // repeats, rows, :].astype(BF16),
                held[r, h * hd : (h + 1) * hd, :],
                preferred_element_type=F32,
            )

    def emit(h, c, updates):
        c_s[h] = jnp.broadcast_to(c, (requests, hd))
        for t, u in enumerate(updates):
            u_s[h, pl.ds(t, requests, stride=steps), :] = u

    for kh in range(key_heads):
        recurrence(kh, repeats, steps, requests, hd, k_s, None, v_s, a_s, b_s, m_s, None, emit)
    sent = []
    for r in range(requests):
        slot = r % 2
        if r >= 2:
            sent[r - 2].wait()
        rows = slice(r * steps, (r + 1) * steps)
        for h in range(heads):
            k4 = k_s[h // repeats, rows, :]
            k8 = jnp.concatenate([k4, k4], axis=0).astype(BF16)
            u4 = u_s[h, rows, :]
            high = u4.astype(BF16).astype(F32)
            u8 = jnp.concatenate([high, u4 - high], axis=0).astype(BF16)
            added = lax.dot_general(
                k8, u8, (((0,), (0,)), ((), ())), preferred_element_type=F32
            )
            kept = held[r, h * hd : (h + 1) * hd, :].astype(F32) * c_s[h, r : r + 1, :]
            ready[slot, h * hd : (h + 1) * hd, :] = (kept + added).astype(BF16)
        sent.append(pltpu.make_async_copy(ready.at[slot], out_ref.at[places[r]], out_sem.at[slot]))
        sent[-1].start()
    for c in sent[-2:]:
        c.wait()


def landed_states(arrived, before, total, key_heads, heads, steps):
    _, all_rows, hd = arrived[0].shape
    requests = sum(a.shape[0] for a in arrived)
    tokens = requests * steps
    state_rows = heads * hd
    hbm = pl.BlockSpec(memory_space=pl.ANY)
    out = pl.pallas_call(
        functools.partial(state_kernel, key_heads, heads, steps, len(arrived)),
        in_specs=[hbm] * (len(arrived) + len(before)),
        out_specs=hbm,
        out_shape=jax.ShapeDtypeStruct((total, state_rows, hd), BF16),
        input_output_aliases={len(arrived): 0} if before else {},
        scratch_shapes=[
            pltpu.VMEM((key_heads, tokens, hd), F32),
            pltpu.VMEM((heads, tokens, hd), F32),
            pltpu.VMEM((tokens, hd), F32),
            pltpu.VMEM((tokens, hd), F32),
            pltpu.VMEM((heads, tokens, hd), F32),
            pltpu.VMEM((heads, tokens, hd), F32),
            pltpu.VMEM((heads, requests, hd), F32),
            pltpu.VMEM((requests, state_rows, hd), BF16),
            pltpu.VMEM((requests, all_rows - state_rows, hd), BF16),
            pltpu.VMEM((2, state_rows, hd), BF16),
            pltpu.SemaphoreType.DMA((requests,)),
            pltpu.SemaphoreType.DMA((requests,)),
            pltpu.SemaphoreType.DMA((2,)),
        ],
        compiler_params=pltpu.CompilerParams(vmem_limit_bytes=32 * MIB),
        cost_estimate=pl.CostEstimate(flops=20_000_000, bytes_accessed=requests * MIB, transcendentals=10_000),
        name="landed_states",
    )(*arrived, *before)
    return out


def expert_kernel(sides, own_out, experts, where_ref, *rest):
    sources = rest[: 2 * sides]
    gain_ref, up_ref, down_ref = rest[2 * sides : 2 * sides + 3]
    keeps = rest[2 * sides + 3 : 3 * sides + 3]
    give_ref = rest[3 * sides + 3]
    pieces, result_s, sems = rest[-3 - 2 * sides + 1 : -2], rest[-2], rest[-1]
    copies = [pltpu.make_async_copy(a, b, sems.at[i]) for i, (a, b) in enumerate(zip(sources, pieces))]
    for c in copies:
        c.start()
    for c in copies:
        c.wait()
    group_rows = pieces[0].shape[0]
    cols = gain_ref.shape[-1]
    spans = give_ref.shape[1]
    tokens = give_ref.shape[2]
    width = down_ref.shape[-1]
    hidden_units = down_ref.shape[1]
    e = where_ref[0]
    blocks = [(x, c) for x in range(spans) for c in range(2)]
    values = {}
    for x, c in blocks:
        span = slice(x * cols, (x + 1) * cols)
        parts = [
            pieces[2 * y + c][(p ^ c) * tokens : ((p ^ c) + 1) * tokens, span]
            for y in range(sides)
            for p in range(2 * spans)
        ]
        values[x, c] = jnp.concatenate(parts, axis=0).astype(F32)
    total = sum(row_sum(values[b] * values[b]) for b in blocks)
    scale = lax.rsqrt(total * (1.0 / width) + EPS)
    joined = None
    for x, c in blocks:
        block = e ^ (2 * x + c)
        normed = (values[x, c] * scale * gain_ref[pl.ds(block, 1), :]).astype(BF16)
        up = up_ref[0, pl.ds(pl.multiple_of(block * cols, cols), cols), :]
        term = jnp.dot(normed, up, preferred_element_type=F32)
        joined = term if joined is None else joined + term
        if own_out:
            own = values[x, c][:tokens].astype(BF16)
            rest[3 * sides + 4][:, pl.ds(pl.multiple_of(block * cols, cols), cols)] = own
    active = (jax.nn.silu(joined[:, :hidden_units]) * joined[:, hidden_units:]).astype(BF16)
    result = jnp.dot(active, down_ref[0], preferred_element_type=F32).astype(BF16)
    marks = [pieces[2 * y][:, spans * cols :].astype(F32) for y in range(sides)]
    marks = jnp.concatenate(marks, axis=0)
    place = lax.broadcasted_iota(jnp.int32, marks.shape, 1)
    mine = (place == where_ref[1]) | (place == where_ref[1] + experts)
    weight = row_sum(jnp.where(mine, marks, 0.0))
    result_s[...] = (result.astype(F32) * weight).astype(BF16)
    for y in range(sides):
        for x in range(spans):
            for c in range(2):
                start = y * group_rows + (2 * x + c) * tokens
                rows = result_s[start : start + tokens, :]
                if c:
                    give_ref[y, x] = rows
                else:
                    keeps[y][x] = rows


def expert_chunk(where, pieces, gain, gate_up, down_weight, tokens, experts, own_out):
    sides = len(pieces) // 2
    spans, group_rows = gain.shape[0] // 2, pieces[0].shape[0]
    width = down_weight.shape[-1]
    vmem = pl.BlockSpec(memory_space=pltpu.VMEM)
    hbm = pl.BlockSpec(memory_space=pltpu.HBM)
    keep = jax.ShapeDtypeStruct((spans, tokens, width), BF16)
    give = jax.ShapeDtypeStruct((sides, spans, tokens, width), BF16)
    own = [jax.ShapeDtypeStruct((tokens, width), BF16)] if own_out else []
    rows = sides * group_rows
    outs = pl.pallas_call(
        functools.partial(expert_kernel, sides, own_out, experts),
        in_specs=[pl.BlockSpec(memory_space=pltpu.SMEM)] + [hbm] * len(pieces) + [vmem] * 3,
        out_specs=[vmem] * (sides + 1 + len(own)),
        out_shape=[keep] * sides + [give] + own,
        scratch_shapes=[pltpu.VMEM(p.shape, BF16) for p in pieces]
        + [pltpu.VMEM((rows, width), BF16), pltpu.SemaphoreType.DMA((len(pieces),))],
        compiler_params=pltpu.CompilerParams(vmem_limit_bytes=32 * MIB),
        cost_estimate=pl.CostEstimate(
            flops=6 * rows * width * down_weight.shape[1], bytes_accessed=6 * MIB, transcendentals=0
        ),
        name="expert_chunk",
    )(where, *pieces, gain, gate_up, down_weight)
    return outs


def swap(x, axis, d):
    size = lax.axis_size(axis)
    return lax.ppermute(x, axis, [(i, i ^ d) for i in range(size)])


def summed(*terms):
    return functools.reduce(lambda p, q: p + q, [t.astype(F32) for t in terms])


def shards(
    states, query_rows, key_rows, value_rows, gate_rows, beta_logit, decay_logit, residual,
    route_ids, route_prob, out_weight, core_gain, moe_gain, gate_up, down_weight, new_home,
):
    requests, heads, hd, _ = states.shape
    steps = query_rows.shape[1]
    width = residual.shape[-1]
    tokens = requests * steps
    lanes = lax.axis_size("ep")
    groups = lax.axis_size("dp")
    my_lane = lax.axis_index("ep")
    my_group = lax.axis_index("dp")
    kw, vw = key_rows.shape[-1], value_rows.shape[-1]
    top = route_ids.shape[-1]

    experts = groups * lanes
    cols = out_weight.shape[1]
    me = my_group * lanes + my_lane

    with jax.named_scope("core"):
        sent = core_rows(
            my_lane.reshape(1), lanes, experts, states, query_rows, key_rows, value_rows,
            gate_rows, beta_logit, decay_logit, core_gain, residual, route_ids, route_prob,
        )
        sent, new_home = lax.optimization_barrier((sent, new_home))
        got = {j: swap(sent[j], "ep", j) for j in range(lanes - 1, 0, -1)}
        got = [sent[0]] + [got[j] for j in range(1, lanes)]
    with jax.named_scope("send_states"):
        packed = pack_states(
            new_home, my_lane.reshape(1), lanes, states, key_rows, value_rows, beta_logit, decay_logit
        )
    with jax.named_scope("attention"):
        got, packed = lax.optimization_barrier((got, packed))
        hidden_cols, marks = project(got, out_weight)
        others = []
        for d in range(2, lanes, 2):
            other = swap(hidden_cols, "ep", d).reshape(lanes, tokens, cols)
            others.append(jnp.concatenate([other[j ^ d] for j in range(lanes)], axis=0))
        held = jnp.concatenate([hidden_cols] + others + [marks], axis=1)
        held, packed = lax.optimization_barrier((held, packed))
    with jax.named_scope("send_states"):
        cap = requests // lanes
        near_states = [packed[0], swap(packed[1], "ep", 1)]
        first_across = swap(held, "dp", 1)
        packed = list(packed)
        packed[2], first_across = lax.optimization_barrier((packed[2], first_across))
        far_states = []
        for i, piece in enumerate(packed[2:]):
            if i:
                piece, far_states[-1] = lax.optimization_barrier((piece, far_states[-1]))
            far_states.append(swap(piece, "ep", 2 + i // cap))

    gain = moe_gain.reshape(lanes, cols)
    where = jnp.stack([my_lane, me])
    far = groups // 2
    chunks = [0] + [d for d in range(groups - 2, 0, -2) if d != far] + [far]
    tie = lax.optimization_barrier
    own_rows = None
    with jax.named_scope("tokens"):
        near = {d: swap(held, "dp", d) if d else held for d in chunks[:-1]}
        later, near[chunks[1]] = tie((held, near[chunks[1]]))
        across = {d: swap(near[d], "dp", 1) if d else first_across for d in chunks[:-1]}
        near[far] = swap(later, "dp", far)
        pieces = {}
        for d in chunks:
            aside = across.get(d)
            if d == far:
                near[d], pieces[chunks[-2]][2] = tie((near[d], pieces[chunks[-2]][2]))
                aside = swap(near[d], "dp", 1)
                last_across = aside
            else:
                pieces[d] = [near[d], swap(near[d], "ep", 1), aside, swap(aside, "ep", 1)]
        pieces[0], pieces[chunks[1]][2] = tie((pieces[0], pieces[chunks[1]][2]))
        pieces[0], far_states[0] = tie((pieces[0], far_states[0]))
    sums, keeps, parts, asides = {}, {}, {}, {}
    for d in chunks:
        if d == far:
            with jax.named_scope("tokens"):
                beside, keeps = tie((last_across, keeps))
                pieces[d] = [near[d], swap(near[d], "ep", 1), last_across, swap(beside, "ep", 1)]
                pieces[d], far_states[1], asides[chunks[1]] = tie(
                    (pieces[d], far_states[1], asides[chunks[1]])
                )
        with jax.named_scope("experts"):
            outs = expert_chunk(where, pieces[d], gain, gate_up, down_weight, tokens, experts, d == 0)
            keep_near, keep_across, give = outs[:3]
            if d == 0:
                own_rows = outs[3]
        with jax.named_scope("way_back"):
            taken = swap(give, "ep", 1)
            aside = summed(keep_across, taken[1]).astype(BF16)
            parts[d], asides[d] = taken, aside
            keeps[d] = keep_near
    for d in [far, chunks[1], 0] + chunks[2:-1]:
        with jax.named_scope("way_back"):
            back = swap(asides[d], "dp", 1)
            if d == far:
                others = {p: asides[p] for p in chunks if p not in (far, chunks[1])}
                others, back = tie((others, back))
                asides.update(others)
            chunk = summed(keeps[d], parts[d][0], back)
            sums[d] = chunk.astype(BF16) if d else chunk
    with jax.named_scope("landed"):
        sizes = (requests, kw // hd, heads, steps)
        sums[far], arrived = tie((sums[far], near_states + far_states[:-2]))
        sums[chunks[-2]], arrived = tie((sums[chunks[-2]], arrived))
        moved_out = landed_states(arrived, [], *sizes)
    with jax.named_scope("way_back"):
        sums = [swap(sums[d], "dp", d) if d else sums[d] for d in chunks]
        sums, moved_out = tie((sums, moved_out))
    with jax.named_scope("landed"):
        moved_out = landed_states(far_states[-2:], [moved_out], *sizes)
        moved_out = moved_out.reshape(requests, heads, hd, hd)
    with jax.named_scope("mixed"):
        mixed = summed(own_rows, *[s[0] for s in sums])
        for x in range(1, lanes // 2):
            mixed = mixed + swap(summed(*[s[x] for s in sums]).astype(BF16), "ep", 2 * x).astype(F32)
        mixed_out = mixed.astype(BF16)
    return mixed_out.reshape(requests, steps, width), moved_out


def solution(mesh):
    row = P(("dp", "ep"), None, None)
    placed = (P(("dp", "ep"), None, None, None),) + (row,) * 9 + (
        P(None, "ep"), P(), P(), row, row, P(("dp", "ep")),
    )
    return jax.shard_map(
        shards,
        mesh=mesh,
        in_specs=placed,
        out_specs=(row, P(("dp", "ep"), None, None, None)),
        check_vma=False,
    )
```

```python
import functools

import jax
import jax.numpy as jnp
from jax import lax
from jax.experimental import pallas as pl
from jax.experimental.pallas import tpu as pltpu
from jax.sharding import PartitionSpec as P

EPS = 1e-06
F32 = jnp.float32
BF16 = jnp.bfloat16
MIB = 1 << 20


def row_sum(x):
    return jnp.sum(x, axis=-1, keepdims=True)


def spread_rows(ref, scratch, requests, steps):
    for r in range(requests):
        split_heads(ref[r].astype(F32), scratch, r, steps)


def split_heads(values, scratch, r, steps):
    hd = scratch.shape[-1]
    for h in range(scratch.shape[0]):
        scratch[h, r * steps : (r + 1) * steps, :] = values[:, h * hd : (h + 1) * hd]


def at_step(scratch, t, requests, steps, head=None):
    if head is None:
        return scratch[pl.ds(t, requests, stride=steps), :]
    return scratch[head, pl.ds(t, requests, stride=steps), :]


def recurrence(kh, repeats, steps, requests, hd, k_s, q_s, v_s, a_s, b_s, m_s, emit_out, emit_state):
    per = m_s.shape[1] // requests
    ks = [at_step(k_s, t, requests, steps, kh) for t in range(steps)]
    rk = [lax.rsqrt(row_sum(k * k) + EPS) for k in ks]
    kn = [k * r for k, r in zip(ks, rk)]
    kk = {(i, t): row_sum(kn[i] * kn[t]) for t in range(steps) for i in range(t)}
    if emit_out is not None:
        qs = [at_step(q_s, t, requests, steps, kh) for t in range(steps)]
        rq = [lax.rsqrt(row_sum(q * q) + EPS) * hd**-0.5 for q in qs]
        qn = [q * r for q, r in zip(qs, rq)]
        kq = {(i, t): row_sum(kn[i] * qn[t]) for t in range(steps) for i in range(t + 1)}
    for h in range(kh * repeats, (kh + 1) * repeats):
        decayed = []
        c = None
        for t in range(steps):
            a = at_step(a_s, t, requests, steps)[:, h : h + 1]
            b = at_step(b_s, t, requests, steps)[:, h : h + 1]
            decayed = [w * a for w in decayed]
            c = a if c is None else c * a
            m = (c * rk[t]) * at_step(m_s, t, requests, per, h)
            for i in range(t):
                m = m + kk[i, t] * decayed[i]
            decayed.append((at_step(v_s, t, requests, steps, h) - m) * b)
            if emit_out is not None:
                o = (c * rq[t]) * at_step(m_s, steps + t, requests, per, h)
                for i in range(t + 1):
                    o = o + kq[i, t] * decayed[i]
                emit_out(t, h, o)
        if emit_state is not None:
            emit_state(h, c, [w * r for w, r in zip(decayed, rk)])


def sigmoid_rows(ref, scratch, requests, steps):
    for r in range(requests):
        scratch[r * steps : (r + 1) * steps, : ref.shape[-1]] = jax.nn.sigmoid(ref[r].astype(F32))


def packed_rows(key_heads, heads, steps):
    used = (key_heads + heads + 3) * steps
    return used, -(-used // 16) * 16


def core_kernel(
    lanes, experts, lane_ref, state_ref, q_ref, k_ref, v_ref, g_ref, b_ref, a_ref, gain_ref,
    res_ref, ids_ref, prob_ref, *rest,
):
    outs = rest[:lanes]
    k_s, q_s, v_s, g_s, a_s, b_s, m_s, o_s, r_s, w_s, held, in_sem = rest[lanes:]
    requests, steps, _ = k_ref.shape
    hd = held.shape[-1]
    heads, key_heads = v_s.shape[0], k_s.shape[0]
    repeats = heads // key_heads
    copies = []
    for r in range(requests):
        copies.append(pltpu.make_async_copy(state_ref.at[r], held.at[r], in_sem.at[r]))
        copies[-1].start()
    spread_rows(k_ref, k_s, requests, steps)
    spread_rows(q_ref, q_s, requests, steps)
    spread_rows(v_ref, v_s, requests, steps)
    spread_rows(g_ref, g_s, requests, steps)
    sigmoid_rows(a_ref, a_s, requests, steps)
    sigmoid_rows(b_ref, b_s, requests, steps)
    top = ids_ref.shape[-1]
    place = lax.broadcasted_iota(jnp.int32, (steps, w_s.shape[-1]), 1)
    for r in range(requests):
        rows = slice(r * steps, (r + 1) * steps)
        r_s[rows, :] = res_ref[r].astype(F32)
        prob = prob_ref[r]
        prob = prob / row_sum(prob)
        weight = jnp.zeros(place.shape, F32)
        ids = ids_ref[r]
        for j in range(top):
            high = prob[:, j : j + 1].astype(BF16).astype(F32)
            weight = jnp.where(place == ids[:, j : j + 1], high, weight)
            weight = jnp.where(place == ids[:, j : j + 1] + experts, prob[:, j : j + 1] - high, weight)
        w_s[rows, :] = weight
    for r in range(requests):
        copies[r].wait()
        rows = slice(r * steps, (r + 1) * steps)
        for kh in range(key_heads):
            left = jnp.concatenate([k_s[kh, rows, :], q_s[kh, rows, :]], axis=0).astype(BF16)
            for h in range(kh * repeats, (kh + 1) * repeats):
                m_s[h, r * 2 * steps : (r + 1) * 2 * steps, :] = jnp.dot(
                    left, held[r, h * hd : (h + 1) * hd, :], preferred_element_type=F32
                )
    gain = gain_ref[...]

    def emit(t, h, o):
        gate = at_step(g_s, t, requests, steps, h)
        scaled = o * lax.rsqrt(row_sum(o * o) * (1.0 / hd) + EPS)
        o_s[h, pl.ds(t, requests, stride=steps), :] = scaled * gain * jax.nn.silu(gate)

    for kh in range(key_heads):
        recurrence(kh, repeats, steps, requests, hd, k_s, q_s, v_s, a_s, b_s, m_s, emit, None)
    width = heads * hd
    cols = res_ref.shape[-1] // lanes
    for h in range(heads):
        part = o_s[h].astype(BF16)
        for j in range(lanes):
            outs[j][:, h * hd : (h + 1) * hd] = part
    marks = w_s[...].astype(BF16)
    for j in range(lanes):
        start = pl.multiple_of((lane_ref[0] ^ j) * cols, cols)
        outs[j][:, width : width + cols] = r_s[:, pl.ds(start, cols)].astype(BF16)
        outs[j][:, width + cols :] = marks


def core_rows(
    lane, lanes, experts, states, query_rows, key_rows, value_rows, gate_rows, beta_logit, decay_logit,
    core_gain, residual, route_ids, route_prob,
):
    requests, heads, hd, _ = states.shape
    steps = key_rows.shape[1]
    kw, vw = key_rows.shape[-1], value_rows.shape[-1]
    tokens = requests * steps
    width = residual.shape[-1]
    weight_lanes = -(-2 * experts // 128) * 128
    vmem, hbm = pl.BlockSpec(memory_space=pltpu.VMEM), pl.BlockSpec(memory_space=pl.ANY)
    return pl.pallas_call(
        functools.partial(core_kernel, lanes, experts),
        in_specs=[pl.BlockSpec(memory_space=pltpu.SMEM), hbm] + [vmem] * 10,
        out_specs=[vmem] * lanes,
        out_shape=[jax.ShapeDtypeStruct((tokens, vw + width // lanes + weight_lanes), BF16)] * lanes,
        scratch_shapes=[
            pltpu.VMEM((kw // hd, tokens, hd), F32),
            pltpu.VMEM((kw // hd, tokens, hd), F32),
            pltpu.VMEM((heads, tokens, hd), F32),
            pltpu.VMEM((heads, tokens, hd), F32),
            pltpu.VMEM((tokens, 128), F32),
            pltpu.VMEM((tokens, 128), F32),
            pltpu.VMEM((heads, 2 * tokens, hd), F32),
            pltpu.VMEM((heads, tokens, hd), F32),
            pltpu.VMEM((tokens, width), F32),
            pltpu.VMEM((tokens, weight_lanes), F32),
            pltpu.VMEM((requests, heads * hd, hd), BF16),
            pltpu.SemaphoreType.DMA((requests,)),
        ],
        compiler_params=pltpu.CompilerParams(vmem_limit_bytes=60 * MIB),
        cost_estimate=pl.CostEstimate(flops=20_000_000, bytes_accessed=9 * MIB, transcendentals=100_000),
        name="core_rows",
    )(
        lane, states.reshape(requests, heads * hd, hd), query_rows, key_rows, value_rows, gate_rows,
        beta_logit, decay_logit, core_gain.reshape(1, hd), residual, route_ids, route_prob,
    )


def pack_kernel(lanes, key_heads, home_ref, lane_ref, state_ref, k_ref, v_ref, b_ref, a_ref, *rest):
    outs = rest[:-4]
    held, pay_f, in_sem, out_sem = rest[-4:]
    requests, steps, _ = k_ref.shape
    hd = held.shape[-1]
    heads = v_ref.shape[-1] // hd
    state_rows = heads * hd
    cap = requests // lanes
    copies = []
    for r in range(requests):
        source = state_ref.at[r]
        copies.append(pltpu.make_async_copy(source, held.at[r, pl.ds(0, state_rows)], in_sem.at[r]))
        copies[-1].start()
    target = [lax.rem(lax.div(home_ref[r], requests), lanes) ^ lane_ref[0] for r in range(requests)]
    ranks = [
        sum([(target[p] == target[r]).astype(jnp.int32) for p in range(r)], jnp.int32(0))
        for r in range(requests)
    ]
    pay_f[...] = jnp.zeros_like(pay_f)
    for r in range(requests):
        keys, vals = k_ref[r].astype(F32), v_ref[r].astype(F32)
        for kh in range(key_heads):
            pay_f[kh * steps : (kh + 1) * steps, :] = keys[:, kh * hd : (kh + 1) * hd]
        for h in range(heads):
            at = (key_heads + h) * steps
            pay_f[at : at + steps, :] = vals[:, h * hd : (h + 1) * hd]
        at = (key_heads + heads) * steps
        pay_f[at : at + steps, :heads] = a_ref[r].astype(F32)
        pay_f[at + steps : at + 2 * steps, :heads] = b_ref[r].astype(F32)
        place = lax.rem(home_ref[r], requests).astype(F32)
        pay_f[at + 2 * steps : at + 3 * steps, :] = jnp.full((steps, hd), place, F32)
        held[r, state_rows:, :] = pay_f[...].astype(BF16)
    for r in range(requests):
        copies[r].wait()
        for d in range(lanes):
            for q in range(cap if d > 1 else 1):
                dest = outs[d].at[ranks[r]] if d < 2 else outs[2 + (d - 2) * cap + q].at[0]
                chosen = (target[r] == d) & (ranks[r] == q) if d > 1 else target[r] == d

                @pl.when(chosen)
                def _():
                    pltpu.make_async_copy(held.at[r], dest, out_sem.at[r]).start()

    for r in range(requests):
        pltpu.make_async_copy(held.at[r], outs[0].at[0], out_sem.at[r]).wait()


def pack_states(home, lane, lanes, states, key_rows, value_rows, beta_logit, decay_logit):
    requests, heads, hd, _ = states.shape
    steps = key_rows.shape[1]
    key_heads = key_rows.shape[-1] // hd
    cap = requests // lanes
    _, pay_rows = packed_rows(key_heads, heads, steps)
    all_rows = heads * hd + pay_rows
    vmem, hbm = pl.BlockSpec(memory_space=pltpu.VMEM), pl.BlockSpec(memory_space=pl.ANY)
    smem = pl.BlockSpec(memory_space=pltpu.SMEM)
    sizes = [cap] * 2 + [1] * (cap * (lanes - 2))
    return pl.pallas_call(
        functools.partial(pack_kernel, lanes, key_heads),
        in_specs=[smem, smem, hbm] + [vmem] * 4,
        out_specs=[hbm] * len(sizes),
        out_shape=[jax.ShapeDtypeStruct((n, all_rows, hd), BF16) for n in sizes],
        scratch_shapes=[
            pltpu.VMEM((requests, all_rows, hd), BF16),
            pltpu.VMEM((pay_rows, hd), F32),
            pltpu.SemaphoreType.DMA((requests,)),
            pltpu.SemaphoreType.DMA((requests,)),
        ],
        compiler_params=pltpu.CompilerParams(vmem_limit_bytes=48 * MIB),
        cost_estimate=pl.CostEstimate(flops=0, bytes_accessed=9 * MIB, transcendentals=0),
        name="pack_states",
    )(home, lane, states.reshape(requests, heads * hd, hd), key_rows, value_rows, beta_logit, decay_logit)


def project_kernel(*refs):
    lanes = len(refs) - 3
    weight_ref, out_ref, marks_ref = refs[lanes:]
    depth, cols = weight_ref.shape
    rows = jnp.concatenate([refs[j][...] for j in range(lanes)], axis=0)
    attention = jnp.dot(rows[:, :depth], weight_ref[...], preferred_element_type=F32).astype(BF16)
    before = rows[:, depth : depth + cols].astype(F32)
    out_ref[...] = (before + attention.astype(F32)).astype(BF16)
    marks_ref[...] = rows[:, depth + cols :]


def project(got, out_weight):
    tokens, wide = got[0].shape
    depth, cols = out_weight.shape
    rows = tokens * len(got)
    vmem = pl.BlockSpec(memory_space=pltpu.VMEM)
    return pl.pallas_call(
        project_kernel,
        in_specs=[vmem] * (len(got) + 1),
        out_specs=[vmem] * 2,
        out_shape=[
            jax.ShapeDtypeStruct((rows, cols), BF16),
            jax.ShapeDtypeStruct((rows, wide - depth - cols), BF16),
        ],
        compiler_params=pltpu.CompilerParams(vmem_limit_bytes=24 * MIB),
        cost_estimate=pl.CostEstimate(
            flops=2 * rows * depth * cols, bytes_accessed=3 * MIB, transcendentals=0
        ),
        name="project",
    )(*got, out_weight)


def state_kernel(
    key_heads, heads, steps, count, *rest
):
    arrived = rest[:count]
    out_ref, k_s, v_s, a_s, b_s, m_s, u_s, c_s, held, pay_s, ready, in_sem, pay_sem, out_sem = rest[-14:]
    requests, state_rows, hd = held.shape
    origin = [(a, j) for a in arrived for j in range(a.shape[0])]
    repeats = heads // key_heads
    pays, copies = [], []
    for r in range(requests):
        pays.append(
            pltpu.make_async_copy(
                origin[r][0].at[origin[r][1], pl.ds(state_rows, pay_s.shape[1])], pay_s.at[r], pay_sem.at[r]
            )
        )
        pays[-1].start()
    for r in range(requests):
        copies.append(
            pltpu.make_async_copy(
                origin[r][0].at[origin[r][1], pl.ds(0, state_rows)], held.at[r], in_sem.at[r]
            )
        )
        copies[-1].start()
    places = []
    for r in range(requests):
        pays[r].wait()
        rows = slice(r * steps, (r + 1) * steps)
        pay = pay_s[r].astype(F32)
        for kh in range(key_heads):
            k_s[kh, rows, :] = pay[kh * steps : (kh + 1) * steps]
        for h in range(heads):
            v_s[h, rows, :] = pay[(key_heads + h) * steps : (key_heads + h + 1) * steps]
        at = (key_heads + heads) * steps
        a_s[rows, :] = jax.nn.sigmoid(pay[at : at + steps])
        b_s[rows, :] = jax.nn.sigmoid(pay[at + steps : at + 2 * steps])
        places.append(jnp.max(pay[at + 2 * steps : at + 3 * steps]).astype(jnp.int32))
    for r in range(requests):
        copies[r].wait()
        rows = slice(r * steps, (r + 1) * steps)
        for h in range(heads):
            m_s[h, rows, :] = jnp.dot(
                k_s[h // repeats, rows, :].astype(BF16),
                held[r, h * hd : (h + 1) * hd, :],
                preferred_element_type=F32,
            )

    def emit(h, c, updates):
        c_s[h] = jnp.broadcast_to(c, (requests, hd))
        for t, u in enumerate(updates):
            u_s[h, pl.ds(t, requests, stride=steps), :] = u

    for kh in range(key_heads):
        recurrence(kh, repeats, steps, requests, hd, k_s, None, v_s, a_s, b_s, m_s, None, emit)
    sent = []
    for r in range(requests):
        slot = r % 2
        if r >= 2:
            sent[r - 2].wait()
        rows = slice(r * steps, (r + 1) * steps)
        for h in range(heads):
            k4 = k_s[h // repeats, rows, :]
            k8 = jnp.concatenate([k4, k4], axis=0).astype(BF16)
            u4 = u_s[h, rows, :]
            high = u4.astype(BF16).astype(F32)
            u8 = jnp.concatenate([high, u4 - high], axis=0).astype(BF16)
            added = lax.dot_general(
                k8, u8, (((0,), (0,)), ((), ())), preferred_element_type=F32
            )
            kept = held[r, h * hd : (h + 1) * hd, :].astype(F32) * c_s[h, r : r + 1, :]
            ready[slot, h * hd : (h + 1) * hd, :] = (kept + added).astype(BF16)
        sent.append(pltpu.make_async_copy(ready.at[slot], out_ref.at[places[r]], out_sem.at[slot]))
        sent[-1].start()
    for c in sent[-2:]:
        c.wait()


def landed_states(arrived, before, total, key_heads, heads, steps):
    _, all_rows, hd = arrived[0].shape
    requests = sum(a.shape[0] for a in arrived)
    tokens = requests * steps
    state_rows = heads * hd
    hbm = pl.BlockSpec(memory_space=pl.ANY)
    out = pl.pallas_call(
        functools.partial(state_kernel, key_heads, heads, steps, len(arrived)),
        in_specs=[hbm] * (len(arrived) + len(before)),
        out_specs=hbm,
        out_shape=jax.ShapeDtypeStruct((total, state_rows, hd), BF16),
        input_output_aliases={len(arrived): 0} if before else {},
        scratch_shapes=[
            pltpu.VMEM((key_heads, tokens, hd), F32),
            pltpu.VMEM((heads, tokens, hd), F32),
            pltpu.VMEM((tokens, hd), F32),
            pltpu.VMEM((tokens, hd), F32),
            pltpu.VMEM((heads, tokens, hd), F32),
            pltpu.VMEM((heads, tokens, hd), F32),
            pltpu.VMEM((heads, requests, hd), F32),
            pltpu.VMEM((requests, state_rows, hd), BF16),
            pltpu.VMEM((requests, all_rows - state_rows, hd), BF16),
            pltpu.VMEM((2, state_rows, hd), BF16),
            pltpu.SemaphoreType.DMA((requests,)),
            pltpu.SemaphoreType.DMA((requests,)),
            pltpu.SemaphoreType.DMA((2,)),
        ],
        compiler_params=pltpu.CompilerParams(vmem_limit_bytes=32 * MIB),
        cost_estimate=pl.CostEstimate(flops=20_000_000, bytes_accessed=requests * MIB, transcendentals=10_000),
        name="landed_states",
    )(*arrived, *before)
    return out


def expert_kernel(sides, own_out, experts, where_ref, *rest):
    sources = rest[: 2 * sides]
    gain_ref, up_ref, down_ref = rest[2 * sides : 2 * sides + 3]
    keeps = rest[2 * sides + 3 : 3 * sides + 3]
    give_ref = rest[3 * sides + 3]
    pieces, result_s, sems = rest[-3 - 2 * sides + 1 : -2], rest[-2], rest[-1]
    copies = [pltpu.make_async_copy(a, b, sems.at[i]) for i, (a, b) in enumerate(zip(sources, pieces))]
    for c in copies:
        c.start()
    for c in copies:
        c.wait()
    group_rows = pieces[0].shape[0]
    cols = gain_ref.shape[-1]
    spans = give_ref.shape[1]
    tokens = give_ref.shape[2]
    width = down_ref.shape[-1]
    hidden_units = down_ref.shape[1]
    e = where_ref[0]
    blocks = [(x, c) for x in range(spans) for c in range(2)]
    values = {}
    for x, c in blocks:
        span = slice(x * cols, (x + 1) * cols)
        parts = [
            pieces[2 * y + c][(p ^ c) * tokens : ((p ^ c) + 1) * tokens, span]
            for y in range(sides)
            for p in range(2 * spans)
        ]
        values[x, c] = jnp.concatenate(parts, axis=0).astype(F32)
    total = sum(row_sum(values[b] * values[b]) for b in blocks)
    scale = lax.rsqrt(total * (1.0 / width) + EPS)
    joined = None
    for x, c in blocks:
        block = e ^ (2 * x + c)
        normed = (values[x, c] * scale * gain_ref[pl.ds(block, 1), :]).astype(BF16)
        up = up_ref[0, pl.ds(pl.multiple_of(block * cols, cols), cols), :]
        term = jnp.dot(normed, up, preferred_element_type=F32)
        joined = term if joined is None else joined + term
        if own_out:
            own = values[x, c][:tokens].astype(BF16)
            rest[3 * sides + 4][:, pl.ds(pl.multiple_of(block * cols, cols), cols)] = own
    active = (jax.nn.silu(joined[:, :hidden_units]) * joined[:, hidden_units:]).astype(BF16)
    result = jnp.dot(active, down_ref[0], preferred_element_type=F32).astype(BF16)
    marks = [pieces[2 * y][:, spans * cols :].astype(F32) for y in range(sides)]
    marks = jnp.concatenate(marks, axis=0)
    place = lax.broadcasted_iota(jnp.int32, marks.shape, 1)
    mine = (place == where_ref[1]) | (place == where_ref[1] + experts)
    weight = row_sum(jnp.where(mine, marks, 0.0))
    result_s[...] = (result.astype(F32) * weight).astype(BF16)
    for y in range(sides):
        for x in range(spans):
            for c in range(2):
                start = y * group_rows + (2 * x + c) * tokens
                rows = result_s[start : start + tokens, :]
                if c:
                    give_ref[y, x] = rows
                else:
                    keeps[y][x] = rows


def expert_chunk(where, pieces, gain, gate_up, down_weight, tokens, experts, own_out):
    sides = len(pieces) // 2
    spans, group_rows = gain.shape[0] // 2, pieces[0].shape[0]
    width = down_weight.shape[-1]
    vmem = pl.BlockSpec(memory_space=pltpu.VMEM)
    hbm = pl.BlockSpec(memory_space=pltpu.HBM)
    keep = jax.ShapeDtypeStruct((spans, tokens, width), BF16)
    give = jax.ShapeDtypeStruct((sides, spans, tokens, width), BF16)
    own = [jax.ShapeDtypeStruct((tokens, width), BF16)] if own_out else []
    rows = sides * group_rows
    outs = pl.pallas_call(
        functools.partial(expert_kernel, sides, own_out, experts),
        in_specs=[pl.BlockSpec(memory_space=pltpu.SMEM)] + [hbm] * len(pieces) + [vmem] * 3,
        out_specs=[vmem] * (sides + 1 + len(own)),
        out_shape=[keep] * sides + [give] + own,
        scratch_shapes=[pltpu.VMEM(p.shape, BF16) for p in pieces]
        + [pltpu.VMEM((rows, width), BF16), pltpu.SemaphoreType.DMA((len(pieces),))],
        compiler_params=pltpu.CompilerParams(vmem_limit_bytes=32 * MIB),
        cost_estimate=pl.CostEstimate(
            flops=6 * rows * width * down_weight.shape[1], bytes_accessed=6 * MIB, transcendentals=0
        ),
        name="expert_chunk",
    )(where, *pieces, gain, gate_up, down_weight)
    return outs


def swap(x, axis, d):
    size = lax.axis_size(axis)
    return lax.ppermute(x, axis, [(i, i ^ d) for i in range(size)])


def summed(*terms):
    return functools.reduce(lambda p, q: p + q, [t.astype(F32) for t in terms])


def shards(
    states, query_rows, key_rows, value_rows, gate_rows, beta_logit, decay_logit, residual,
    route_ids, route_prob, out_weight, core_gain, moe_gain, gate_up, down_weight, new_home,
):
    requests, heads, hd, _ = states.shape
    steps = query_rows.shape[1]
    width = residual.shape[-1]
    tokens = requests * steps
    lanes = lax.axis_size("ep")
    groups = lax.axis_size("dp")
    my_lane = lax.axis_index("ep")
    my_group = lax.axis_index("dp")
    kw, vw = key_rows.shape[-1], value_rows.shape[-1]
    top = route_ids.shape[-1]

    experts = groups * lanes
    cols = out_weight.shape[1]
    me = my_group * lanes + my_lane

    with jax.named_scope("core"):
        sent = core_rows(
            my_lane.reshape(1), lanes, experts, states, query_rows, key_rows, value_rows,
            gate_rows, beta_logit, decay_logit, core_gain, residual, route_ids, route_prob,
        )
        sent, new_home = lax.optimization_barrier((sent, new_home))
        got = {j: swap(sent[j], "ep", j) for j in range(lanes - 1, 0, -1)}
        got = [sent[0]] + [got[j] for j in range(1, lanes)]
    with jax.named_scope("send_states"):
        packed = pack_states(
            new_home, my_lane.reshape(1), lanes, states, key_rows, value_rows, beta_logit, decay_logit
        )
    with jax.named_scope("attention"):
        got, packed = lax.optimization_barrier((got, packed))
        hidden_cols, marks = project(got, out_weight)
        others = []
        for d in range(2, lanes, 2):
            other = swap(hidden_cols, "ep", d).reshape(lanes, tokens, cols)
            others.append(jnp.concatenate([other[j ^ d] for j in range(lanes)], axis=0))
        held = jnp.concatenate([hidden_cols] + others + [marks], axis=1)
        held, packed = lax.optimization_barrier((held, packed))
    with jax.named_scope("send_states"):
        cap = requests // lanes
        near_states = [packed[0], swap(packed[1], "ep", 1)]
        first_across = swap(held, "dp", 1)
        far_states = []
        for i, piece in enumerate(packed[2:]):
            if i:
                piece, far_states[-1] = lax.optimization_barrier((piece, far_states[-1]))
            far_states.append(swap(piece, "ep", 2 + i // cap))

    gain = moe_gain.reshape(lanes, cols)
    where = jnp.stack([my_lane, me])
    far = groups // 2
    chunks = [0] + [d for d in range(groups - 2, 0, -2) if d != far] + [far]
    tie = lax.optimization_barrier
    own_rows = None
    with jax.named_scope("tokens"):
        near = {d: swap(held, "dp", d) if d else held for d in chunks[:-1]}
        later, near[chunks[1]] = tie((held, near[chunks[1]]))
        across = {d: swap(near[d], "dp", 1) if d else first_across for d in chunks[:-1]}
        near[far] = swap(later, "dp", far)
        pieces = {}
        for d in chunks:
            aside = across.get(d)
            if d == far:
                near[d], pieces[chunks[-2]][2] = tie((near[d], pieces[chunks[-2]][2]))
                aside = swap(near[d], "dp", 1)
                last_across = aside
            else:
                pieces[d] = [near[d], swap(near[d], "ep", 1), aside, swap(aside, "ep", 1)]
        pieces[0], pieces[chunks[1]][2] = tie((pieces[0], pieces[chunks[1]][2]))
        pieces[0], far_states[0] = tie((pieces[0], far_states[0]))
    sums, keeps, parts, asides = {}, {}, {}, {}
    for d in chunks:
        if d == far:
            with jax.named_scope("tokens"):
                beside, keeps = tie((last_across, keeps))
                pieces[d] = [near[d], swap(near[d], "ep", 1), last_across, swap(beside, "ep", 1)]
                pieces[d], far_states[1], asides[chunks[1]] = tie(
                    (pieces[d], far_states[1], asides[chunks[1]])
                )
        with jax.named_scope("experts"):
            outs = expert_chunk(where, pieces[d], gain, gate_up, down_weight, tokens, experts, d == 0)
            keep_near, keep_across, give = outs[:3]
            if d == 0:
                own_rows = outs[3]
        with jax.named_scope("way_back"):
            taken = swap(give, "ep", 1)
            aside = summed(keep_across, taken[1]).astype(BF16)
            parts[d], asides[d] = taken, aside
            keeps[d] = keep_near
    for d in [far, chunks[1], 0] + chunks[2:-1]:
        with jax.named_scope("way_back"):
            back = swap(asides[d], "dp", 1)
            if d == far:
                others = {p: asides[p] for p in chunks if p not in (far, chunks[1])}
                others, back = tie((others, back))
                asides.update(others)
            chunk = summed(keeps[d], parts[d][0], back)
            sums[d] = chunk.astype(BF16) if d else chunk
    with jax.named_scope("landed"):
        sizes = (requests, kw // hd, heads, steps)
        sums[far], arrived = tie((sums[far], near_states + far_states[:-2]))
        moved_out = landed_states(arrived, [], *sizes)
    with jax.named_scope("way_back"):
        sums = [swap(sums[d], "dp", d) if d else sums[d] for d in chunks]
        sums, moved_out = tie((sums, moved_out))
    with jax.named_scope("landed"):
        moved_out = landed_states(far_states[-2:], [moved_out], *sizes)
        moved_out = moved_out.reshape(requests, heads, hd, hd)
    with jax.named_scope("mixed"):
        mixed = summed(own_rows, *[s[0] for s in sums])
        for x in range(1, lanes // 2):
            mixed = mixed + swap(summed(*[s[x] for s in sums]).astype(BF16), "ep", 2 * x).astype(F32)
        mixed_out = mixed.astype(BF16)
    return mixed_out.reshape(requests, steps, width), moved_out


def solution(mesh):
    row = P(("dp", "ep"), None, None)
    placed = (P(("dp", "ep"), None, None, None),) + (row,) * 9 + (
        P(None, "ep"), P(), P(), row, row, P(("dp", "ep")),
    )
    return jax.shard_map(
        shards,
        mesh=mesh,
        in_specs=placed,
        out_specs=(row, P(("dp", "ep"), None, None, None)),
        check_vma=False,
    )
```
